256 devices in a mesh: gx: 32 (over z_lo, x, core), gy: 8 (over z_hi, y).
Axes of the slice: x: 4, y: 4, z: 8 (z_hi: 2, z_lo: 4; z = z_hi * 4 + z_lo), core: 2. Of those that a mesh axis runs over, the one named last changes fastest.
Arguments:
- input_field: bfloat16 [1, 32, 192, 256, 256], P(None, None, 'gx', 'gy'), may hold values from -6 to 6
- cotangent: bfloat16 [1, 32, 192, 256, 256], P(None, None, 'gx', 'gy'), may hold values from -6 to 6
- spectral_weights: float32 [2, 17, 48, 64, 1024], P(None, None, 'gy', 'gx'), may hold values from -6 to 6
- point_weight: bfloat16 [32, 32], replicated, may hold values from -1 to 1
- point_bias: float32 [32], replicated, may hold values from -1 to 1
Outputs:
- input_grad: bfloat16 [1, 32, 192, 256, 256], P(None, None, 'gx', 'gy')
- weight_grad: float32 [2, 17, 48, 64, 1024], P(None, None, 'gy', 'gx')
The draws below stay inside these ranges and needn't reach their ends.
All inputs are finite; a program needn't handle non-finite values.
Results may differ from the reference program's by a relative error of at most 0.0052.
Values sent between devices are 32-bit elements; how exact they have to be, the bound alone decides.
A program may use at most 128 MiB of HBM per device.

```python
import math
import jax
import jax.numpy as jnp
from jax import lax

C = 32
NX = 192
NY = 256
NZ = 256
KX = 48
KY = 64
KZ = 17
SAMPLES = 1


def steps_of(own_key, shape, pieces, smallest, high):
    factor_of, own = 1.0, jax.random.fold_in(own_key, 6)
    for axis_at, shards_of in pieces:
        steps = jnp.exp(jax.random.uniform(jax.random.fold_in(own, axis_at), (shards_of,), jnp.float32, smallest / len(pieces), high / len(pieces)))
        factor_of = factor_of * jnp.repeat(steps, shape[axis_at] // shards_of).reshape([-1 if axis == axis_at else 1 for axis in range(len(shape))])
    return factor_of


def bell_draw(key, dims, width, bound, cuts=(), kind=jnp.bfloat16):
    values = width * jax.random.normal(key, dims, jnp.float32)
    if cuts:
        values = values * steps_of(key, dims, cuts, -0.22, 0.18)
    return jnp.clip(values, -bound, bound).astype(kind)


def setup_inputs(seed: int = 0) -> dict:
    seeds = jax.random.split(jax.random.key(seed), 6)
    input_field = bell_draw(seeds[0], (SAMPLES, C, NX, NY, NZ), 1.0, 6.0, ((2, 32), (3, 8)))
    cotangent = bell_draw(seeds[1], (SAMPLES, C, NX, NY, NZ), 1.0, 6.0, ((2, 32), (3, 8)))
    spectral_weights = bell_draw(seeds[2], (2, KZ, KX, KY, C * C), 1.0, 6.0, ((2, 8), (3, 32)), jnp.float32)
    point_weight = bell_draw(seeds[3], (C, C), C ** -0.5, 1.0)
    point_bias = jnp.clip(jax.random.uniform(seeds[4], (C,), jnp.float32, -1.0, 1.0), -1.0, 1.0)
    return dict(input_field=input_field, cotangent=cotangent, spectral_weights=spectral_weights, point_weight=point_weight, point_bias=point_bias)


HIGHEST = lax.Precision.HIGHEST

def kept_list(count, number):
    half_count = number // 2
    lower = jnp.arange(half_count, dtype=jnp.int32)
    return jnp.concatenate([lower, lower + (count - half_count)])

def trig_tables(count, kept):
    points = jnp.arange(count, dtype=jnp.int32)
    product = points[:, None] * kept[None, :] % count
    angles = product.astype(jnp.float32) * (2.0 * math.pi / count)
    return (jnp.cos(angles), jnp.sin(angles))

def rotate(real_part, imag_part, cosine, sine, form, sign):
    cos_real = jnp.einsum(form, real_part, cosine, precision=HIGHEST)
    cos_imag = jnp.einsum(form, imag_part, cosine, precision=HIGHEST)
    sin_real = jnp.einsum(form, real_part, sine, precision=HIGHEST)
    sin_imag = jnp.einsum(form, imag_part, sine, precision=HIGHEST)
    return (cos_real + sign * sin_imag, cos_imag - sign * sin_real)

def gelu_slope(values):
    normal_cdf = 0.5 * (1.0 + lax.erf(values * (1.0 / math.sqrt(2.0))))
    density = jnp.exp(-0.5 * values * values) * (1.0 / math.sqrt(2.0 * math.pi))
    return normal_cdf + values * density

def reference(input_field, cotangent, spectral_weights, point_weight, point_bias):
    x_cos, x_sin = trig_tables(NX, kept_list(NX, KX))
    y_cos, y_sin = trig_tables(NY, kept_list(NY, KY))
    z_cos, z_sin = trig_tables(NZ, jnp.arange(KZ, dtype=jnp.int32))
    z_cos_low = z_cos.astype(jnp.bfloat16).astype(jnp.float32)
    z_sin_low = z_sin.astype(jnp.bfloat16).astype(jnp.float32)
    scale_factor = (NX * NY * NZ) ** (-0.5)

    def analyse(source):
        flat = source.reshape(SAMPLES * C * NX * NY, NZ).astype(jnp.float32)
        real_part = jnp.dot(flat, z_cos_low, precision=HIGHEST).reshape(SAMPLES, C, NX, NY, KZ)
        imag_part = -jnp.dot(flat, z_sin_low, precision=HIGHEST).reshape(SAMPLES, C, NX, NY, KZ)
        real_part, imag_part = rotate(real_part, imag_part, y_cos, y_sin, 'scxyk,yj->scxjk', 1.0)
        real_part, imag_part = rotate(real_part, imag_part, x_cos, x_sin, 'scxjk,xi->kscij', 1.0)
        return (real_part * scale_factor, imag_part * scale_factor)

    def synthesise(real_part, imag_part):
        real_part, imag_part = rotate(real_part, imag_part, x_cos, x_sin, 'kscij,xi->kscxj', -1.0)
        real_part, imag_part = rotate(real_part, imag_part, y_cos, y_sin, 'kscxj,yj->kscxy', -1.0)
        result = jnp.einsum('kscxy,zk->scxyz', real_part, z_cos, precision=HIGHEST)
        result = result - jnp.einsum('kscxy,zk->scxyz', imag_part, z_sin, precision=HIGHEST)
        return result * scale_factor

    def linear_part(matrix, source):

        def per_sample(sample):
            flat = sample.reshape(C, NX * NY * NZ).astype(jnp.float32)
            return jnp.dot(matrix.astype(jnp.float32), flat, precision=HIGHEST).reshape(C, NX, NY, NZ)
        return lax.map(per_sample, source)
    weight_real = spectral_weights[0].reshape(KZ, KX, KY, C, C)
    weight_imag = spectral_weights[1].reshape(KZ, KX, KY, C, C)
    modes_real, modes_imag = analyse(input_field)
    mixed_real = jnp.einsum('kijco,kscij->ksoij', weight_real, modes_real, precision=HIGHEST) - jnp.einsum('kijco,kscij->ksoij', weight_imag, modes_imag, precision=HIGHEST)
    mixed_imag = jnp.einsum('kijco,kscij->ksoij', weight_real, modes_imag, precision=HIGHEST) + jnp.einsum('kijco,kscij->ksoij', weight_imag, modes_real, precision=HIGHEST)
    pre = synthesise(mixed_real, mixed_imag) + linear_part(point_weight, input_field) + point_bias[None, :, None, None, None]
    pre_grad = (cotangent.astype(jnp.float32) * gelu_slope(pre)).astype(jnp.bfloat16)
    grad_real, grad_imag = analyse(pre_grad)
    grad_w_real = jnp.einsum('kscij,ksoij->kijco', modes_real, grad_real, precision=HIGHEST) + jnp.einsum('kscij,ksoij->kijco', modes_imag, grad_imag, precision=HIGHEST)
    grad_w_imag = jnp.einsum('kscij,ksoij->kijco', modes_real, grad_imag, precision=HIGHEST) - jnp.einsum('kscij,ksoij->kijco', modes_imag, grad_real, precision=HIGHEST)
    weight_grad = jnp.stack([grad_w_real, grad_w_imag]).reshape(2, KZ, KX, KY, C * C)
    back_real = jnp.einsum('kijco,ksoij->kscij', weight_real, grad_real, precision=HIGHEST) + jnp.einsum('kijco,ksoij->kscij', weight_imag, grad_imag, precision=HIGHEST)
    back_imag = jnp.einsum('kijco,ksoij->kscij', weight_real, grad_imag, precision=HIGHEST) - jnp.einsum('kijco,ksoij->kscij', weight_imag, grad_real, precision=HIGHEST)
    input_grad = synthesise(back_real, back_imag) + linear_part(point_weight.T, pre_grad)
    return (input_grad.astype(jnp.bfloat16), weight_grad)
```

```python
import math

import jax
import jax.numpy as jnp
import ml_dtypes
import numpy as np
from jax import lax
from jax.experimental import pallas as pl
from jax.experimental.pallas import tpu as pltpu
from jax.sharding import PartitionSpec as P

C = 32
NX = 192
NY = 256
NZ = 256
KX = 48
KY = 64
KZ = 17
SCALE = (NX * NY * NZ) ** (-0.5)
MESH = pl.DeviceIdType.MESH
F32 = jnp.float32
BF16 = jnp.bfloat16


def kept(count, number):
    half = number // 2
    return np.concatenate([np.arange(half), np.arange(half) + count - half])


def trig(points, freqs, count):
    angle = 2.0 * np.pi * ((points[:, None] * freqs[None, :]) % count) / count
    return np.cos(angle), np.sin(angle)


def hi_lo(table):
    table = np.asarray(table, np.float32)
    high = table.astype(ml_dtypes.bfloat16)
    low = (table - high.astype(np.float32)).astype(ml_dtypes.bfloat16)
    return high, low


def make_tables():
    z_cos, z_sin = trig(np.arange(NZ), np.arange(KZ), NZ)
    y_cos, y_sin = trig(np.arange(NY), kept(NY, KY), NY)
    x_cos, x_sin = trig(np.arange(NX), kept(NX, KX), NX)
    tabs = {}
    wz = np.zeros((4, NZ, 2, 2, 4, 16))
    zz = np.zeros((4, 2, 2, 4, 16, NZ))
    for c4 in range(4):
        wz[c4, :, 0, 0, c4, :] = z_cos[:, :16]
        wz[c4, :, 0, 1, c4, :] = -z_sin[:, :16]
        wz[c4, :, 1, 0, c4, :] = z_cos[:, 16:17]
        wz[c4, :, 1, 1, c4, :] = -z_sin[:, 16:17]
        zz[c4, 0, 0, c4] = z_cos[:, :16].T
        zz[c4, 0, 1, c4] = -z_sin[:, :16].T
        zz[c4, 1, 0, c4] = z_cos[:, 16:17].T
        zz[c4, 1, 1, c4] = -z_sin[:, 16:17].T
    tabs["wz"] = wz.reshape(4, NZ, 256).astype(np.float32).astype(ml_dtypes.bfloat16)
    tabs["zz"] = np.stack(hi_lo(zz.reshape(4, 256, NZ)))
    s_at, zl_at, j_at = np.meshgrid(np.arange(8), np.arange(4), np.arange(2), indexing="ij")
    order = ((zl_at * 8 + s_at) * 2 + j_at).reshape(-1)
    yc = (y_cos * SCALE)[:, order].reshape(2, 128, 64)
    ys = (y_sin * SCALE)[:, order].reshape(2, 128, 64)
    inv = np.concatenate([yc, ys], 2)
    fwd = inv.transpose(0, 2, 1)
    tabs["t1"] = np.stack([np.concatenate([h, h, l], -1) for h, l in [hi_lo(fwd[0]), hi_lo(fwd[1])]])
    tabs["t1i"] = np.stack([np.concatenate([h, h, l], -1) for h, l in [hi_lo(inv[0]), hi_lo(inv[1])]])
    xt = np.stack([x_cos, x_sin]).reshape(2, 4, 8, 6, 2, 4, 6)
    t2 = np.zeros((4, 2, 4, 2, 4, 16, 6, 8, 8))
    for zl_to in range(4):
        for i in range(6):
            for j in range(2):
                block = xt[:, :, :, :, :, :, i]
                t2[:, :, zl_to, :, :, 2 * i + j, :, :, zl_to * 2 + j] = block.transpose(1, 4, 0, 5, 3, 2)
    fwd = t2.reshape(4, 8, 128, 384)
    tabs["t2"] = np.stack(hi_lo(fwd), 1)
    inv = t2.transpose(0, 6, 7, 8, 3, 1, 2, 4, 5).reshape(4, 6, 64, 1024)
    tabs["t2i"] = np.stack(hi_lo(inv), 1)
    eye2, eye4 = np.eye(2), np.eye(4)
    ones16, ones32 = np.ones(16), np.ones(32)
    e1 = np.einsum("qr,cd,s,o->qcsrdo", eye2, eye4, ones16, ones32)
    tabs["e1"] = e1.reshape(128, 256)
    tabs["r2"] = e1.reshape(128, 256).T
    pick = np.eye(32).reshape(8, 4, 32)
    e2 = np.einsum("qr,bio,s,c->bqisrco", eye2, pick, ones16, np.ones(4)).reshape(8, 128, 256)
    tabs["e2"] = e2
    tabs["rr"] = e2.transpose(0, 2, 1)
    slot = np.zeros((6, 16, 16))
    for x in range(6):
        slot[x, x, :] = 1.0
    spread = np.einsum("qr,cd,xst->xqcsrdt", eye2, eye4, slot).reshape(6, 128, 128)
    tabs["spread"] = spread.transpose(1, 0, 2).reshape(128, 768)
    tabs["gather"] = spread.transpose(0, 2, 1)
    tabs["a16"] = np.repeat(np.eye(32), 16, axis=0)
    for name in ("e1", "r2", "e2", "rr", "spread", "gather", "a16"):
        tabs[name] = tabs[name].astype(ml_dtypes.bfloat16)
    return tabs


TABLES = make_tables()
IN_VMEM = ("wz", "t1", "a16", "spread", "gather", "t1i", "e1", "r2")
IN_HBM = ("t2", "t2i", "zz", "e2", "rr")


def mm(left, right):
    return jnp.dot(left, right, preferred_element_type=F32)


def halves(values):
    high = values.astype(BF16)
    return high, (values - high.astype(F32)).astype(BF16)


def gelu_slope(values):
    size = jnp.abs(values)
    t = 1.0 / (1.0 + (0.3275911 / math.sqrt(2.0)) * size)
    poly = t * (0.254829592 + t * (-0.284496736 + t * (1.421413741 + t * (-1.453152027 + t * 1.061405429))))
    bell = jnp.exp(-0.5 * values * values)
    part = bell * ((1.0 / math.sqrt(2.0 * math.pi)) * size - 0.5 * poly)
    return jnp.where(values >= 0.0, 1.0 + part, -part)


def swap(values, first):
    lane = lax.broadcasted_iota(jnp.int32, (values.shape[0], 128), 1)
    sign = jnp.where(lane < 64, first, -first)
    parts = [
        pltpu.roll(values[:, at : at + 128], 64, 1) * sign for at in range(0, values.shape[1], 128)
    ]
    return parts[0] if len(parts) == 1 else jnp.concatenate(parts, 1)


def slot_of(shape):
    return lax.broadcasted_iota(jnp.int32, shape, len(shape) - 1) % 16


def spread_rows(block):
    slots = slot_of((16, 128))
    rows = lax.broadcasted_iota(jnp.int32, (16, 128), 0)
    parts = [jnp.where(slots == k, block, 0.0) for k in range(16)]
    parts.append(jnp.where(slots == rows, jnp.broadcast_to(block[12:13], (16, 128)), 0.0))
    return jnp.concatenate(parts, 0)


def gather_rows(values):
    slots = slot_of((16, 128))
    rows = lax.broadcasted_iota(jnp.int32, (16, 128), 0)
    total = jnp.where(slots == 0, values[0:16], 0.0)
    for k in range(1, 16):
        total = total + jnp.where(slots == k, values[16 * k : 16 * k + 16], 0.0)
    last = jnp.sum(jnp.where(slots == rows, values[256:272], 0.0), axis=0, keepdims=True)
    return jnp.where(rows == 12, jnp.broadcast_to(last, (16, 128)), total)


def body(
    f, pw, pwt, bias, wz, t1, a16, spread, gather, t1i, e1, r2,
    t2_hbm, t2i_hbm, zz_hbm, e2_hbm, rr_hbm, cot_hbm, w_hbm,
    ig_hbm, wg_hbm,
    t2, t2i, zz, e2, rr, cot, w, ig, wg, pg, lin, kron,
    u, r0, vs, r1, rsb, r3a, s4b, md, xb, mexp, gexp, acc,
    mq, r4, r3b, xb2, vs2, r1s, ys, r0s, t6,
    local_sem, s1s, s1r, s2s, s2r, s3s, s3r, s4s, s4r, g4s, g4r, g3s, g3r, g2s, g2r, g1s, g1r, out_sem,
):
    gx = lax.axis_index("gx")
    gy = lax.axis_index("gy")
    zl, s = gx // 8, gx % 8
    zh, yy = gy // 4, gy % 4
    zz_me = zh * 4 + zl

    def y_id(to):
        return (gx, zh * 4 + to)

    def s_id(to):
        return (zl * 8 + to, gy)

    def z_id(to):
        return ((to % 4) * 8 + s, (to // 4) * 4 + yy)

    loads = [
        pltpu.make_async_copy(src, dst, local_sem.at[n])
        for n, (src, dst) in enumerate(
            [
                (t2_hbm.at[zl], t2),
                (w_hbm, w),
                (rr_hbm, rr),
                (t2i_hbm.at[zl], t2i),
                (cot_hbm, cot),
                (zz_hbm, zz),
                (e2_hbm, e2),
            ]
        )
    ]
    for load in loads:
        load.start()

    barrier = pltpu.get_barrier_semaphore()
    for d in range(1, 4):
        pl.semaphore_signal(barrier, inc=1, device_id=y_id((yy + d) % 4), device_id_type=MESH)
    for d in range(1, 8):
        pl.semaphore_signal(barrier, inc=1, device_id=s_id((s + d) % 8), device_id_type=MESH)
        pl.semaphore_signal(barrier, inc=1, device_id=z_id((zz_me + d) % 8), device_id_type=MESH)
    pl.semaphore_wait(barrier, 17)

    def y_send(src, dst, send, recv, to):
        return pltpu.make_async_remote_copy(src, dst, send, recv, device_id=y_id(to), device_id_type=MESH)

    def s_send(src, dst, send, recv, to):
        return pltpu.make_async_remote_copy(src, dst, send, recv, device_id=s_id(to), device_id_type=MESH)

    def z_send(src, dst, send, recv, to):
        return pltpu.make_async_remote_copy(src, dst, send, recv, device_id=z_id(to), device_id_type=MESH)

    def c1(h, d):
        to = (yy + d) % 4
        return y_send(u.at[h, to], r0.at[h, yy], s1s.at[h, d], s1r.at[h, d], to)

    def w1(h, d):
        fr = (yy + 4 - d) % 4
        return y_send(u.at[h, fr], r0.at[h, fr], s1s.at[h, d], s1r.at[h, d], fr)

    def c2(h, d):
        to = (s + d) % 8
        return s_send(vs.at[h, to], r1.at[h, s], s2s.at[h, d], s2r.at[h, d], to)

    def w2(h, d):
        fr = (s + 8 - d) % 8
        return s_send(vs.at[h, fr], r1.at[h, fr], s2s.at[h, d], s2r.at[h, d], fr)

    def c3(h, d):
        to = (zz_me + d) % 8
        return z_send(rsb.at[h, to], r3a.at[h, zz_me], s3s.at[h, d], s3r.at[h, d], to)

    def w3(h, d):
        fr = (zz_me + 8 - d) % 8
        return z_send(rsb.at[h, fr], r3a.at[h, fr], s3s.at[h, d], s3r.at[h, d], fr)

    def c4(d):
        to = (yy + d) % 4
        return y_send(s4b.at[to], md.at[yy], s4s.at[d], s4r.at[d], to)

    def w4(d):
        fr = (yy + 4 - d) % 4
        return y_send(s4b.at[fr], md.at[fr], s4s.at[d], s4r.at[d], fr)

    def k4(d):
        to = (yy + d) % 4
        return y_send(mq.at[to], r4.at[yy], g4s.at[d], g4r.at[d], to)

    def v4(d):
        fr = (yy + 4 - d) % 4
        return y_send(mq.at[fr], r4.at[fr], g4s.at[d], g4r.at[d], fr)

    def k3(h, d):
        to = (zz_me + d) % 8
        return z_send(r3b.at[h, zz_me], r3b.at[h, zz_me], g3s.at[h, d], g3r.at[h, d], to)

    def v3(h, d):
        fr = (zz_me + 8 - d) % 8
        return z_send(r3b.at[h, fr], r3b.at[h, fr], g3s.at[h, d], g3r.at[h, d], fr)

    def k2(h, d):
        to = (s + d) % 8
        return s_send(vs2.at[h, to], r1s.at[h, s], g2s.at[h, d], g2r.at[h, d], to)

    def v2(h, d):
        fr = (s + 8 - d) % 8
        return s_send(vs2.at[h, fr], r1s.at[h, fr], g2s.at[h, d], g2r.at[h, d], fr)

    def k1(h, d):
        to = (yy + d) % 4
        return y_send(ys.at[h, to], r0s.at[h, yy], g1s.at[h, d], g1r.at[h, d], to)

    def v1(h, d):
        fr = (yy + 4 - d) % 4
        return y_send(ys.at[h, fr], r0s.at[h, fr], g1s.at[h, d], g1r.at[h, d], fr)

    def each(low, high, fn):
        def step(d, carry):
            fn(d)
            return carry

        lax.fori_loop(low, high, step, 0)

    def z_analysis(source, h, to, dest):
        total = None
        for q in range(4):
            term = mm(source[to, h, q].reshape(192, 256), wz[q])
            total = term if total is None else total + term
        slots = slot_of((32, 128))
        last = None
        for x in range(6):
            rows = total[32 * x : 32 * x + 32]
            dest[:, 128 * x : 128 * x + 128] = rows[:, :128]
            part = jnp.where(slots == x, rows[:, 128:], 0.0)
            last = part if last is None else last + part
        dest[:, 768:896] = last

    def y_analysis(h):
        table = t1.at[zh]
        for at, wide in ((0, 256), (256, 256), (512, 256), (768, 128)):
            high, low = halves(r0[h, :, :, at : at + wide].reshape(128, wide))
            both = jnp.concatenate([high, low], 0)
            out = mm(table[:, 0:256], both) + mm(table[:, 256:384], high)
            vs[h, :, :, at : at + wide] = (out[:64] + swap(out[64:], 1.0)).reshape(8, 8, wide)

    def x_analysis_load(h):
        last_high, last_low = halves(r1[h, :, :, 768:896].reshape(64, 128))
        last_high = mm(last_high, spread[...]).astype(BF16)
        last_low = mm(last_low, spread[...]).astype(BF16)
        for x in range(6):
            at = 128 * x
            high, low = halves(r1[h, :, :, at : at + 128].reshape(64, 128))
            xb[0, 64 * x : 64 * x + 64, 0:128] = high
            xb[1, 64 * x : 64 * x + 64, 0:128] = low
            xb[0, 64 * x : 64 * x + 64, 128:256] = last_high[:, at : at + 128]
            xb[1, 64 * x : 64 * x + 64, 128:256] = last_low[:, at : at + 128]

    def x_analysis(h, to, dest):
        high = t2[0, to]
        out = mm(high, xb[0]) + mm(high, xb[1]) + mm(t2[1, to], xb[0])
        out = out[:64] + swap(out[64:], 1.0)
        rows = lax.broadcasted_iota(jnp.int32, (64, 128), 0) % 16
        last = jnp.where(slot_of((64, 128)) == rows, out[:, 128:], 0.0)
        last = jnp.sum(last.reshape(4, 16, 128), axis=1, keepdims=True)
        last = jnp.broadcast_to(last, (4, 16, 128)).reshape(64, 128)
        dest[...] = jnp.where(rows == 12, last, out[:, :128])

    def analysis(source, meanwhile):
        for h in range(2):

            def one(d, h=h):
                to = (yy + d) % 4
                z_analysis(source, h, to, u.at[h, to])
                c1(h, d).start()

            each(1, 4, one)
            z_analysis(source, h, yy, r0.at[h, yy])
        meanwhile()
        for h in range(2):
            each(1, 4, lambda d: w1(h, d).wait_recv())
            y_analysis(h)
            each(1, 8, lambda d: c2(h, d).start())
            r1[h, s] = vs[h, s]
        for h in range(2):
            each(1, 8, lambda d: w2(h, d).wait_recv())
            x_analysis_load(h)

            def one(d, h=h):
                to = (zz_me + d) % 8
                x_analysis(h, to, rsb.at[h, to])
                c3(h, d).start()

            each(1, 8, one)
            x_analysis(h, zz_me, r3a.at[h, zz_me])
        for h in range(2):
            each(1, 8, lambda d: w3(h, d).wait_recv())
            total = r3a[h, 0]
            for z in range(1, 8):
                total = total + r3a[h, z]
            s4b[:, h] = total.reshape(4, 16, 128)
        each(1, 4, lambda d: c4(d).start())
        md[yy] = s4b[yy]
        each(1, 4, lambda d: w4(d).wait_recv())
        for h in range(2):
            each(1, 4, lambda d: c1(h, d).wait_send())
            each(1, 8, lambda d: c2(h, d).wait_send())
            each(1, 8, lambda d: c3(h, d).wait_send())
        each(1, 4, lambda d: c4(d).wait_send())

    def x_synthesis_load(h):
        main = r3b[h].reshape(512, 128)
        rows = lax.broadcasted_iota(jnp.int32, (512, 128), 0) % 16
        last = jnp.broadcast_to(r3b[h].reshape(32, 16, 128)[:, 12:13], (32, 16, 128)).reshape(512, 128)
        last = jnp.where(slot_of((512, 128)) == rows, last, 0.0)
        for at, values in ((0, main), (128, last)):
            high, low = halves(values)
            xb2[0, 0:512, at : at + 128] = high
            xb2[1, 0:512, at : at + 128] = low
            high, low = halves(swap(values, -1.0))
            xb2[0, 512:1024, at : at + 128] = high
            xb2[1, 512:1024, at : at + 128] = low

    def x_synthesis(h):
        for x in range(6):
            high = t2i[0, x]
            out = mm(high, xb2[0]) + mm(high, xb2[1]) + mm(t2i[1, x], xb2[0])
            vs2[h, :, :, 128 * x : 128 * x + 128] = out[:, :128].reshape(8, 8, 128)
            high, low = halves(out[:, 128:])
            part = mm(high, gather[x]) + mm(low, gather[x])
            t6[...] = part if x == 0 else t6[...] + part
        vs2[h, :, :, 768:896] = t6[...].reshape(8, 8, 128)

    def y_synthesis(h):
        table = t1i.at[zh]
        for at, wide in ((0, 256), (256, 256), (512, 256), (768, 128)):
            values = r1s[h, :, :, at : at + wide].reshape(64, wide)
            high, low = halves(jnp.concatenate([values, swap(values, -1.0)], 0))
            out = mm(table[:, 0:256], jnp.concatenate([high, low], 0)) + mm(table[:, 256:384], high)
            ys[h, :, :, at : at + wide] = out.reshape(4, 32, wide)

    def z_synthesis(h, fr, finish):
        slots = slot_of((32, 128))
        last = r0s[h, fr, :, 768:896]
        stacked = jnp.concatenate(
            [
                jnp.concatenate(
                    [r0s[h, fr, :, 128 * x : 128 * x + 128], jnp.where(slots == x, last, 0.0)], 1
                )
                for x in range(6)
            ],
            0,
        )
        high, low = halves(stacked)

        def one(q):
            table = zz[0, q]
            out = mm(high, table) + mm(low, table) + mm(high, zz[1, q])
            finish(fr, h, q, out.reshape(6, 32, 256))

        each(0, 4, one)

    def synthesis(finish):
        each(1, 4, lambda d: k4(d).start())
        r4[yy] = mq[yy]
        each(1, 4, lambda d: v4(d).wait_recv())
        for h in range(2):
            r3b[h, zz_me] = r4[:, h]
            each(1, 8, lambda d: k3(h, d).start())
        for h in range(2):
            each(1, 8, lambda d: v3(h, d).wait_recv())
            x_synthesis_load(h)
            x_synthesis(h)
            each(1, 8, lambda d: k2(h, d).start())
            r1s[h, s] = vs2[h, s]
        for h in range(2):
            each(1, 8, lambda d: v2(h, d).wait_recv())
            y_synthesis(h)
            each(1, 4, lambda d: k1(h, d).start())
            r0s[h, yy] = ys[h, yy]
        for h in range(2):
            z_synthesis(h, yy, finish)

            def one(d, h=h):
                v1(h, d).wait_recv()
                z_synthesis(h, (yy + 4 - d) % 4, finish)

            each(1, 4, one)
        each(1, 4, lambda d: k4(d).wait_send())
        for h in range(2):
            each(1, 8, lambda d: k3(h, d).wait_send())
            each(1, 8, lambda d: k2(h, d).wait_send())
            each(1, 4, lambda d: k1(h, d).wait_send())

    def channel_map(matrix, source):
        rows = lax.broadcasted_iota(jnp.int32, (512, 512), 0) % 16
        columns = lax.broadcasted_iota(jnp.int32, (512, 512), 1) % 16
        wide = mm(a16[...], matrix[...]).astype(BF16)
        full = lax.dot_general(wide, a16[...], (((1,), (1,)), ((), ())), preferred_element_type=F32)
        kron[...] = jnp.where(rows == columns, full, 0.0).astype(BF16)

        def one(x):
            for at in (0, 16):
                block = source[:, :, :, x, at : at + 16, :].reshape(512, 256)
                out = mm(kron[...], block)
                lin[:, :, :, x, at : at + 16, :] = out.reshape(4, 2, 4, 16, 256)

        each(0, 6, one)

    def lanes(b):
        return pl.ds(pl.multiple_of(b * 128, 128), 128)

    def mix():
        acc[...] = jnp.zeros_like(acc)

        def one(b):
            high, low = halves(spread_rows(md[b // 2, b % 2]))
            modes = mm(high, e1[...]) + mm(low, e1[...])
            mexp[b] = modes
            real, imag = modes[:, :128], modes[:, 128:]
            w_real, w_imag = w[0, :, lanes(b)], w[1, :, lanes(b)]
            acc[:, :128] += w_real * real - w_imag * imag
            acc[:, 128:] += w_real * imag + w_imag * real

        each(0, 8, one)
        high, low = halves(acc[...])

        def two(b):
            mq[b // 2, b % 2] = gather_rows(mm(high, rr[b]) + mm(low, rr[b]))

        each(0, 8, two)

    def mix_back():
        gexp[...] = jnp.zeros_like(gexp)

        def one(b):
            high, low = halves(spread_rows(md[b // 2, b % 2]))
            gexp[...] += mm(high, e2[b]) + mm(low, e2[b])

        each(0, 8, one)

        def two(b):
            g_real, g_imag = gexp[:, :128], gexp[:, 128:]
            real, imag = mexp[b, :, :128], mexp[b, :, 128:]
            wg[0, :, lanes(b)] = real * g_real + imag * g_imag
            wg[1, :, lanes(b)] = real * g_imag - imag * g_real
            w_real, w_imag = w[0, :, lanes(b)], w[1, :, lanes(b)]
            high_r, low_r = halves(w_real * g_real + w_imag * g_imag)
            high_i, low_i = halves(w_real * g_imag - w_imag * g_real)
            high = jnp.concatenate([high_r, high_i], 1)
            low = jnp.concatenate([low_r, low_i], 1)
            mq[b // 2, b % 2] = gather_rows(mm(high, r2[...]) + mm(low, r2[...]))

        each(0, 8, two)

    def finish_pre(fr, h, q, spectral):
        pre = spectral + lin[fr, h, q] + bias[fr * 8 + h * 4 + q]
        pg[fr, h, q] = (cot[fr, h, q].astype(F32) * gelu_slope(pre)).astype(BF16)

    def finish_grad(fr, h, q, spectral):
        ig[fr, h, q] = (spectral + lin[fr, h, q]).astype(BF16)

    def first_meanwhile():
        channel_map(pw, f)
        loads[0].wait()

    analysis(f, first_meanwhile)
    loads[1].wait()
    loads[2].wait()
    mix()
    loads[3].wait()
    loads[4].wait()
    loads[5].wait()
    loads[6].wait()
    synthesis(finish_pre)
    analysis(pg, lambda: channel_map(pwt, pg))
    mix_back()
    wg_copy = pltpu.make_async_copy(wg, wg_hbm, out_sem.at[0])
    wg_copy.start()
    synthesis(finish_grad)
    ig_copy = pltpu.make_async_copy(ig, ig_hbm, out_sem.at[1])
    ig_copy.start()
    wg_copy.wait()
    ig_copy.wait()


def per_device(input_field, cotangent, spectral_weights, point_weight, point_bias):
    field_shape = (4, 2, 4, 6, 32, 256)
    f = input_field.reshape(field_shape)
    cot = cotangent.reshape(field_shape)
    w = spectral_weights.reshape(2, KZ, 12, C * C)
    w = jnp.pad(w, ((0, 0), (0, 0), (0, 4), (0, 0))).reshape(2, KZ * 16, C * C)
    tabs = {name: jnp.asarray(value) for name, value in TABLES.items()}
    vmem = pl.BlockSpec(memory_space=pltpu.VMEM)
    smem = pl.BlockSpec(memory_space=pltpu.SMEM)
    hbm = pl.BlockSpec(memory_space=pl.ANY)
    dma = pltpu.SemaphoreType.DMA
    scratch = [
        pltpu.VMEM((2, 8, 128, 384), BF16),
        pltpu.VMEM((2, 6, 64, 1024), BF16),
        pltpu.VMEM((2, 4, 256, 256), BF16),
        pltpu.VMEM((8, 128, 256), BF16),
        pltpu.VMEM((8, 256, 128), BF16),
        pltpu.VMEM(field_shape, BF16),
        pltpu.VMEM((2, 272, 1024), F32),
        pltpu.VMEM(field_shape, BF16),
        pltpu.VMEM((2, 272, 1024), F32),
        pltpu.VMEM(field_shape, BF16),
        pltpu.VMEM(field_shape, F32),
        pltpu.VMEM((512, 512), BF16),
        pltpu.VMEM((2, 4, 32, 896), F32),
        pltpu.VMEM((2, 4, 32, 896), F32),
        pltpu.VMEM((2, 8, 8, 896), F32),
        pltpu.VMEM((2, 8, 8, 896), F32),
        pltpu.VMEM((2, 8, 64, 128), F32),
        pltpu.VMEM((2, 8, 64, 128), F32),
        pltpu.VMEM((4, 2, 16, 128), F32),
        pltpu.VMEM((4, 2, 16, 128), F32),
        pltpu.VMEM((2, 384, 256), BF16),
        pltpu.VMEM((8, 272, 256), F32),
        pltpu.VMEM((272, 256), F32),
        pltpu.VMEM((272, 256), F32),
        pltpu.VMEM((4, 2, 16, 128), F32),
        pltpu.VMEM((4, 2, 16, 128), F32),
        pltpu.VMEM((2, 8, 4, 16, 128), F32),
        pltpu.VMEM((2, 1024, 256), BF16),
        pltpu.VMEM((2, 8, 8, 896), F32),
        pltpu.VMEM((2, 8, 8, 896), F32),
        pltpu.VMEM((2, 4, 32, 896), F32),
        pltpu.VMEM((2, 4, 32, 896), F32),
        pltpu.VMEM((64, 128), F32),
        dma((7,)),
        dma((2, 4)), dma((2, 4)), dma((2, 8)), dma((2, 8)), dma((2, 8)), dma((2, 8)), dma((4,)), dma((4,)),
        dma((4,)), dma((4,)), dma((2, 8)), dma((2, 8)), dma((2, 8)), dma((2, 8)), dma((2, 4)), dma((2, 4)),
        dma((2,)),
    ]
    ig, wg = pl.pallas_call(
        body,
        out_shape=(
            jax.ShapeDtypeStruct(field_shape, BF16),
            jax.ShapeDtypeStruct((2, KZ * 16, C * C), F32),
        ),
        in_specs=[vmem, vmem, vmem, smem] + [vmem] * len(IN_VMEM) + [hbm] * (len(IN_HBM) + 2),
        out_specs=(hbm, hbm),
        scratch_shapes=scratch,
        compiler_params=pltpu.CompilerParams(
            collective_id=0, has_side_effects=True, vmem_limit_bytes=58 * 1024 * 1024
        ),
        cost_estimate=pl.CostEstimate(flops=10**10, bytes_accessed=2 * 10**7, transcendentals=0),
    )(
        f, point_weight, point_weight.T, point_bias,
        *[tabs[name] for name in IN_VMEM],
        *[tabs[name] for name in IN_HBM],
        cot, w,
    )
    input_grad = ig.reshape(1, C, 6, 32, 256)
    weight_grad = wg.reshape(2, KZ, 16, C * C)[:, :, :12].reshape(2, KZ, 6, 2, C * C)
    return (input_grad, weight_grad)


def solution(mesh):
    return jax.shard_map(
        per_device,
        mesh=mesh,
        in_specs=(
            P(None, None, "gx", "gy", None),
            P(None, None, "gx", "gy", None),
            P(None, None, "gy", "gx", None),
            P(),
            P(),
        ),
        out_specs=(P(None, None, "gx", "gy", None), P(None, None, "gy", "gx", None)),
        check_vma=False,
    )
```

```python
import math

import jax
import jax.numpy as jnp
import ml_dtypes
import numpy as np
from jax import lax
from jax.experimental import pallas as pl
from jax.experimental.pallas import tpu as pltpu
from jax.sharding import PartitionSpec as P

C = 32
NX = 192
NY = 256
NZ = 256
KX = 48
KY = 64
KZ = 17
SCALE = (NX * NY * NZ) ** (-0.5)
MESH = pl.DeviceIdType.MESH
F32 = jnp.float32
BF16 = jnp.bfloat16


def kept(count, number):
    half = number // 2
    return np.concatenate([np.arange(half), np.arange(half) + count - half])


def trig(points, freqs, count):
    angle = 2.0 * np.pi * ((points[:, None] * freqs[None, :]) % count) / count
    return np.cos(angle), np.sin(angle)


def hi_lo(table):
    table = np.asarray(table, np.float32)
    high = table.astype(ml_dtypes.bfloat16)
    low = (table - high.astype(np.float32)).astype(ml_dtypes.bfloat16)
    return high, low


def make_tables():
    z_cos, z_sin = trig(np.arange(NZ), np.arange(KZ), NZ)
    y_cos, y_sin = trig(np.arange(NY), kept(NY, KY), NY)
    x_cos, x_sin = trig(np.arange(NX), kept(NX, KX), NX)
    tabs = {}
    wz = np.zeros((4, NZ, 2, 2, 4, 16))
    zz = np.zeros((4, 2, 2, 4, 16, NZ))
    for c4 in range(4):
        wz[c4, :, 0, 0, c4, :] = z_cos[:, :16]
        wz[c4, :, 0, 1, c4, :] = -z_sin[:, :16]
        wz[c4, :, 1, 0, c4, :] = z_cos[:, 16:17]
        wz[c4, :, 1, 1, c4, :] = -z_sin[:, 16:17]
        zz[c4, 0, 0, c4] = z_cos[:, :16].T
        zz[c4, 0, 1, c4] = -z_sin[:, :16].T
        zz[c4, 1, 0, c4] = z_cos[:, 16:17].T
        zz[c4, 1, 1, c4] = -z_sin[:, 16:17].T
    tabs["wz"] = wz.reshape(4, NZ, 256).astype(np.float32).astype(ml_dtypes.bfloat16)
    tabs["zz"] = hi_lo(zz.reshape(4, 256, NZ))[0]
    s_at, zl_at, j_at = np.meshgrid(np.arange(8), np.arange(4), np.arange(2), indexing="ij")
    order = ((zl_at * 8 + s_at) * 2 + j_at).reshape(-1)
    yc = (y_cos * SCALE)[:, order].reshape(2, 128, 64)
    ys = (y_sin * SCALE)[:, order].reshape(2, 128, 64)
    inv = np.concatenate([yc, ys], 2)
    fwd = inv.transpose(0, 2, 1)
    tabs["t1"] = np.stack([np.concatenate([h, h, l], -1) for h, l in [hi_lo(fwd[0]), hi_lo(fwd[1])]])
    tabs["t1i"] = np.stack([np.concatenate([h, h, l], -1) for h, l in [hi_lo(inv[0]), hi_lo(inv[1])]])
    xt = np.stack([x_cos, x_sin]).reshape(2, 4, 8, 6, 2, 4, 6)
    t2 = np.zeros((4, 2, 4, 2, 4, 16, 6, 8, 8))
    for zl_to in range(4):
        for i in range(6):
            for j in range(2):
                block = xt[:, :, :, :, :, :, i]
                t2[:, :, zl_to, :, :, 2 * i + j, :, :, zl_to * 2 + j] = block.transpose(1, 4, 0, 5, 3, 2)
    t2 = t2[:, :, :, :, :, :12]
    fwd = t2.reshape(4, 8, 96, 384)
    tabs["t2"] = np.concatenate(hi_lo(fwd), 2)
    inv = t2.transpose(0, 6, 3, 7, 8, 1, 2, 4, 5).reshape(4, 6, 128, 384)
    tabs["t2i"] = np.concatenate(hi_lo(inv), 2)
    eye2, eye4 = np.eye(2), np.eye(4)
    ones16, ones32 = np.ones(16), np.ones(32)
    e1 = np.einsum("qr,cd,s,o->qcsrdo", eye2, eye4, ones16, ones32)
    tabs["e1"] = e1.reshape(128, 256)
    tabs["r2"] = e1.reshape(128, 256).T
    pick = np.eye(32).reshape(8, 4, 32)
    e2 = np.einsum("qr,bio,s,c->bqisrco", eye2, pick, ones16, np.ones(4)).reshape(8, 128, 256)
    tabs["e2"] = e2
    tabs["rr"] = e2.transpose(0, 2, 1)
    slot = np.zeros((6, 16, 16))
    for x in range(6):
        slot[x, x, :] = 1.0
    spread = np.einsum("qr,cd,xst->xqcsrdt", eye2, eye4, slot).reshape(6, 128, 128)
    tabs["spread"] = spread.transpose(1, 0, 2).reshape(128, 768)
    tabs["gather"] = spread.transpose(0, 2, 1)
    tabs["a16"] = np.repeat(np.eye(32), 16, axis=0)
    perm = np.zeros((4, 16, 56))
    for y in range(4):
        perm[y, np.arange(12), 12 * y + np.arange(12)] = 1.0
        perm[y, 12, 48 + y] = 1.0
    tabs["perm"] = perm.reshape(64, 56)
    tabs["unperm"] = perm.reshape(64, 56).T
    for name in ("perm", "unperm", "e1", "r2", "e2", "rr", "spread", "gather", "a16"):
        tabs[name] = tabs[name].astype(ml_dtypes.bfloat16)
    return tabs


TABLES = make_tables()
IN_VMEM = ("wz", "t1", "a16", "spread", "gather", "t1i", "e1", "r2", "perm", "unperm")
IN_HBM = ("t2", "t2i", "zz", "e2", "rr")


def mm(left, right):
    return jnp.dot(left, right, preferred_element_type=F32)


def halves(values):
    high = values.astype(BF16)
    return high, (values - high.astype(F32)).astype(BF16)


def gelu_slope(values):
    size = jnp.abs(values)
    below = 1.0 + (0.3275911 / math.sqrt(2.0)) * size
    t = pl.reciprocal(below, approx=True)
    t = t * (2.0 - below * t)
    poly = t * (0.127414796 + t * (-0.142248368 + t * (0.7107068705 + t * (-0.7265760135 + t * 0.5307027145))))
    bell = jnp.exp2((-0.5 / math.log(2.0)) * (values * values))
    part = bell * ((1.0 / math.sqrt(2.0 * math.pi)) * size - poly)
    return jnp.where(values >= 0.0, 1.0 + part, -part)


def swap(values, first):
    lane = lax.broadcasted_iota(jnp.int32, (values.shape[0], 128), 1)
    sign = jnp.where(lane < 64, first, -first)
    parts = [
        pltpu.roll(values[:, at : at + 128], 64, 1) * sign for at in range(0, values.shape[1], 128)
    ]
    return parts[0] if len(parts) == 1 else jnp.concatenate(parts, 1)


def slot_of(shape):
    return lax.broadcasted_iota(jnp.int32, shape, len(shape) - 1) % 16


def spread_rows(block):
    slots = slot_of((16, 128))
    rows = lax.broadcasted_iota(jnp.int32, (16, 128), 0)
    parts = [jnp.where(slots == k, block, 0.0) for k in range(16)]
    parts.append(jnp.where(slots == rows, jnp.broadcast_to(block[12:13], (16, 128)), 0.0))
    return jnp.concatenate(parts, 0)


def gather_rows(values):
    slots = slot_of((16, 128))
    rows = lax.broadcasted_iota(jnp.int32, (16, 128), 0)
    total = jnp.where(slots == 0, values[0:16], 0.0)
    for k in range(1, 16):
        total = total + jnp.where(slots == k, values[16 * k : 16 * k + 16], 0.0)
    last = jnp.sum(jnp.where(slots == rows, values[256:272], 0.0), axis=0, keepdims=True)
    return jnp.where(rows == 12, jnp.broadcast_to(last, (16, 128)), total)


def split_mm(table, values):
    high, low = halves(values)
    return mm(table, high) + mm(table, low)


def body(
    pw, bias, wz, t1, a16, spread, gather, t1i, e1, r2, perm, unperm,
    t2_hbm, t2i_hbm, zz_hbm, e2_hbm, rr_hbm, f_hbm, cot_hbm, w_hbm,
    ig_hbm, wg_hbm,
    t2, t2i, zz, e2, rr, f, cot, w_in, w, ig, wg_out, wg, pg, lin, kron,
    u, r0, vs, r1, rsb, r3a, s4b, md, xb, mexp, gexp, acc,
    mq, r4, r3b, xb2, vs2, r1s, ys, r0s, zb,
    f_sem, local_sem, s1s, s1r, s2s, s2r, s3s, s3r, s4s, s4r, g4s, g4r, g3s, g3r, g2s, g2r, g1s, g1r, out_sem,
):
    gx = lax.axis_index("gx")
    gy = lax.axis_index("gy")
    zl, s = gx // 8, gx % 8
    zh, yy = gy // 4, gy % 4
    zz_me = zh * 4 + zl

    def y_id(to):
        return (gx, zh * 4 + to)

    def s_id(to):
        return (zl * 8 + to, gy)

    def z_id(to):
        return ((to % 4) * 8 + s, (to // 4) * 4 + yy)

    def each(low, high, fn):
        def step(d, carry):
            fn(d)
            return carry

        lax.fori_loop(low, high, step, 0)

    def f_load(to, h):
        return pltpu.make_async_copy(f_hbm.at[to, h], f.at[to, h], f_sem.at[to, h])

    for h in range(2):
        each(1, 5, lambda d, h=h: f_load((yy + d) % 4, h).start())

    barrier = pltpu.get_barrier_semaphore()
    for d in range(1, 4):
        pl.semaphore_signal(barrier, inc=1, device_id=y_id((yy + d) % 4), device_id_type=MESH)
    for d in range(1, 8):
        pl.semaphore_signal(barrier, inc=1, device_id=s_id((s + d) % 8), device_id_type=MESH)
        pl.semaphore_signal(barrier, inc=1, device_id=z_id((zz_me + d) % 8), device_id_type=MESH)

    loads = [
        pltpu.make_async_copy(src, dst, local_sem.at[n])
        for n, (src, dst) in enumerate(
            [
                (w_hbm, w_in),
                (t2_hbm.at[zl], t2),
                (rr_hbm, rr),
                (t2i_hbm.at[zl], t2i),
                (cot_hbm, cot),
                (zz_hbm, zz),
                (e2_hbm, e2),
            ]
        )
    ]
    for load in loads:
        load.start()
    pl.semaphore_wait(barrier, 17)

    def y_send(src, dst, send, recv, to):
        return pltpu.make_async_remote_copy(src, dst, send, recv, device_id=y_id(to), device_id_type=MESH)

    def s_send(src, dst, send, recv, to):
        return pltpu.make_async_remote_copy(src, dst, send, recv, device_id=s_id(to), device_id_type=MESH)

    def z_send(src, dst, send, recv, to):
        return pltpu.make_async_remote_copy(src, dst, send, recv, device_id=z_id(to), device_id_type=MESH)

    def c1(h, d):
        to = (yy + d) % 4
        return y_send(u.at[h, to], r0.at[h, yy], s1s.at[h, d], s1r.at[h, d], to)

    def w1(h, d):
        fr = (yy + 4 - d) % 4
        return y_send(u.at[h, fr], r0.at[h, fr], s1s.at[h, d], s1r.at[h, d], fr)

    def c2(h, d):
        to = (s + d) % 8
        return s_send(vs.at[h, to], r1.at[h, s], s2s.at[h, d], s2r.at[h, d], to)

    def w2(h, d):
        fr = (s + 8 - d) % 8
        return s_send(vs.at[h, fr], r1.at[h, fr], s2s.at[h, d], s2r.at[h, d], fr)

    def c3(h, d):
        to = (zz_me + d) % 8
        return z_send(rsb.at[h, to], r3a.at[h, zz_me], s3s.at[h, d], s3r.at[h, d], to)

    def w3(h, d):
        fr = (zz_me + 8 - d) % 8
        return z_send(rsb.at[h, fr], r3a.at[h, fr], s3s.at[h, d], s3r.at[h, d], fr)

    def c4(h, d):
        to = (yy + d) % 4
        return y_send(s4b.at[h, to], md.at[h, yy], s4s.at[h, d], s4r.at[h, d], to)

    def w4(h, d):
        fr = (yy + 4 - d) % 4
        return y_send(s4b.at[h, fr], md.at[h, fr], s4s.at[h, d], s4r.at[h, d], fr)

    def k4(h, d):
        to = (yy + d) % 4
        return y_send(mq.at[h, to], r4.at[h, yy], g4s.at[h, d], g4r.at[h, d], to)

    def v4(h, d):
        fr = (yy + 4 - d) % 4
        return y_send(mq.at[h, fr], r4.at[h, fr], g4s.at[h, d], g4r.at[h, d], fr)

    def k3(h, d):
        to = (zz_me + d) % 8
        return z_send(r3b.at[h, zz_me], r3b.at[h, zz_me], g3s.at[h, d], g3r.at[h, d], to)

    def v3(h, d):
        fr = (zz_me + 8 - d) % 8
        return z_send(r3b.at[h, fr], r3b.at[h, fr], g3s.at[h, d], g3r.at[h, d], fr)

    def k2(h, d):
        to = (s + d) % 8
        return s_send(vs2.at[h, to], r1s.at[h, s], g2s.at[h, d], g2r.at[h, d], to)

    def v2(h, d):
        fr = (s + 8 - d) % 8
        return s_send(vs2.at[h, fr], r1s.at[h, fr], g2s.at[h, d], g2r.at[h, d], fr)

    def k1(h, d):
        to = (yy + d) % 4
        return y_send(ys.at[h, to], r0s.at[h, yy], g1s.at[h, d], g1r.at[h, d], to)

    def v1(h, d):
        fr = (yy + 4 - d) % 4
        return y_send(ys.at[h, fr], r0s.at[h, fr], g1s.at[h, d], g1r.at[h, d], fr)

    def z_analysis(source, h, to, dest):
        total = None
        for q in range(4):
            term = mm(source[to, h, q].reshape(192, 256), wz[q])
            total = term if total is None else total + term
        slots = slot_of((32, 128))
        last = None
        for x in range(6):
            rows = total[32 * x : 32 * x + 32]
            dest[:, 128 * x : 128 * x + 128] = rows[:, :128]
            part = jnp.where(slots == x, rows[:, 128:], 0.0)
            last = part if last is None else last + part
        dest[:, 768:896] = last

    def analysis_start(source, h, load):
        def one(d):
            to = (yy + d) % 4
            if load:
                f_load(to, h).wait()
            z_analysis(source, h, to, u.at[h, to])
            c1(h, d).start()

        each(1, 4, one)
        if load:
            f_load(yy, h).wait()
        z_analysis(source, h, yy, r0.at[h, yy])

    def y_analysis(h):
        table = t1.at[zh]
        for at, wide in ((0, 256), (256, 256), (512, 256), (768, 128)):
            high, low = halves(r0[h, :, :, at : at + wide].reshape(128, wide))
            both = jnp.concatenate([high, low], 0)
            out = mm(table[:, 0:256], both) + mm(table[:, 256:384], high)
            vs[h, :, :, at : at + wide] = (out[:64] + swap(out[64:], 1.0)).reshape(8, 8, wide)

    def x_analysis_load(h):
        last = r1[h, :, :, 768:896].reshape(64, 128).astype(BF16)
        last = mm(last, spread[...]).astype(BF16)
        for x in range(6):
            at = 128 * x
            xb[64 * x : 64 * x + 64, 0:128] = r1[h, :, :, at : at + 128].reshape(64, 128).astype(BF16)
            xb[64 * x : 64 * x + 64, 128:256] = last[:, at : at + 128]

    def x_analysis_store(out, dest):
        out = out[:48] + swap(out[48:], 1.0)
        rows = lax.broadcasted_iota(jnp.int32, (48, 128), 0)
        last = jnp.where(slot_of((48, 128)) == rows % 12, out[:, 128:], 0.0)
        ends = lax.broadcasted_iota(jnp.int32, (8, 128), 0)
        tail = jnp.zeros((8, 128), F32)
        for y in range(4):
            line = jnp.sum(jnp.where(rows // 12 == y, last, 0.0), axis=0, keepdims=True)
            tail = jnp.where(ends == y, jnp.broadcast_to(line, (8, 128)), tail)
        dest[0:48, :] = out[:, :128]
        dest[48:56, :] = tail

    def x_analysis(h):
        for group in ((1, 2, 3, 4), (5, 6, 7, 8)):
            to = [(zz_me + d) % 8 for d in group]
            out = mm(jnp.concatenate([t2[z] for z in to], 0), xb[...])
            for n, d in enumerate(group):
                part = out[192 * n : 192 * n + 96] + out[192 * n + 96 : 192 * n + 192]
                if d < 8:
                    x_analysis_store(part, rsb.at[h, to[n]])
                    c3(h, d).start()
                else:
                    x_analysis_store(part, r3a.at[h, zz_me])

    def analysis(meanwhile, received):
        meanwhile()
        for h in range(2):
            each(1, 4, lambda d: w1(h, d).wait_recv())
            y_analysis(h)
            each(1, 8, lambda d: c2(h, d).start())
            r1[h, s] = vs[h, s]
            each(1, 8, lambda d: w2(h, d).wait_recv())
            x_analysis_load(h)
            x_analysis(h)
        for h in range(2):
            each(1, 8, lambda d: w3(h, d).wait_recv())
            total = r3a[h, 0]
            for z in range(1, 8):
                total = total + r3a[h, z]
            s4b[h] = split_mm(perm[...], total).reshape(4, 16, 128)
            each(1, 4, lambda d: c4(h, d).start())
            md[h, yy] = s4b[h, yy]
            each(1, 4, lambda d: w4(h, d).wait_recv())
            received(h)

    def analysis_end():
        for h in range(2):
            each(1, 4, lambda d: c1(h, d).wait_send())
            each(1, 8, lambda d: c2(h, d).wait_send())
            each(1, 8, lambda d: c3(h, d).wait_send())
            each(1, 4, lambda d: c4(h, d).wait_send())

    def x_synthesis_load(h):
        xb2[:, 0:128] = r3b[h, :, 0:48, :].reshape(384, 128).astype(BF16)
        rows = lax.broadcasted_iota(jnp.int32, (48, 128), 0)
        own = slot_of((48, 128)) == rows % 12
        for z in range(8):
            last = jnp.zeros((48, 128), F32)
            for y in range(4):
                line = jnp.broadcast_to(r3b[h, z, 48 + y : 49 + y, :], (48, 128))
                last = jnp.where(rows // 12 == y, line, last)
            xb2[48 * z : 48 * z + 48, 128:256] = jnp.where(own, last, 0.0).astype(BF16)

    def x_synthesis(h):
        total = None
        for group in ((0, 1), (2, 3), (4, 5)):
            out = mm(jnp.concatenate([t2i[x] for x in group], 0), xb2[...])
            for n, x in enumerate(group):
                part = out[256 * n : 256 * n + 128] + out[256 * n + 128 : 256 * n + 256]
                part = part[:64] + swap(part[64:], -1.0)
                vs2[h, :, :, 128 * x : 128 * x + 128] = part[:, :128].reshape(8, 8, 128)
                high, low = halves(part[:, 128:])
                last = mm(high, gather[x]) + mm(low, gather[x])
                total = last if total is None else total + last
        vs2[h, :, :, 768:896] = total.reshape(8, 8, 128)

    def y_synthesis(h):
        table = t1i.at[zh]
        for at, wide in ((0, 256), (256, 256), (512, 256), (768, 128)):
            values = r1s[h, :, :, at : at + wide].reshape(64, wide)
            high, low = halves(jnp.concatenate([values, swap(values, -1.0)], 0))
            out = mm(table[:, 0:256], jnp.concatenate([high, low], 0)) + mm(table[:, 256:384], high)
            ys[h, :, :, at : at + wide] = out.reshape(4, 32, wide)

    def z_synthesis(h, finish):
        slots = slot_of((32, 128))
        for fr in range(4):
            last = r0s[h, fr, :, 768:896]
            for x in range(6):
                at = 192 * fr + 32 * x
                zb[at : at + 32, 0:128] = r0s[h, fr, :, 128 * x : 128 * x + 128].astype(BF16)
                zb[at : at + 32, 128:256] = jnp.where(slots == x, last, 0.0).astype(BF16)

        def one(q):
            out = mm(zb[...], zz[q])
            for fr in range(4):
                finish(fr, h, q, out[192 * fr : 192 * fr + 192].reshape(6, 32, 256))

        each(0, 4, one)

    def synthesis(meanwhile, finish, after):
        for h in range(2):
            each(1, 4, lambda d: v4(h, d).wait_recv())
            r3b[h, zz_me] = split_mm(unperm[...], r4[h].reshape(64, 128))
            each(1, 8, lambda d: k3(h, d).start())
        meanwhile()
        for h in range(2):
            each(1, 8, lambda d: v3(h, d).wait_recv())
            x_synthesis_load(h)
            x_synthesis(h)
            each(1, 8, lambda d: k2(h, d).start())
            r1s[h, s] = vs2[h, s]
            each(1, 8, lambda d: v2(h, d).wait_recv())
            y_synthesis(h)
            each(1, 4, lambda d: k1(h, d).start())
            r0s[h, yy] = ys[h, yy]
        for h in range(2):
            each(1, 4, lambda d: v1(h, d).wait_recv())
            z_synthesis(h, finish)
            after(h)
        for h in range(2):
            each(1, 4, lambda d: k4(h, d).wait_send())
            each(1, 8, lambda d: k3(h, d).wait_send())
            each(1, 8, lambda d: k2(h, d).wait_send())
            each(1, 4, lambda d: k1(h, d).wait_send())

    def channel_map(wide, source):
        rows = lax.broadcasted_iota(jnp.int32, (512, 512), 0) % 16
        columns = lax.broadcasted_iota(jnp.int32, (512, 512), 1) % 16
        full = lax.dot_general(
            wide.astype(BF16), a16[...], (((1,), (1,)), ((), ())), preferred_element_type=F32
        )
        kron[...] = jnp.where(rows == columns, full, 0.0).astype(BF16)

        def one(x):
            for at in (0, 16):
                block = source[:, :, :, x, at : at + 16, :].reshape(512, 256)
                out = mm(kron[...], block)
                lin[:, :, :, x, at : at + 16, :] = out.reshape(4, 2, 4, 16, 256)

        each(0, 6, one)

    def lanes(b):
        return pl.ds(pl.multiple_of(b * 128, 128), 128)

    def weights_in():
        loads[0].wait()

        def one(k):
            for part in range(2):
                for i in range(6):
                    w[part, k, 2 * i : 2 * i + 2, :] = w_in[part, k, i]
                w[part, k, 12:16, :] = jnp.zeros((4, 1024), F32)

        each(0, KZ, one)

    def weight_grad_out():
        def one(k):
            for part in range(2):
                for i in range(6):
                    wg_out[part, k, i] = wg[part, k, 2 * i : 2 * i + 2, :]

        each(0, KZ, one)
        wg_copy.start()

    def w_at(part, b):
        return w[part, :, :, lanes(b)].reshape(272, 128)

    def mix_one(h):
        def one(y):
            b = 2 * y + h
            modes = split_left(spread_rows(md[h, y]), e1[...])
            mexp[b] = modes
            real, imag = modes[:, :128], modes[:, 128:]
            w_real, w_imag = w_at(0, b), w_at(1, b)
            acc[:, :128] += w_real * real - w_imag * imag
            acc[:, 128:] += w_real * imag + w_imag * real

        each(0, 4, one)

    def mix_two():
        high, low = halves(acc[...])
        for h in range(2):

            def two(y, h=h):
                table = rr[2 * y + h]
                mq[h, y] = gather_rows(mm(high, table) + mm(low, table))

            each(0, 4, two)
            each(1, 4, lambda d: k4(h, d).start())
            r4[h, yy] = mq[h, yy]

    def split_left(values, table):
        high, low = halves(values)
        return mm(high, table) + mm(low, table)

    def back_one(h):
        def one(y):
            gexp[...] += split_left(spread_rows(md[h, y]), e2[2 * y + h])

        each(0, 4, one)

    def back_two():
        for h in range(2):

            def two(y, h=h):
                b = 2 * y + h
                g_real, g_imag = gexp[:, :128], gexp[:, 128:]
                w_real, w_imag = w_at(0, b), w_at(1, b)
                real = w_real * g_real + w_imag * g_imag
                imag = w_real * g_imag - w_imag * g_real
                mq[h, y] = gather_rows(split_left(jnp.concatenate([real, imag], 1), r2[...]))

            each(0, 4, two)
            each(1, 4, lambda d: k4(h, d).start())
            r4[h, yy] = mq[h, yy]

    def weight_grad():
        def one(b):
            g_real, g_imag = gexp[:, :128], gexp[:, 128:]
            real, imag = mexp[b, :, :128], mexp[b, :, 128:]
            wg[0, :, :, lanes(b)] = (real * g_real + imag * g_imag).reshape(KZ, 16, 128)
            wg[1, :, :, lanes(b)] = (real * g_imag - imag * g_real).reshape(KZ, 16, 128)

        each(0, 8, one)
        weight_grad_out()

    def finish_pre(fr, h, q, spectral):
        pre = spectral + lin[fr, h, q] + bias[fr * 8 + h * 4 + q]
        pg[fr, h, q] = (cot[fr, h, q].astype(F32) * gelu_slope(pre)).astype(BF16)

    def finish_grad(fr, h, q, spectral):
        ig[fr, h, q] = (spectral + lin[fr, h, q]).astype(BF16)

    wg_copy = pltpu.make_async_copy(wg_out, wg_hbm, out_sem.at[0])

    def ig_copy(h):
        return pltpu.make_async_copy(ig.at[:, h], ig_hbm.at[:, h], out_sem.at[1 + h])

    def first_meanwhile():
        channel_map(mm(a16[...], pw[...]), f)
        weights_in()
        acc[...] = jnp.zeros_like(acc)
        loads[1].wait()

    def second_meanwhile():
        wide = lax.dot_general(a16[...], pw[...], (((1,), (1,)), ((), ())), preferred_element_type=F32)
        channel_map(wide, pg)
        gexp[...] = jnp.zeros_like(gexp)

    def wait_loads():
        for load in loads[3:]:
            load.wait()

    for h in range(2):
        analysis_start(f, h, True)
    analysis(first_meanwhile, mix_one)
    loads[2].wait()
    mix_two()
    analysis_end()
    synthesis(wait_loads, finish_pre, lambda h: analysis_start(pg, h, False))
    analysis(second_meanwhile, back_one)
    back_two()
    synthesis(weight_grad, finish_grad, lambda h: ig_copy(h).start())
    analysis_end()
    wg_copy.wait()
    ig_copy(0).wait()
    ig_copy(1).wait()


def per_device(input_field, cotangent, spectral_weights, point_weight, point_bias):
    field_shape = (4, 2, 4, 6, 32, 256)
    w_shape = spectral_weights.shape
    tabs = {name: jnp.asarray(value) for name, value in TABLES.items()}
    vmem = pl.BlockSpec(memory_space=pltpu.VMEM)
    smem = pl.BlockSpec(memory_space=pltpu.SMEM)
    hbm = pl.BlockSpec(memory_space=pl.ANY)
    dma = pltpu.SemaphoreType.DMA
    scratch = [
        pltpu.VMEM((8, 192, 384), BF16),
        pltpu.VMEM((6, 256, 384), BF16),
        pltpu.VMEM((4, 256, 256), BF16),
        pltpu.VMEM((8, 128, 256), BF16),
        pltpu.VMEM((8, 256, 128), BF16),
        pltpu.VMEM(field_shape, BF16),
        pltpu.VMEM(field_shape, BF16),
        pltpu.VMEM(w_shape, F32),
        pltpu.VMEM((2, KZ, 16, 1024), F32),
        pltpu.VMEM(field_shape, BF16),
        pltpu.VMEM(w_shape, F32),
        pltpu.VMEM((2, KZ, 16, 1024), F32),
        pltpu.VMEM(field_shape, BF16),
        pltpu.VMEM(field_shape, F32),
        pltpu.VMEM((512, 512), BF16),
        pltpu.VMEM((2, 4, 32, 896), F32),
        pltpu.VMEM((2, 4, 32, 896), F32),
        pltpu.VMEM((2, 8, 8, 896), F32),
        pltpu.VMEM((2, 8, 8, 896), F32),
        pltpu.VMEM((2, 8, 56, 128), F32),
        pltpu.VMEM((2, 8, 56, 128), F32),
        pltpu.VMEM((2, 4, 16, 128), F32),
        pltpu.VMEM((2, 4, 16, 128), F32),
        pltpu.VMEM((384, 256), BF16),
        pltpu.VMEM((8, 272, 256), F32),
        pltpu.VMEM((272, 256), F32),
        pltpu.VMEM((272, 256), F32),
        pltpu.VMEM((2, 4, 16, 128), F32),
        pltpu.VMEM((2, 4, 16, 128), F32),
        pltpu.VMEM((2, 8, 56, 128), F32),
        pltpu.VMEM((384, 256), BF16),
        pltpu.VMEM((2, 8, 8, 896), F32),
        pltpu.VMEM((2, 8, 8, 896), F32),
        pltpu.VMEM((2, 4, 32, 896), F32),
        pltpu.VMEM((2, 4, 32, 896), F32),
        pltpu.VMEM((768, 256), BF16),
        dma((4, 2)),
        dma((7,)),
        dma((2, 4)), dma((2, 4)), dma((2, 8)), dma((2, 8)), dma((2, 8)), dma((2, 8)), dma((2, 4)), dma((2, 4)),
        dma((2, 4)), dma((2, 4)), dma((2, 8)), dma((2, 8)), dma((2, 8)), dma((2, 8)), dma((2, 4)), dma((2, 4)),
        dma((3,)),
    ]
    ig, wg = pl.pallas_call(
        body,
        out_shape=(
            jax.ShapeDtypeStruct(field_shape, BF16),
            jax.ShapeDtypeStruct(w_shape, F32),
        ),
        in_specs=[vmem, smem] + [vmem] * len(IN_VMEM) + [hbm] * (len(IN_HBM) + 3),
        out_specs=(hbm, hbm),
        scratch_shapes=scratch,
        compiler_params=pltpu.CompilerParams(
            collective_id=0, has_side_effects=True, vmem_limit_bytes=58 * 1024 * 1024
        ),
        cost_estimate=pl.CostEstimate(flops=10**10, bytes_accessed=2 * 10**7, transcendentals=0),
    )(
        point_weight, point_bias,
        *[tabs[name] for name in IN_VMEM],
        *[tabs[name] for name in IN_HBM],
        input_field.reshape(field_shape), cotangent.reshape(field_shape), spectral_weights,
    )
    return (ig.reshape(input_field.shape), wg)


def solution(mesh):
    return jax.shard_map(
        per_device,
        mesh=mesh,
        in_specs=(
            P(None, None, "gx", "gy", None),
            P(None, None, "gx", "gy", None),
            P(None, None, "gy", "gx", None),
            P(),
            P(),
        ),
        out_specs=(P(None, None, "gx", "gy", None), P(None, None, "gy", "gx", None)),
        check_vma=False,
    )
```

```python
import math

import jax
import jax.numpy as jnp
import ml_dtypes
import numpy as np
from jax import lax
from jax.experimental import pallas as pl
from jax.experimental.pallas import tpu as pltpu
from jax.sharding import PartitionSpec as P

C = 32
NX = 192
NY = 256
NZ = 256
KX = 48
KY = 64
KZ = 17
SCALE = (NX * NY * NZ) ** (-0.5)
MESH = pl.DeviceIdType.MESH
F32 = jnp.float32
BF16 = jnp.bfloat16


def kept(count, number):
    half = number // 2
    return np.concatenate([np.arange(half), np.arange(half) + count - half])


def trig(points, freqs, count):
    angle = 2.0 * np.pi * ((points[:, None] * freqs[None, :]) % count) / count
    return np.cos(angle), np.sin(angle)


def hi_lo(table):
    table = np.asarray(table, np.float32)
    high = table.astype(ml_dtypes.bfloat16)
    low = (table - high.astype(np.float32)).astype(ml_dtypes.bfloat16)
    return high, low


def make_tables():
    z_cos, z_sin = trig(np.arange(NZ), np.arange(KZ), NZ)
    y_cos, y_sin = trig(np.arange(NY), kept(NY, KY), NY)
    x_cos, x_sin = trig(np.arange(NX), kept(NX, KX), NX)
    tabs = {}
    wz = np.zeros((4, NZ, 2, 2, 4, 16))
    zz = np.zeros((4, 2, 2, 4, 16, NZ))
    for c4 in range(4):
        wz[c4, :, 0, 0, c4, :] = z_cos[:, :16]
        wz[c4, :, 0, 1, c4, :] = -z_sin[:, :16]
        wz[c4, :, 1, 0, c4, :] = z_cos[:, 16:17]
        wz[c4, :, 1, 1, c4, :] = -z_sin[:, 16:17]
        zz[c4, 0, 0, c4] = z_cos[:, :16].T
        zz[c4, 0, 1, c4] = -z_sin[:, :16].T
        zz[c4, 1, 0, c4] = z_cos[:, 16:17].T
        zz[c4, 1, 1, c4] = -z_sin[:, 16:17].T
    tabs["wz"] = wz.reshape(4, NZ, 256).astype(np.float32).astype(ml_dtypes.bfloat16)
    tabs["zz"] = hi_lo(zz.reshape(4, 256, NZ))[0]
    s_at, zl_at, j_at = np.meshgrid(np.arange(8), np.arange(4), np.arange(2), indexing="ij")
    order = ((zl_at * 8 + s_at) * 2 + j_at).reshape(-1)
    yc = (y_cos * SCALE)[:, order].reshape(2, 128, 64)
    ys = (y_sin * SCALE)[:, order].reshape(2, 128, 64)
    inv = np.concatenate([yc, ys], 2)
    fwd = inv.transpose(0, 2, 1)
    tabs["t1"] = np.stack([np.concatenate([h, h, l], -1) for h, l in [hi_lo(fwd[0]), hi_lo(fwd[1])]])
    tabs["t1i"] = np.stack([np.concatenate([h, h, l], -1) for h, l in [hi_lo(inv[0]), hi_lo(inv[1])]])
    xt = np.stack([x_cos, x_sin]).reshape(2, 4, 8, 6, 2, 4, 6)
    t2 = np.zeros((4, 2, 4, 2, 4, 16, 6, 8, 8))
    for zl_to in range(4):
        for i in range(6):
            for j in range(2):
                block = xt[:, :, :, :, :, :, i]
                t2[:, :, zl_to, :, :, 2 * i + j, :, :, zl_to * 2 + j] = block.transpose(1, 4, 0, 5, 3, 2)
    t2 = t2[:, :, :, :, :, :12]
    fwd = t2.reshape(4, 8, 96, 384)
    tabs["t2"] = np.concatenate(hi_lo(fwd), 2)
    inv = t2.transpose(0, 6, 3, 7, 8, 1, 2, 4, 5).reshape(4, 6, 128, 384)
    tabs["t2i"] = np.concatenate(hi_lo(inv), 2)
    eye2, eye4 = np.eye(2), np.eye(4)
    ones16, ones32 = np.ones(16), np.ones(32)
    e1 = np.einsum("qr,cd,s,o->qcsrdo", eye2, eye4, ones16, ones32)
    tabs["e1"] = e1.reshape(128, 256)
    tabs["r2"] = e1.reshape(128, 256).T
    pick = np.eye(32).reshape(8, 4, 32)
    e2 = np.einsum("qr,bio,s,c->bqisrco", eye2, pick, ones16, np.ones(4)).reshape(8, 128, 256)
    tabs["e2"] = e2
    tabs["rr"] = e2.transpose(0, 2, 1)
    slot = np.zeros((6, 16, 16))
    for x in range(6):
        slot[x, x, :] = 1.0
    spread = np.einsum("qr,cd,xst->xqcsrdt", eye2, eye4, slot).reshape(6, 128, 128)
    tabs["spread"] = spread.transpose(1, 0, 2).reshape(128, 768)
    tabs["gather"] = spread.transpose(0, 2, 1)
    tabs["a16"] = np.repeat(np.eye(32), 16, axis=0)
    perm = np.zeros((4, 16, 56))
    for y in range(4):
        perm[y, np.arange(12), 12 * y + np.arange(12)] = 1.0
        perm[y, 12, 48 + y] = 1.0
    tabs["perm"] = perm.reshape(64, 56)
    tabs["unperm"] = perm.reshape(64, 56).T
    for name in ("perm", "unperm", "e1", "r2", "e2", "rr", "spread", "gather", "a16"):
        tabs[name] = tabs[name].astype(ml_dtypes.bfloat16)
    return tabs


TABLES = make_tables()
IN_VMEM = ("wz", "t1", "a16", "spread", "gather", "t1i", "e1", "r2", "perm", "unperm")
IN_HBM = ("t2", "t2i", "zz", "e2", "rr")


def mm(left, right):
    return jnp.dot(left, right, preferred_element_type=F32)


def halves(values):
    high = values.astype(BF16)
    return high, (values - high.astype(F32)).astype(BF16)


def gelu_slope(values):
    size = jnp.abs(values)
    below = 1.0 + (0.3275911 / math.sqrt(2.0)) * size
    t = pl.reciprocal(below, approx=True)
    t = t * (2.0 - below * t)
    poly = t * (0.127414796 + t * (-0.142248368 + t * (0.7107068705 + t * (-0.7265760135 + t * 0.5307027145))))
    bell = jnp.exp2((-0.5 / math.log(2.0)) * (values * values))
    part = bell * ((1.0 / math.sqrt(2.0 * math.pi)) * size - poly)
    return jnp.where(values >= 0.0, 1.0 + part, -part)


def swap(values, first):
    lane = lax.broadcasted_iota(jnp.int32, (values.shape[0], 128), 1)
    sign = jnp.where(lane < 64, first, -first)
    parts = [
        pltpu.roll(values[:, at : at + 128], 64, 1) * sign for at in range(0, values.shape[1], 128)
    ]
    return parts[0] if len(parts) == 1 else jnp.concatenate(parts, 1)


def slot_of(shape):
    return lax.broadcasted_iota(jnp.int32, shape, len(shape) - 1) % 16


def spread_rows(block):
    slots = slot_of((16, 128))
    rows = lax.broadcasted_iota(jnp.int32, (16, 128), 0)
    parts = [jnp.where(slots == k, block, 0.0) for k in range(16)]
    parts.append(jnp.where(slots == rows, jnp.broadcast_to(block[12:13], (16, 128)), 0.0))
    return jnp.concatenate(parts, 0)


def gather_rows(values):
    slots = slot_of((16, 128))
    rows = lax.broadcasted_iota(jnp.int32, (16, 128), 0)
    total = jnp.where(slots == 0, values[0:16], 0.0)
    for k in range(1, 16):
        total = total + jnp.where(slots == k, values[16 * k : 16 * k + 16], 0.0)
    last = jnp.sum(jnp.where(slots == rows, values[256:272], 0.0), axis=0, keepdims=True)
    return jnp.where(rows == 12, jnp.broadcast_to(last, (16, 128)), total)


def split_mm(table, values):
    high, low = halves(values)
    return mm(table, high) + mm(table, low)


def body(
    pw, bias, wz, t1, a16, spread, gather, t1i, e1, r2, perm, unperm,
    t2_hbm, t2i_hbm, zz_hbm, e2_hbm, rr_hbm, f_hbm, cot_hbm, w_hbm,
    ig_hbm, wg_hbm,
    t2, t2i, zz, e2, rr, f, cot, w_in, w, ig, wg_out, wg, pg, lin, kron,
    u, r0, vs, r1, rsb, r3a, s4b, md, xb, mexp, gexp, acc,
    mq, r4, r3b, xb2, vs2, r1s, ys, r0s, zb, rel, rel_g, mrg,
    f_sem, local_sem, s1s, s1r, s2s, s2r, s3s, s3r, s4s, s4r, g4s, g4r, g3s, g3r, g2s, g2r, g1s, g1r, out_sem,
    rs, rr_sem, fs, fr_sem, rgs, rgr, fgs, fgr, ms, mr,
):
    gx = lax.axis_index("gx")
    gy = lax.axis_index("gy")
    zl, s = gx // 8, gx % 8
    zh, yy = gy // 4, gy % 4
    zz_me = zh * 4 + zl

    def y_id(to):
        return (gx, zh * 4 + to)

    def s_id(to):
        return (zl * 8 + to, gy)

    def z_id(to):
        return ((to % 4) * 8 + s, (to // 4) * 4 + yy)

    def each(low, high, fn):
        def step(d, carry):
            fn(d)
            return carry

        lax.fori_loop(low, high, step, 0)

    def f_load(to, h):
        return pltpu.make_async_copy(f_hbm.at[to, h], f.at[to, h], f_sem.at[to, h])

    for h in range(2):
        each(1, 5, lambda d, h=h: f_load((yy + d) % 4, h).start())

    barrier = pltpu.get_barrier_semaphore()
    for d in range(1, 4):
        pl.semaphore_signal(barrier, inc=1, device_id=y_id((yy + d) % 4), device_id_type=MESH)
    for d in range(1, 8):
        pl.semaphore_signal(barrier, inc=1, device_id=s_id((s + d) % 8), device_id_type=MESH)
        pl.semaphore_signal(barrier, inc=1, device_id=z_id((zz_me + d) % 8), device_id_type=MESH)

    loads = [
        pltpu.make_async_copy(src, dst, local_sem.at[n])
        for n, (src, dst) in enumerate(
            [
                (w_hbm, w_in),
                (t2_hbm.at[zl], t2),
                (rr_hbm, rr),
                (t2i_hbm.at[zl], t2i),
                (cot_hbm, cot),
                (zz_hbm, zz),
                (e2_hbm, e2),
            ]
        )
    ]
    for load in loads:
        load.start()
    pl.semaphore_wait(barrier, 17)

    def y_send(src, dst, send, recv, to):
        return pltpu.make_async_remote_copy(src, dst, send, recv, device_id=y_id(to), device_id_type=MESH)

    def s_send(src, dst, send, recv, to):
        return pltpu.make_async_remote_copy(src, dst, send, recv, device_id=s_id(to), device_id_type=MESH)

    def z_send(src, dst, send, recv, to):
        return pltpu.make_async_remote_copy(src, dst, send, recv, device_id=z_id(to), device_id_type=MESH)

    def c1(h, d):
        to = (yy + d) % 4
        return y_send(u.at[h, to], r0.at[h, yy], s1s.at[h, d], s1r.at[h, d], to)

    def w1(h, d):
        fr = (yy + 4 - d) % 4
        return y_send(u.at[h, fr], r0.at[h, fr], s1s.at[h, d], s1r.at[h, d], fr)

    def c2(h, d):
        to = (s + d) % 8
        return s_send(vs.at[h, to], r1.at[h, s], s2s.at[h, d], s2r.at[h, d], to)

    def w2(h, d):
        fr = (s + 8 - d) % 8
        return s_send(vs.at[h, fr], r1.at[h, fr], s2s.at[h, d], s2r.at[h, d], fr)

    def c3(h, d):
        to = (zz_me + d) % 8
        return z_send(rsb.at[h, to], r3a.at[h, zz_me], s3s.at[h, d], s3r.at[h, d], to)

    def w3(h, d):
        fr = (zz_me + 8 - d) % 8
        return z_send(rsb.at[h, fr], r3a.at[h, fr], s3s.at[h, d], s3r.at[h, d], fr)

    def c4(h, d):
        to = (yy + d) % 4
        return y_send(s4b.at[h, to], md.at[h, yy], s4s.at[h, d], s4r.at[h, d], to)

    def w4(h, d):
        fr = (yy + 4 - d) % 4
        return y_send(s4b.at[h, fr], md.at[h, fr], s4s.at[h, d], s4r.at[h, d], fr)

    def k4(h, d):
        to = (yy + d) % 4
        return y_send(mq.at[h, to], r4.at[h, yy], g4s.at[h, d], g4r.at[h, d], to)

    def v4(h, d):
        fr = (yy + 4 - d) % 4
        return y_send(mq.at[h, fr], r4.at[h, fr], g4s.at[h, d], g4r.at[h, d], fr)

    def k3(h, d):
        to = (zz_me + d) % 8
        return z_send(r3b.at[h, zz_me], r3b.at[h, zz_me], g3s.at[h, d], g3r.at[h, d], to)

    def v3(h, d):
        fr = (zz_me + 8 - d) % 8
        return z_send(r3b.at[h, fr], r3b.at[h, fr], g3s.at[h, d], g3r.at[h, d], fr)

    def k2(h, d):
        to = (s + d) % 8
        return s_send(vs2.at[h, to], r1s.at[h, s], g2s.at[h, d], g2r.at[h, d], to)

    def v2(h, d):
        fr = (s + 8 - d) % 8
        return s_send(vs2.at[h, fr], r1s.at[h, fr], g2s.at[h, d], g2r.at[h, d], fr)

    def k1(h, d):
        to = (yy + d) % 4
        return y_send(ys.at[h, to], r0s.at[h, yy], g1s.at[h, d], g1r.at[h, d], to)

    def v1(h, d):
        fr = (yy + 4 - d) % 4
        return y_send(ys.at[h, fr], r0s.at[h, fr], g1s.at[h, d], g1r.at[h, d], fr)

    def relay(h, part, source, buffer, send, recv):
        rows = pl.ds(16 * part, 16)
        to = (yy + 1 + 2 * part) % 4
        return y_send(source.at[h, (yy + 2) % 4, rows], buffer.at[h, part], send.at[h, part], recv.at[h, part], to)

    def pass_on(h, part, buffer, dest, send, recv):
        to = (yy + 1 + 2 * part) % 4
        fr = (yy + 3 + 2 * part) % 4
        return y_send(
            buffer.at[h, part], dest.at[h, fr, pl.ds(16 * part, 16)], send.at[h, part], recv.at[h, part], to
        )

    def passed(h, part, buffer, dest, send, recv):
        fr = (yy + 3 + 2 * part) % 4
        return y_send(
            buffer.at[h, part],
            dest.at[h, (yy + 2) % 4, pl.ds(16 * part, 16)],
            send.at[h, part],
            recv.at[h, part],
            fr,
        )

    relay_f = lambda h, part: relay(h, part, u, rel, rs, rr_sem)
    pass_f = lambda h, part: pass_on(h, part, rel, r0, fs, fr_sem)
    passed_f = lambda h, part: passed(h, part, rel, r0, fs, fr_sem)
    relay_g = lambda h, part: relay(h, part, ys, rel_g, rgs, rgr)
    pass_g = lambda h, part: pass_on(h, part, rel_g, r0s, fgs, fgr)
    passed_g = lambda h, part: passed(h, part, rel_g, r0s, fgs, fgr)

    def forward(h, first, second):
        for part in range(2):
            first(h, part).wait_recv()
            second(h, part).start()

    def far_block(h):
        step = 6 if h == 0 else 2
        return z_send(rsb.at[h, (zz_me + 4) % 8], mrg.at[h], ms.at[h], mr.at[h], (zz_me + step) % 8)

    def far_pass(h):
        step = 2 if h == 0 else 6
        at = r3b.at[h, (zz_me + 8 - step) % 8]
        return z_send(at, at, g3s.at[h, 4], g3r.at[h, 4], (zz_me + step) % 8)

    def far_passed(h):
        step = 2 if h == 0 else 6
        at = r3b.at[h, (zz_me + 4) % 8]
        return z_send(at, at, g3s.at[h, 4], g3r.at[h, 4], (zz_me + 8 - step) % 8)

    NEAR = (1, 2, 3, 5, 6, 7)

    def z_analysis(source, h, to, dest):
        total = None
        for q in range(4):
            term = mm(source[to, h, q].reshape(192, 256), wz[q])
            total = term if total is None else total + term
        slots = slot_of((32, 128))
        last = None
        for x in range(6):
            rows = total[32 * x : 32 * x + 32]
            dest[:, 128 * x : 128 * x + 128] = rows[:, :128]
            part = jnp.where(slots == x, rows[:, 128:], 0.0)
            last = part if last is None else last + part
        dest[:, 768:896] = last

    def analysis_far(source, h, load):
        to = (yy + 2) % 4
        if load:
            f_load(to, h).wait()
        z_analysis(source, h, to, u.at[h, to])
        for part in range(2):
            relay_f(h, part).start()

    def analysis_near(source, h, load):
        def one(n):
            to = (yy + 1 + 2 * n) % 4
            if load:
                f_load(to, h).wait()
            z_analysis(source, h, to, u.at[h, to])
            c1(h, 1 + 2 * n).start()

        each(0, 2, one)

    def analysis_own(source, h, load):
        if load:
            f_load(yy, h).wait()
        z_analysis(source, h, yy, r0.at[h, yy])

    def y_analysis(h):
        table = t1.at[zh]
        for at, wide in ((0, 256), (256, 256), (512, 256), (768, 128)):
            high, low = halves(r0[h, :, :, at : at + wide].reshape(128, wide))
            both = jnp.concatenate([high, low], 0)
            out = mm(table[:, 0:256], both) + mm(table[:, 256:384], high)
            vs[h, :, :, at : at + wide] = (out[:64] + swap(out[64:], 1.0)).reshape(8, 8, wide)

    def x_analysis_load(h):
        last = r1[h, :, :, 768:896].reshape(64, 128).astype(BF16)
        last = mm(last, spread[...]).astype(BF16)
        for x in range(6):
            at = 128 * x
            xb[64 * x : 64 * x + 64, 0:128] = r1[h, :, :, at : at + 128].reshape(64, 128).astype(BF16)
            xb[64 * x : 64 * x + 64, 128:256] = last[:, at : at + 128]

    def x_analysis_store(out, dest):
        out = out[:48] + swap(out[48:], 1.0)
        rows = lax.broadcasted_iota(jnp.int32, (48, 128), 0)
        last = jnp.where(slot_of((48, 128)) == rows % 12, out[:, 128:], 0.0)
        ends = lax.broadcasted_iota(jnp.int32, (8, 128), 0)
        tail = jnp.zeros((8, 128), F32)
        for y in range(4):
            line = jnp.sum(jnp.where(rows // 12 == y, last, 0.0), axis=0, keepdims=True)
            tail = jnp.where(ends == y, jnp.broadcast_to(line, (8, 128)), tail)
        dest[0:48, :] = out[:, :128]
        dest[48:56, :] = tail

    def x_analysis(h):
        step = 6 if h == 0 else 2
        for group in ((4, 1, 3, 7), (5, 8 - step, step, 8)):
            to = [(zz_me + d) % 8 for d in group]
            out = mm(jnp.concatenate([t2[z] for z in to], 0), xb[...])
            for n, d in enumerate(group):
                part = out[192 * n : 192 * n + 96] + out[192 * n + 96 : 192 * n + 192]
                if d == 8:
                    x_analysis_store(part, r3a.at[h, zz_me])
                    continue
                x_analysis_store(part, rsb.at[h, to[n]])
                if d == 4:
                    far_block(h).start()
                elif d != step:
                    c3(h, d).start()
        far_block(h).wait_recv()
        at = (zz_me + step) % 8
        rsb[h, at] = rsb[h, at] + mrg[h]
        c3(h, step).start()

    def analysis(meanwhile, received):
        meanwhile()
        forward(1, relay_f, pass_f)
        for h in range(2):
            for d in (1, 3):
                w1(h, d).wait_recv()
            for part in range(2):
                passed_f(h, part).wait_recv()
            y_analysis(h)
            each(1, 8, lambda d: c2(h, d).start())
            r1[h, s] = vs[h, s]
            each(1, 8, lambda d: w2(h, d).wait_recv())
            x_analysis_load(h)
            x_analysis(h)
        for h in range(2):
            total = r3a[h, zz_me]
            for d in NEAR:
                w3(h, d).wait_recv()
                total = total + r3a[h, (zz_me + 8 - d) % 8]
            s4b[h] = split_mm(perm[...], total).reshape(4, 16, 128)
            each(1, 4, lambda d: c4(h, d).start())
            md[h, yy] = s4b[h, yy]
            each(1, 4, lambda d: w4(h, d).wait_recv())
            received(h)

    def analysis_end():
        for h in range(2):
            for d in (1, 3):
                c1(h, d).wait_send()
            for part in range(2):
                relay_f(h, part).wait_send()
                pass_f(h, part).wait_send()
            each(1, 8, lambda d: c2(h, d).wait_send())
            for d in NEAR:
                c3(h, d).wait_send()
            far_block(h).wait_send()
            each(1, 4, lambda d: c4(h, d).wait_send())

    def x_synthesis_load(h):
        xb2[:, 0:128] = r3b[h, :, 0:48, :].reshape(384, 128).astype(BF16)
        rows = lax.broadcasted_iota(jnp.int32, (48, 128), 0)
        own = slot_of((48, 128)) == rows % 12
        for z in range(8):
            last = jnp.zeros((48, 128), F32)
            for y in range(4):
                line = jnp.broadcast_to(r3b[h, z, 48 + y : 49 + y, :], (48, 128))
                last = jnp.where(rows // 12 == y, line, last)
            xb2[48 * z : 48 * z + 48, 128:256] = jnp.where(own, last, 0.0).astype(BF16)

    def x_synthesis(h):
        total = None
        for group in ((0, 1), (2, 3), (4, 5)):
            out = mm(jnp.concatenate([t2i[x] for x in group], 0), xb2[...])
            for n, x in enumerate(group):
                part = out[256 * n : 256 * n + 128] + out[256 * n + 128 : 256 * n + 256]
                part = part[:64] + swap(part[64:], -1.0)
                vs2[h, :, :, 128 * x : 128 * x + 128] = part[:, :128].reshape(8, 8, 128)
                high, low = halves(part[:, 128:])
                last = mm(high, gather[x]) + mm(low, gather[x])
                total = last if total is None else total + last
        vs2[h, :, :, 768:896] = total.reshape(8, 8, 128)

    def y_synthesis(h):
        table = t1i.at[zh]
        for at, wide in ((0, 256), (256, 256), (512, 256), (768, 128)):
            values = r1s[h, :, :, at : at + wide].reshape(64, wide)
            high, low = halves(jnp.concatenate([values, swap(values, -1.0)], 0))
            out = mm(table[:, 0:256], jnp.concatenate([high, low], 0)) + mm(table[:, 256:384], high)
            ys[h, :, :, at : at + wide] = out.reshape(4, 32, wide)

    def z_synthesis(h, fr, finish):
        slots = slot_of((32, 128))
        last = r0s[h, fr, :, 768:896]
        for x in range(6):
            zb[32 * x : 32 * x + 32, 0:128] = r0s[h, fr, :, 128 * x : 128 * x + 128].astype(BF16)
            zb[32 * x : 32 * x + 32, 128:256] = jnp.where(slots == x, last, 0.0).astype(BF16)

        def one(q):
            finish(fr, h, q, mm(zb[...], zz[q]).reshape(6, 32, 256))

        each(0, 4, one)

    def z_synthesis_near(h, finish):
        z_synthesis(h, yy, finish)

        def one(n):
            v1(h, 1 + 2 * n).wait_recv()
            z_synthesis(h, (yy + 3 + 2 * n) % 4, finish)

        each(0, 2, one)

    def z_synthesis_far(h, finish):
        for part in range(2):
            passed_g(h, part).wait_recv()
        z_synthesis(h, (yy + 2) % 4, finish)

    def synthesis(meanwhile, finish, after):
        for h in range(2):
            each(1, 4, lambda d: v4(h, d).wait_recv())
            r3b[h, zz_me] = split_mm(unperm[...], r4[h].reshape(64, 128))
            for d in ((2, 6, 1, 3, 5, 7), (6, 2, 1, 3, 5, 7))[h]:
                k3(h, d).start()
        for h in range(2):
            v3(h, (2, 6)[h]).wait_recv()
            far_pass(h).start()
        meanwhile()
        for h in range(2):
            for d in ((6, 1, 3, 5, 7), (2, 1, 3, 5, 7))[h]:
                v3(h, d).wait_recv()
            far_passed(h).wait_recv()
            x_synthesis_load(h)
            x_synthesis(h)
            each(1, 8, lambda d: k2(h, d).start())
            r1s[h, s] = vs2[h, s]
            if h == 1:
                forward(0, relay_g, pass_g)
            each(1, 8, lambda d: v2(h, d).wait_recv())
            y_synthesis(h)
            for part in range(2):
                relay_g(h, part).start()
            for d in (1, 3):
                k1(h, d).start()
            r0s[h, yy] = ys[h, yy]
        z_synthesis_near(0, finish)
        forward(1, relay_g, pass_g)
        z_synthesis_far(0, finish)
        after(0)
        z_synthesis_near(1, finish)
        after(1)
        z_synthesis_far(1, finish)
        after(2)
        for h in range(2):
            each(1, 4, lambda d: k4(h, d).wait_send())
            for d in NEAR:
                k3(h, d).wait_send()
            far_pass(h).wait_send()
            each(1, 8, lambda d: k2(h, d).wait_send())
            for d in (1, 3):
                k1(h, d).wait_send()
            for part in range(2):
                relay_g(h, part).wait_send()
                pass_g(h, part).wait_send()

    def channel_map(wide, source):
        rows = lax.broadcasted_iota(jnp.int32, (512, 512), 0) % 16
        columns = lax.broadcasted_iota(jnp.int32, (512, 512), 1) % 16
        full = lax.dot_general(
            wide.astype(BF16), a16[...], (((1,), (1,)), ((), ())), preferred_element_type=F32
        )
        kron[...] = jnp.where(rows == columns, full, 0.0).astype(BF16)

        def one(x):
            for at in (0, 16):
                block = source[:, :, :, x, at : at + 16, :].reshape(512, 256)
                out = mm(kron[...], block)
                lin[:, :, :, x, at : at + 16, :] = out.reshape(4, 2, 4, 16, 256)

        each(0, 6, one)

    def lanes(b):
        return pl.ds(pl.multiple_of(b * 128, 128), 128)

    def weights_in():
        loads[0].wait()

        def one(k):
            for part in range(2):
                for i in range(6):
                    w[part, k, 2 * i : 2 * i + 2, :] = w_in[part, k, i]
                w[part, k, 12:16, :] = jnp.zeros((4, 1024), F32)

        each(0, KZ, one)

    def weight_grad_out():
        def one(k):
            for part in range(2):
                for i in range(6):
                    wg_out[part, k, i] = wg[part, k, 2 * i : 2 * i + 2, :]

        each(0, KZ, one)
        wg_copy.start()

    def w_at(part, b):
        return w[part, :, :, lanes(b)].reshape(272, 128)

    def mix_one(h):
        def one(y):
            b = 2 * y + h
            modes = split_left(spread_rows(md[h, y]), e1[...])
            mexp[b] = modes
            real, imag = modes[:, :128], modes[:, 128:]
            w_real, w_imag = w_at(0, b), w_at(1, b)
            acc[:, :128] += w_real * real - w_imag * imag
            acc[:, 128:] += w_real * imag + w_imag * real

        each(0, 4, one)

    def mix_two():
        high, low = halves(acc[...])
        for h in range(2):

            def two(y, h=h):
                table = rr[2 * y + h]
                mq[h, y] = gather_rows(mm(high, table) + mm(low, table))

            each(0, 4, two)
            each(1, 4, lambda d: k4(h, d).start())
            r4[h, yy] = mq[h, yy]

    def split_left(values, table):
        high, low = halves(values)
        return mm(high, table) + mm(low, table)

    def back_one(h):
        def one(y):
            gexp[...] += split_left(spread_rows(md[h, y]), e2[2 * y + h])

        each(0, 4, one)

    def back_two():
        for h in range(2):

            def two(y, h=h):
                b = 2 * y + h
                g_real, g_imag = gexp[:, :128], gexp[:, 128:]
                w_real, w_imag = w_at(0, b), w_at(1, b)
                real = w_real * g_real + w_imag * g_imag
                imag = w_real * g_imag - w_imag * g_real
                mq[h, y] = gather_rows(split_left(jnp.concatenate([real, imag], 1), r2[...]))

            each(0, 4, two)
            each(1, 4, lambda d: k4(h, d).start())
            r4[h, yy] = mq[h, yy]

    def weight_grad():
        def one(b):
            g_real, g_imag = gexp[:, :128], gexp[:, 128:]
            real, imag = mexp[b, :, :128], mexp[b, :, 128:]
            wg[0, :, :, lanes(b)] = (real * g_real + imag * g_imag).reshape(KZ, 16, 128)
            wg[1, :, :, lanes(b)] = (real * g_imag - imag * g_real).reshape(KZ, 16, 128)

        each(0, 8, one)
        weight_grad_out()

    def finish_pre(fr, h, q, spectral):
        pre = spectral + lin[fr, h, q] + bias[fr * 8 + h * 4 + q]
        pg[fr, h, q] = (cot[fr, h, q].astype(F32) * gelu_slope(pre)).astype(BF16)

    def finish_grad(fr, h, q, spectral):
        ig[fr, h, q] = (spectral + lin[fr, h, q]).astype(BF16)

    wg_copy = pltpu.make_async_copy(wg_out, wg_hbm, out_sem.at[0])

    def ig_copy(h):
        return pltpu.make_async_copy(ig.at[:, h], ig_hbm.at[:, h], out_sem.at[1 + h])

    def first_meanwhile():
        channel_map(mm(a16[...], pw[...]), f)
        weights_in()
        acc[...] = jnp.zeros_like(acc)
        loads[1].wait()

    def second_meanwhile():
        wide = lax.dot_general(a16[...], pw[...], (((1,), (1,)), ((), ())), preferred_element_type=F32)
        channel_map(wide, pg)
        gexp[...] = jnp.zeros_like(gexp)

    def wait_loads():
        for load in loads[3:]:
            load.wait()

    def second_start(step):
        if step == 0:
            analysis_far(pg, 0, False)
            analysis_near(pg, 0, False)
            analysis_own(pg, 0, False)
        elif step == 1:
            forward(0, relay_f, pass_f)
        else:
            analysis_far(pg, 1, False)
            analysis_near(pg, 1, False)
            analysis_own(pg, 1, False)

    def last_copies(step):
        if step != 1:
            ig_copy(step // 2).start()

    analysis_far(f, 0, True)
    analysis_near(f, 0, True)
    analysis_far(f, 1, True)
    analysis_own(f, 0, True)
    forward(0, relay_f, pass_f)
    analysis_near(f, 1, True)
    analysis_own(f, 1, True)
    analysis(first_meanwhile, mix_one)
    loads[2].wait()
    mix_two()
    analysis_end()
    synthesis(wait_loads, finish_pre, second_start)
    analysis(second_meanwhile, back_one)
    back_two()
    synthesis(weight_grad, finish_grad, last_copies)
    analysis_end()
    wg_copy.wait()
    ig_copy(0).wait()
    ig_copy(1).wait()


def per_device(input_field, cotangent, spectral_weights, point_weight, point_bias):
    field_shape = (4, 2, 4, 6, 32, 256)
    w_shape = spectral_weights.shape
    tabs = {name: jnp.asarray(value) for name, value in TABLES.items()}
    vmem = pl.BlockSpec(memory_space=pltpu.VMEM)
    smem = pl.BlockSpec(memory_space=pltpu.SMEM)
    hbm = pl.BlockSpec(memory_space=pl.ANY)
    dma = pltpu.SemaphoreType.DMA
    scratch = [
        pltpu.VMEM((8, 192, 384), BF16),
        pltpu.VMEM((6, 256, 384), BF16),
        pltpu.VMEM((4, 256, 256), BF16),
        pltpu.VMEM((8, 128, 256), BF16),
        pltpu.VMEM((8, 256, 128), BF16),
        pltpu.VMEM(field_shape, BF16),
        pltpu.VMEM(field_shape, BF16),
        pltpu.VMEM(w_shape, F32),
        pltpu.VMEM((2, KZ, 16, 1024), F32),
        pltpu.VMEM(field_shape, BF16),
        pltpu.VMEM(w_shape, F32),
        pltpu.VMEM((2, KZ, 16, 1024), F32),
        pltpu.VMEM(field_shape, BF16),
        pltpu.VMEM(field_shape, F32),
        pltpu.VMEM((512, 512), BF16),
        pltpu.VMEM((2, 4, 32, 896), F32),
        pltpu.VMEM((2, 4, 32, 896), F32),
        pltpu.VMEM((2, 8, 8, 896), F32),
        pltpu.VMEM((2, 8, 8, 896), F32),
        pltpu.VMEM((2, 8, 56, 128), F32),
        pltpu.VMEM((2, 8, 56, 128), F32),
        pltpu.VMEM((2, 4, 16, 128), F32),
        pltpu.VMEM((2, 4, 16, 128), F32),
        pltpu.VMEM((384, 256), BF16),
        pltpu.VMEM((8, 272, 256), F32),
        pltpu.VMEM((272, 256), F32),
        pltpu.VMEM((272, 256), F32),
        pltpu.VMEM((2, 4, 16, 128), F32),
        pltpu.VMEM((2, 4, 16, 128), F32),
        pltpu.VMEM((2, 8, 56, 128), F32),
        pltpu.VMEM((384, 256), BF16),
        pltpu.VMEM((2, 8, 8, 896), F32),
        pltpu.VMEM((2, 8, 8, 896), F32),
        pltpu.VMEM((2, 4, 32, 896), F32),
        pltpu.VMEM((2, 4, 32, 896), F32),
        pltpu.VMEM((192, 256), BF16),
        pltpu.VMEM((2, 2, 16, 896), F32),
        pltpu.VMEM((2, 2, 16, 896), F32),
        pltpu.VMEM((2, 56, 128), F32),
        dma((4, 2)),
        dma((7,)),
        dma((2, 4)), dma((2, 4)), dma((2, 8)), dma((2, 8)), dma((2, 8)), dma((2, 8)), dma((2, 4)), dma((2, 4)),
        dma((2, 4)), dma((2, 4)), dma((2, 8)), dma((2, 8)), dma((2, 8)), dma((2, 8)), dma((2, 4)), dma((2, 4)),
        dma((3,)),
        dma((2, 2)), dma((2, 2)), dma((2, 2)), dma((2, 2)), dma((2, 2)), dma((2, 2)), dma((2, 2)), dma((2, 2)),
        dma((2,)), dma((2,)),
    ]
    ig, wg = pl.pallas_call(
        body,
        out_shape=(
            jax.ShapeDtypeStruct(field_shape, BF16),
            jax.ShapeDtypeStruct(w_shape, F32),
        ),
        in_specs=[vmem, smem] + [vmem] * len(IN_VMEM) + [hbm] * (len(IN_HBM) + 3),
        out_specs=(hbm, hbm),
        scratch_shapes=scratch,
        compiler_params=pltpu.CompilerParams(
            collective_id=0, has_side_effects=True, vmem_limit_bytes=58 * 1024 * 1024
        ),
        cost_estimate=pl.CostEstimate(flops=10**10, bytes_accessed=2 * 10**7, transcendentals=0),
    )(
        point_weight, point_bias,
        *[tabs[name] for name in IN_VMEM],
        *[tabs[name] for name in IN_HBM],
        input_field.reshape(field_shape), cotangent.reshape(field_shape), spectral_weights,
    )
    return (ig.reshape(input_field.shape), wg)


def solution(mesh):
    return jax.shard_map(
        per_device,
        mesh=mesh,
        in_specs=(
            P(None, None, "gx", "gy", None),
            P(None, None, "gx", "gy", None),
            P(None, None, "gy", "gx", None),
            P(),
            P(),
        ),
        out_specs=(P(None, None, "gx", "gy", None), P(None, None, "gy", "gx", None)),
        check_vma=False,
    )
```

```python
import math

import jax
import jax.numpy as jnp
import ml_dtypes
import numpy as np
from jax import lax
from jax.experimental import pallas as pl
from jax.experimental.pallas import tpu as pltpu
from jax.sharding import PartitionSpec as P

C = 32
NX = 192
NY = 256
NZ = 256
KX = 48
KY = 64
KZ = 17
SCALE = (NX * NY * NZ) ** (-0.5)
MESH = pl.DeviceIdType.MESH
F32 = jnp.float32
BF16 = jnp.bfloat16


def kept(count, number):
    half = number // 2
    return np.concatenate([np.arange(half), np.arange(half) + count - half])


def trig(points, freqs, count):
    angle = 2.0 * np.pi * ((points[:, None] * freqs[None, :]) % count) / count
    return np.cos(angle), np.sin(angle)


def hi_lo(table):
    table = np.asarray(table, np.float32)
    high = table.astype(ml_dtypes.bfloat16)
    low = (table - high.astype(np.float32)).astype(ml_dtypes.bfloat16)
    return high, low


def make_tables():
    z_cos, z_sin = trig(np.arange(NZ), np.arange(KZ), NZ)
    y_cos, y_sin = trig(np.arange(NY), kept(NY, KY), NY)
    x_cos, x_sin = trig(np.arange(NX), kept(NX, KX), NX)
    tabs = {}
    wz = np.zeros((4, NZ, 2, 2, 4, 16))
    zz = np.zeros((4, 2, 2, 4, 16, NZ))
    for c4 in range(4):
        wz[c4, :, 0, 0, c4, :] = z_cos[:, :16]
        wz[c4, :, 0, 1, c4, :] = -z_sin[:, :16]
        wz[c4, :, 1, 0, c4, :] = z_cos[:, 16:17]
        wz[c4, :, 1, 1, c4, :] = -z_sin[:, 16:17]
        zz[c4, 0, 0, c4] = z_cos[:, :16].T
        zz[c4, 0, 1, c4] = -z_sin[:, :16].T
        zz[c4, 1, 0, c4] = z_cos[:, 16:17].T
        zz[c4, 1, 1, c4] = -z_sin[:, 16:17].T
    tabs["wz"] = wz.reshape(4, NZ, 256).astype(np.float32).astype(ml_dtypes.bfloat16)
    tabs["zz"] = hi_lo(zz.reshape(4, 256, NZ))[0]
    s_at, zl_at, j_at = np.meshgrid(np.arange(8), np.arange(4), np.arange(2), indexing="ij")
    order = ((zl_at * 8 + s_at) * 2 + j_at).reshape(-1)
    yc = (y_cos * SCALE)[:, order].reshape(2, 128, 64)
    ys = (y_sin * SCALE)[:, order].reshape(2, 128, 64)
    inv = np.concatenate([yc, ys], 2)
    fwd = inv.transpose(0, 2, 1)
    tabs["t1"] = np.stack([np.concatenate([h, h, l], -1) for h, l in [hi_lo(fwd[0]), hi_lo(fwd[1])]])
    tabs["t1i"] = np.stack([np.concatenate([h, h, l], -1) for h, l in [hi_lo(inv[0]), hi_lo(inv[1])]])
    xt = np.stack([x_cos, x_sin]).reshape(2, 4, 8, 6, 2, 4, 6)
    t2 = np.zeros((4, 2, 4, 2, 4, 16, 6, 8, 8))
    for zl_to in range(4):
        for i in range(6):
            for j in range(2):
                block = xt[:, :, :, :, :, :, i]
                t2[:, :, zl_to, :, :, 2 * i + j, :, :, zl_to * 2 + j] = block.transpose(1, 4, 0, 5, 3, 2)
    fwd = t2.reshape(4, 8, 128, 384)
    tabs["t2"] = np.concatenate(hi_lo(fwd), 2)
    inv = t2.transpose(0, 6, 3, 7, 8, 1, 2, 4, 5).reshape(4, 6, 128, 512)
    tabs["t2i"] = np.concatenate(hi_lo(inv), 2)
    eye2, eye4 = np.eye(2), np.eye(4)
    ones16, ones32 = np.ones(16), np.ones(32)
    e1 = np.einsum("qr,cd,s,o->qcsrdo", eye2, eye4, ones16, ones32)
    tabs["e1"] = e1.reshape(128, 256)
    tabs["r2"] = e1.reshape(128, 256).T
    pick = np.eye(32).reshape(8, 4, 32)
    e2 = np.einsum("qr,bio,s,c->bqisrco", eye2, pick, ones16, np.ones(4)).reshape(8, 128, 256)
    tabs["e2"] = e2
    tabs["rr"] = e2.reshape(2, 2, 2, 128, 256).transpose(2, 0, 4, 1, 3).reshape(2, 2, 256, 256)
    slot = np.zeros((6, 16, 16))
    for x in range(6):
        slot[x, x, :] = 1.0
    spread = np.einsum("qr,cd,xst->xqcsrdt", eye2, eye4, slot).reshape(6, 128, 128)
    tabs["spread"] = spread.transpose(1, 0, 2).reshape(128, 768)
    tabs["gather"] = spread.transpose(0, 2, 1)
    tabs["a16"] = np.repeat(np.eye(32), 16, axis=0)
    for name in ("e1", "r2", "e2", "rr", "spread", "gather", "a16"):
        tabs[name] = tabs[name].astype(ml_dtypes.bfloat16)
    return tabs


TABLES = make_tables()
IN_VMEM = ("wz", "t1", "a16", "spread", "gather", "t1i", "e1", "r2")
IN_HBM = ("t2", "t2i", "zz", "e2", "rr")


def mm(left, right):
    return jnp.dot(left, right, preferred_element_type=F32)


def halves(values):
    high = values.astype(BF16)
    return high, (values - high.astype(F32)).astype(BF16)


def gelu_slope(values):
    size = jnp.abs(values)
    below = 1.0 + (0.3275911 / math.sqrt(2.0)) * size
    t = pl.reciprocal(below, approx=True)
    t = t * (2.0 - below * t)
    poly = t * (0.127414796 + t * (-0.142248368 + t * (0.7107068705 + t * (-0.7265760135 + t * 0.5307027145))))
    bell = jnp.exp2((-0.5 / math.log(2.0)) * (values * values))
    part = bell * ((1.0 / math.sqrt(2.0 * math.pi)) * size - poly)
    return jnp.where(values >= 0.0, 1.0 + part, -part)


def swap(values, first):
    lane = lax.broadcasted_iota(jnp.int32, (values.shape[0], 128), 1)
    sign = jnp.where(lane < 64, first, -first)
    parts = [
        pltpu.roll(values[:, at : at + 128], 64, 1) * sign for at in range(0, values.shape[1], 128)
    ]
    return parts[0] if len(parts) == 1 else jnp.concatenate(parts, 1)


def slot_of(shape):
    return lax.broadcasted_iota(jnp.int32, shape, len(shape) - 1) % 16


def spread_rows(block):
    slots = slot_of((16, 128))
    rows = lax.broadcasted_iota(jnp.int32, (16, 128), 0)
    parts = [jnp.where(slots == k, block, 0.0) for k in range(16)]
    parts.append(jnp.where(slots == rows, jnp.broadcast_to(block[12:13], (16, 128)), 0.0))
    return jnp.concatenate(parts, 0)


def gather_rows(values):
    slots = slot_of((16, 128))
    rows = lax.broadcasted_iota(jnp.int32, (16, 128), 0)
    total = jnp.where(slots == 0, values[0:16], 0.0)
    for k in range(1, 16):
        total = total + jnp.where(slots == k, values[16 * k : 16 * k + 16], 0.0)
    last = jnp.sum(jnp.where(slots == rows, values[256:272], 0.0), axis=0, keepdims=True)
    return jnp.where(rows == 12, jnp.broadcast_to(last, (16, 128)), total)


def split_mm(table, values):
    high, low = halves(values)
    return mm(table, high) + mm(table, low)


def body(
    pw, bias, wz, t1, a16, spread, gather, t1i, e1, r2,
    t2_hbm, t2i_hbm, zz_hbm, e2_hbm, rr_hbm, f_hbm, cot_hbm, w_hbm,
    ig_hbm, wg_hbm,
    t2, t2i, zz, e2, rr, f, cot, w_in, w, ig, wg_out, wg, pg, lin, kron,
    u, r0, vs, r1, rsb, r3a, md, xb, mexp, gexp, acc,
    mq, r3b, xb2, vs2, r1s, ys, r0s, zb,
    f_sem, local_sem, s1s, s1r, s2s, s2r, s3s, s3r, g3s, g3r, g2s, g2r, g1s, g1r, out_sem,
):
    gx = lax.axis_index("gx")
    gy = lax.axis_index("gy")
    zl, s = gx // 8, gx % 8
    zh, yy = gy // 4, gy % 4
    me = (zh * 4 + zl) * 4 + yy

    def y_id(to):
        return (gx, zh * 4 + to)

    def s_id(to):
        return (zl * 8 + to, gy)

    def m_id(to):
        return (((to // 4) % 4) * 8 + s, (to // 16) * 4 + to % 4)

    def each(low, high, fn):
        def step(d, carry):
            fn(d)
            return carry

        lax.fori_loop(low, high, step, 0)

    def f_load(to, h):
        return pltpu.make_async_copy(f_hbm.at[to, h], f.at[to, h], f_sem.at[to, h])

    for h in range(2):
        each(1, 5, lambda d, h=h: f_load((yy + d) % 4, h).start())

    barrier = pltpu.get_barrier_semaphore()

    def greet(device):
        pl.semaphore_signal(barrier, inc=1, device_id=device, device_id_type=MESH)

    each(1, 8, lambda d: greet(s_id((s + d) % 8)))
    each(1, 32, lambda d: greet(m_id((me + d) % 32)))

    loads = [
        pltpu.make_async_copy(src, dst, local_sem.at[n])
        for n, (src, dst) in enumerate(
            [
                (w_hbm, w_in),
                (t2_hbm.at[zl], t2),
                (rr_hbm, rr),
                (t2i_hbm.at[zl], t2i),
                (cot_hbm, cot),
                (zz_hbm, zz),
                (e2_hbm, e2),
            ]
        )
    ]
    for load in loads:
        load.start()
    pl.semaphore_wait(barrier, 38)

    def send(src, dst, send_sem, recv_sem, device):
        return pltpu.make_async_remote_copy(src, dst, send_sem, recv_sem, device_id=device, device_id_type=MESH)

    def c1(h, to):
        return send(u.at[h, to], r0.at[h, yy], s1s.at[h], s1r.at[h], y_id(to))

    def c2(h, to):
        return send(vs.at[h, to], r1.at[h, s], s2s.at[h], s2r.at[h], s_id(to))

    def c3(h, to):
        return send(rsb.at[h, to], r3a.at[h, me], s3s.at[h], s3r.at[h], m_id(to))

    def k3(h, to):
        return send(mq.at[h, to % 4], r3b.at[h, me], g3s.at[h], g3r.at[h], m_id(to))

    def k2(h, to):
        return send(vs2.at[h, to], r1s.at[h, s], g2s.at[h], g2r.at[h], s_id(to))

    def k1(h, to):
        return send(ys.at[h, to], r0s.at[h, yy], g1s.at[h], g1r.at[h, yy], y_id(to))

    def v1(h, fr):
        return send(ys.at[h, fr], r0s.at[h, fr], g1s.at[h], g1r.at[h, fr], y_id(fr))

    def all_of(buffer, h, count, sem):
        part = buffer.at[h, pl.ds(0, count)]
        pltpu.make_async_copy(part, part, sem.at[h]).wait()

    def z_analysis(source, h, to, dest):
        total = None
        for q in range(4):
            term = mm(source[to, h, q].reshape(192, 256), wz[q])
            total = term if total is None else total + term
        slots = slot_of((32, 128))
        last = None
        for x in range(6):
            rows = total[32 * x : 32 * x + 32]
            dest[:, 128 * x : 128 * x + 128] = rows[:, :128]
            part = jnp.where(slots == x, rows[:, 128:], 0.0)
            last = part if last is None else last + part
        dest[:, 768:896] = last

    def analysis_start(source, h):
        def one(d):
            to = (yy + d) % 4
            f_load(to, h).wait()
            z_analysis(source, h, to, u.at[h, to])
            c1(h, to).start()

        each(1, 4, one)
        f_load(yy, h).wait()
        z_analysis(source, h, yy, r0.at[h, yy])

    def y_analysis(h):
        table = t1.at[zh]
        for at, wide in ((0, 256), (256, 256), (512, 256), (768, 128)):
            high, low = halves(r0[h, :, :, at : at + wide].reshape(128, wide))
            both = jnp.concatenate([high, low], 0)
            out = mm(table[:, 0:256], both) + mm(table[:, 256:384], high)
            vs[h, :, :, at : at + wide] = (out[:64] + swap(out[64:], 1.0)).reshape(8, 8, wide)

    def x_analysis_load(h):
        last = r1[h, :, :, 768:896].reshape(64, 128).astype(BF16)
        last = mm(last, spread[...]).astype(BF16)
        for x in range(6):
            at = 128 * x
            xb[64 * x : 64 * x + 64, 0:128] = r1[h, :, :, at : at + 128].reshape(64, 128).astype(BF16)
            xb[64 * x : 64 * x + 64, 128:256] = last[:, at : at + 128]

    def x_analysis_store(out, h, z):
        out = out[:64] + swap(out[64:], 1.0)
        rows = lax.broadcasted_iota(jnp.int32, (64, 128), 0) % 16
        last = jnp.where(slot_of((64, 128)) == rows, out[:, 128:], 0.0)
        last = jnp.sum(last.reshape(4, 16, 128), axis=1, keepdims=True)
        last = jnp.broadcast_to(last, (4, 16, 128)).reshape(64, 128)
        rsb[h, pl.ds(4 * z, 4)] = jnp.where(rows == 12, last, out[:, :128]).reshape(4, 16, 128)

    def x_analysis(h):
        mine = me // 4
        for group in ((1, 2), (3, 4), (5, 6), (7, 8)):
            to = [(mine + d) % 8 for d in group]
            out = mm(jnp.concatenate([t2[z] for z in to], 0), xb[...])
            for n, d in enumerate(group):
                x_analysis_store(out[256 * n : 256 * n + 128] + out[256 * n + 128 : 256 * n + 256], h, to[n])
                each(0 if d < 8 else 1, 4, lambda y: c3(h, to[n] * 4 + (yy + y) % 4).start())
        r3a[h, me] = rsb[h, me]

    def analysis(meanwhile, received):
        meanwhile()
        for h in range(2):
            all_of(r0, h, 3, s1r)
            y_analysis(h)
            each(1, 8, lambda d: c2(h, (s + d) % 8).start())
            r1[h, s] = vs[h, s]
            all_of(r1, h, 7, s2r)
            x_analysis_load(h)
            x_analysis(h)
        for h in range(2):
            all_of(r3a, h, 31, s3r)
            total = r3a[h, 0:4]
            for z in range(1, 8):
                total = total + r3a[h, 4 * z : 4 * z + 4]
            md[h] = total
            received(h)

    def analysis_end():
        for h in range(2):
            all_of(u, h, 3, s1s)
            all_of(vs, h, 7, s2s)
            all_of(rsb, h, 31, s3s)

    def x_synthesis_load(h):
        main = r3b[h]
        rows = lax.broadcasted_iota(jnp.int32, (512, 128), 0) % 16
        last = jnp.broadcast_to(main[:, 12:13], (32, 16, 128)).reshape(512, 128)
        xb2[:, 0:128] = main.reshape(512, 128).astype(BF16)
        xb2[:, 128:256] = jnp.where(slot_of((512, 128)) == rows, last, 0.0).astype(BF16)

    def x_synthesis(h):
        total = None
        for group in ((0, 1), (2, 3), (4, 5)):
            out = mm(jnp.concatenate([t2i[x] for x in group], 0), xb2[...])
            for n, x in enumerate(group):
                part = out[256 * n : 256 * n + 128] + out[256 * n + 128 : 256 * n + 256]
                part = part[:64] + swap(part[64:], -1.0)
                vs2[h, :, :, 128 * x : 128 * x + 128] = part[:, :128].reshape(8, 8, 128)
                high, low = halves(part[:, 128:])
                last = mm(high, gather[x]) + mm(low, gather[x])
                total = last if total is None else total + last
        vs2[h, :, :, 768:896] = total.reshape(8, 8, 128)

    def y_synthesis(h):
        table = t1i.at[zh]
        for at, wide in ((0, 256), (256, 256), (512, 256), (768, 128)):
            values = r1s[h, :, :, at : at + wide].reshape(64, wide)
            high, low = halves(jnp.concatenate([values, swap(values, -1.0)], 0))
            out = mm(table[:, 0:256], jnp.concatenate([high, low], 0)) + mm(table[:, 256:384], high)
            ys[h, :, :, at : at + wide] = out.reshape(4, 32, wide)

    def z_synthesis(h, fr, finish):
        slots = slot_of((32, 128))
        last = r0s[h, fr, :, 768:896]
        for x in range(6):
            zb[32 * x : 32 * x + 32, 0:128] = r0s[h, fr, :, 128 * x : 128 * x + 128].astype(BF16)
            zb[32 * x : 32 * x + 32, 128:256] = jnp.where(slots == x, last, 0.0).astype(BF16)

        def one(q):
            finish(fr, h, q, mm(zb[...], zz[q]).reshape(6, 32, 256))

        each(0, 4, one)

    def synthesis(meanwhile, finish, after):
        meanwhile()
        for h in range(2):
            all_of(r3b, h, 31, g3r)
            x_synthesis_load(h)
            x_synthesis(h)
            each(1, 8, lambda d: k2(h, (s + d) % 8).start())
            r1s[h, s] = vs2[h, s]
            all_of(r1s, h, 7, g2r)
            y_synthesis(h)
            each(1, 4, lambda d: k1(h, (yy + d) % 4).start())
            r0s[h, yy] = ys[h, yy]
        for h in range(2):
            z_synthesis(h, yy, finish)

            def one(d, h=h):
                fr = (yy + 2 * d - 1 - d // 3 * 3) % 4
                v1(h, fr).wait_recv()
                z_synthesis(h, fr, finish)
                after(h, fr)

            each(1, 4, one)
            after(h, yy)
        for h in range(2):
            all_of(r3b, h, 31, g3s)
            all_of(vs2, h, 7, g2s)
            all_of(ys, h, 3, g1s)

    def channel_map(wide, source):
        rows = lax.broadcasted_iota(jnp.int32, (512, 512), 0) % 16
        columns = lax.broadcasted_iota(jnp.int32, (512, 512), 1) % 16
        full = lax.dot_general(
            wide.astype(BF16), a16[...], (((1,), (1,)), ((), ())), preferred_element_type=F32
        )
        kron[...] = jnp.where(rows == columns, full, 0.0).astype(BF16)

        def one(x):
            for at in (0, 16):
                block = source[:, :, :, x, at : at + 16, :].reshape(512, 256)
                out = mm(kron[...], block)
                lin[:, :, :, x, at : at + 16, :] = out.reshape(4, 2, 4, 16, 256)

        each(0, 6, one)

    def lanes(b):
        return pl.ds(pl.multiple_of(b * 128, 128), 128)

    def weights_in():
        loads[0].wait()

        def one(k):
            for part in range(2):
                for i in range(6):
                    w[part, k, 2 * i : 2 * i + 2, :] = w_in[part, k, i]
                w[part, k, 12:16, :] = jnp.zeros((4, 1024), F32)

        each(0, KZ, one)

    def weight_grad_out():
        def one(k):
            for part in range(2):
                for i in range(6):
                    wg_out[part, k, i] = wg[part, k, 2 * i : 2 * i + 2, :]

        each(0, KZ, one)
        wg_copy.start()

    def w_at(part, b):
        return w[part, :, :, lanes(b)].reshape(272, 128)

    def mix_one(h):
        def one(y):
            b = 2 * y + h
            modes = split_left(spread_rows(md[h, y]), e1[...])
            mexp[b] = modes
            real, imag = modes[:, :128], modes[:, 128:]
            w_real, w_imag = w_at(0, b), w_at(1, b)
            acc[:, :128] += w_real * real - w_imag * imag
            acc[:, 128:] += w_real * imag + w_imag * real

        each(0, 4, one)

    def spread_out(h, y):
        each(0, 8, lambda z: pl.when(z * 4 + y != me)(lambda: k3(h, z * 4 + y).start()))

    def keep_own(h):
        r3b[h, me] = mq[h, yy]

    def mix_two():
        high, low = halves(acc[...])
        for h in range(2):
            for pair in range(2):
                table = rr[h, pair]
                out = mm(high, table) + mm(low, table)
                for n in range(2):
                    y = 2 * pair + n
                    mq[h, y] = gather_rows(out[:, 128 * n : 128 * n + 128])
                    spread_out(h, y)
            keep_own(h)

    def split_left(values, table):
        high, low = halves(values)
        return mm(high, table) + mm(low, table)

    def back_one(h):
        def one(y):
            gexp[...] += split_left(spread_rows(md[h, y]), e2[2 * y + h])

        each(0, 4, one)

    def back_two():
        for h in range(2):

            def two(y, h=h):
                b = 2 * y + h
                g_real, g_imag = gexp[:, :128], gexp[:, 128:]
                w_real, w_imag = w_at(0, b), w_at(1, b)
                real = w_real * g_real + w_imag * g_imag
                imag = w_real * g_imag - w_imag * g_real
                mq[h, y] = gather_rows(split_left(jnp.concatenate([real, imag], 1), r2[...]))
                spread_out(h, y)

            each(0, 4, two)
            keep_own(h)

    def weight_grad():
        def one(b):
            g_real, g_imag = gexp[:, :128], gexp[:, 128:]
            real, imag = mexp[b, :, :128], mexp[b, :, 128:]
            wg[0, :, :, lanes(b)] = (real * g_real + imag * g_imag).reshape(KZ, 16, 128)
            wg[1, :, :, lanes(b)] = (real * g_imag - imag * g_real).reshape(KZ, 16, 128)

        each(0, 8, one)
        weight_grad_out()

    def finish_pre(fr, h, q, spectral):
        pre = spectral + lin[fr, h, q] + bias[fr * 8 + h * 4 + q]
        pg[fr, h, q] = (cot[fr, h, q].astype(F32) * gelu_slope(pre)).astype(BF16)

    def finish_grad(fr, h, q, spectral):
        ig[fr, h, q] = (spectral + lin[fr, h, q]).astype(BF16)

    wg_copy = pltpu.make_async_copy(wg_out, wg_hbm, out_sem.at[0])

    def ig_copy(h):
        return pltpu.make_async_copy(ig.at[:, h], ig_hbm.at[:, h], out_sem.at[1 + h])

    def second_start(h, to):
        @pl.when(to != yy)
        def _():
            z_analysis(pg, h, to, u.at[h, to])
            c1(h, to).start()

        @pl.when(to == yy)
        def _():
            z_analysis(pg, h, yy, r0.at[h, yy])

    def last_copies(h, to):
        pl.when(to == yy)(lambda: ig_copy(h).start())

    def first_meanwhile():
        channel_map(mm(a16[...], pw[...]), f)
        weights_in()
        acc[...] = jnp.zeros_like(acc)
        loads[1].wait()

    def second_meanwhile():
        wide = lax.dot_general(a16[...], pw[...], (((1,), (1,)), ((), ())), preferred_element_type=F32)
        channel_map(wide, pg)
        gexp[...] = jnp.zeros_like(gexp)

    def wait_loads():
        for load in loads[3:]:
            load.wait()

    for h in range(2):
        analysis_start(f, h)
    analysis(first_meanwhile, mix_one)
    loads[2].wait()
    mix_two()
    analysis_end()
    synthesis(wait_loads, finish_pre, second_start)
    analysis(second_meanwhile, back_one)
    back_two()
    synthesis(weight_grad, finish_grad, last_copies)
    analysis_end()
    wg_copy.wait()
    ig_copy(0).wait()
    ig_copy(1).wait()


def per_device(input_field, cotangent, spectral_weights, point_weight, point_bias):
    field_shape = (4, 2, 4, 6, 32, 256)
    w_shape = spectral_weights.shape
    tabs = {name: jnp.asarray(value) for name, value in TABLES.items()}
    vmem = pl.BlockSpec(memory_space=pltpu.VMEM)
    smem = pl.BlockSpec(memory_space=pltpu.SMEM)
    hbm = pl.BlockSpec(memory_space=pl.ANY)
    dma = pltpu.SemaphoreType.DMA
    scratch = [
        pltpu.VMEM((8, 256, 384), BF16),
        pltpu.VMEM((6, 256, 512), BF16),
        pltpu.VMEM((4, 256, 256), BF16),
        pltpu.VMEM((8, 128, 256), BF16),
        pltpu.VMEM((2, 2, 256, 256), BF16),
        pltpu.VMEM(field_shape, BF16),
        pltpu.VMEM(field_shape, BF16),
        pltpu.VMEM(w_shape, F32),
        pltpu.VMEM((2, KZ, 16, 1024), F32),
        pltpu.VMEM(field_shape, BF16),
        pltpu.VMEM(w_shape, F32),
        pltpu.VMEM((2, KZ, 16, 1024), F32),
        pltpu.VMEM(field_shape, BF16),
        pltpu.VMEM(field_shape, F32),
        pltpu.VMEM((512, 512), BF16),
        pltpu.VMEM((2, 4, 32, 896), F32),
        pltpu.VMEM((2, 4, 32, 896), F32),
        pltpu.VMEM((2, 8, 8, 896), F32),
        pltpu.VMEM((2, 8, 8, 896), F32),
        pltpu.VMEM((2, 32, 16, 128), F32),
        pltpu.VMEM((2, 32, 16, 128), F32),
        pltpu.VMEM((2, 4, 16, 128), F32),
        pltpu.VMEM((384, 256), BF16),
        pltpu.VMEM((8, 272, 256), F32),
        pltpu.VMEM((272, 256), F32),
        pltpu.VMEM((272, 256), F32),
        pltpu.VMEM((2, 4, 16, 128), F32),
        pltpu.VMEM((2, 32, 16, 128), F32),
        pltpu.VMEM((512, 256), BF16),
        pltpu.VMEM((2, 8, 8, 896), F32),
        pltpu.VMEM((2, 8, 8, 896), F32),
        pltpu.VMEM((2, 4, 32, 896), F32),
        pltpu.VMEM((2, 4, 32, 896), F32),
        pltpu.VMEM((192, 256), BF16),
        dma((4, 2)),
        dma((7,)),
        dma((2,)), dma((2,)), dma((2,)), dma((2,)), dma((2,)), dma((2,)),
        dma((2,)), dma((2,)), dma((2,)), dma((2,)), dma((2,)), dma((2, 4)),
        dma((3,)),
    ]
    ig, wg = pl.pallas_call(
        body,
        out_shape=(
            jax.ShapeDtypeStruct(field_shape, BF16),
            jax.ShapeDtypeStruct(w_shape, F32),
        ),
        in_specs=[vmem, smem] + [vmem] * len(IN_VMEM) + [hbm] * (len(IN_HBM) + 3),
        out_specs=(hbm, hbm),
        scratch_shapes=scratch,
        compiler_params=pltpu.CompilerParams(
            collective_id=0, has_side_effects=True, vmem_limit_bytes=58 * 1024 * 1024
        ),
        cost_estimate=pl.CostEstimate(flops=10**10, bytes_accessed=2 * 10**7, transcendentals=0),
    )(
        point_weight, point_bias,
        *[tabs[name] for name in IN_VMEM],
        *[tabs[name] for name in IN_HBM],
        input_field.reshape(field_shape), cotangent.reshape(field_shape), spectral_weights,
    )
    return (ig.reshape(input_field.shape), wg)


def solution(mesh):
    return jax.shard_map(
        per_device,
        mesh=mesh,
        in_specs=(
            P(None, None, "gx", "gy", None),
            P(None, None, "gx", "gy", None),
            P(None, None, "gy", "gx", None),
            P(),
            P(),
        ),
        out_specs=(P(None, None, "gx", "gy", None), P(None, None, "gy", "gx", None)),
        check_vma=False,
    )
```

```python
import math

import jax
import jax.numpy as jnp
import ml_dtypes
import numpy as np
from jax import lax
from jax.experimental import pallas as pl
from jax.experimental.pallas import tpu as pltpu
from jax.sharding import PartitionSpec as P

C = 32
NX = 192
NY = 256
NZ = 256
KX = 48
KY = 64
KZ = 17
SCALE = (NX * NY * NZ) ** (-0.5)
MESH = pl.DeviceIdType.MESH
F32 = jnp.float32
BF16 = jnp.bfloat16


def kept(count, number):
    half = number // 2
    return np.concatenate([np.arange(half), np.arange(half) + count - half])


def trig(points, freqs, count):
    angle = 2.0 * np.pi * ((points[:, None] * freqs[None, :]) % count) / count
    return np.cos(angle), np.sin(angle)


def hi_lo(table):
    table = np.asarray(table, np.float32)
    high = table.astype(ml_dtypes.bfloat16)
    low = (table - high.astype(np.float32)).astype(ml_dtypes.bfloat16)
    return high, low


def make_tables():
    z_cos, z_sin = trig(np.arange(NZ), np.arange(KZ), NZ)
    y_cos, y_sin = trig(np.arange(NY), kept(NY, KY), NY)
    x_cos, x_sin = trig(np.arange(NX), kept(NX, KX), NX)
    tabs = {}
    wz = np.zeros((4, NZ, 2, 2, 4, 16))
    zz = np.zeros((4, 2, 2, 4, 16, NZ))
    for c4 in range(4):
        wz[c4, :, 0, 0, c4, :] = z_cos[:, :16]
        wz[c4, :, 0, 1, c4, :] = -z_sin[:, :16]
        wz[c4, :, 1, 0, c4, :] = z_cos[:, 16:17]
        wz[c4, :, 1, 1, c4, :] = -z_sin[:, 16:17]
        zz[c4, 0, 0, c4] = z_cos[:, :16].T
        zz[c4, 0, 1, c4] = -z_sin[:, :16].T
        zz[c4, 1, 0, c4] = z_cos[:, 16:17].T
        zz[c4, 1, 1, c4] = -z_sin[:, 16:17].T
    tabs["wz"] = wz.reshape(4, NZ, 256).astype(np.float32).astype(ml_dtypes.bfloat16)
    tabs["zz"] = hi_lo(zz.reshape(4, 256, NZ))[0]
    s_at, zl_at, j_at = np.meshgrid(np.arange(8), np.arange(4), np.arange(2), indexing="ij")
    order = ((zl_at * 8 + s_at) * 2 + j_at).reshape(-1)
    yc = (y_cos * SCALE)[:, order].reshape(2, 128, 64)
    ys = (y_sin * SCALE)[:, order].reshape(2, 128, 64)
    inv = np.concatenate([yc, ys], 2)
    fwd = inv.transpose(0, 2, 1)
    tabs["t1"] = np.stack([np.concatenate([h, h, l], -1) for h, l in [hi_lo(fwd[0]), hi_lo(fwd[1])]])
    tabs["t1i"] = np.stack([np.concatenate([h, h, l], -1) for h, l in [hi_lo(inv[0]), hi_lo(inv[1])]])
    xt = np.stack([x_cos, x_sin]).reshape(2, 4, 8, 6, 2, 4, 6)
    t2 = np.zeros((4, 2, 4, 2, 4, 16, 6, 8, 8))
    for zl_to in range(4):
        for i in range(6):
            for j in range(2):
                block = xt[:, :, :, :, :, :, i]
                t2[:, :, zl_to, :, :, 2 * i + j, :, :, zl_to * 2 + j] = block.transpose(1, 4, 0, 5, 3, 2)
    fwd = t2.reshape(4, 8, 128, 384)
    tabs["t2"] = np.concatenate(hi_lo(fwd), 2)
    inv = t2.transpose(0, 6, 3, 7, 8, 1, 2, 4, 5).reshape(4, 6, 128, 512)
    tabs["t2i"] = np.concatenate(hi_lo(inv), 2)
    eye2, eye4 = np.eye(2), np.eye(4)
    ones16, ones32 = np.ones(16), np.ones(32)
    e1 = np.einsum("qr,cd,s,o->qcsrdo", eye2, eye4, ones16, ones32)
    tabs["e1"] = e1.reshape(128, 256)
    tabs["r2"] = e1.reshape(128, 256).T
    pick = np.eye(32).reshape(8, 4, 32)
    e2 = np.einsum("qr,bio,s,c->bqisrco", eye2, pick, ones16, np.ones(4)).reshape(8, 128, 256)
    tabs["e2"] = e2
    tabs["rr"] = e2.reshape(2, 2, 2, 128, 256).transpose(2, 0, 4, 1, 3).reshape(2, 2, 256, 256)
    slot = np.zeros((6, 16, 16))
    for x in range(6):
        slot[x, x, :] = 1.0
    spread = np.einsum("qr,cd,xst->xqcsrdt", eye2, eye4, slot).reshape(6, 128, 128)
    tabs["spread"] = spread.transpose(1, 0, 2).reshape(128, 768)
    tabs["gather"] = spread.transpose(0, 2, 1)
    tabs["a16"] = np.repeat(np.eye(32), 16, axis=0)
    for name in ("e1", "r2", "e2", "rr", "spread", "gather", "a16"):
        tabs[name] = tabs[name].astype(ml_dtypes.bfloat16)
    return tabs


TABLES = make_tables()
IN_VMEM = ("wz", "t1", "a16", "spread", "gather", "t1i", "e1", "r2")
IN_HBM = ("t2", "t2i", "zz", "e2", "rr")


def mm(left, right):
    return jnp.dot(left, right, preferred_element_type=F32)


def halves(values):
    high = values.astype(BF16)
    return high, (values - high.astype(F32)).astype(BF16)


def gelu_slope(values):
    size = jnp.abs(values)
    below = 1.0 + (0.3275911 / math.sqrt(2.0)) * size
    t = pl.reciprocal(below, approx=True)
    t = t * (2.0 - below * t)
    poly = t * (0.127414796 + t * (-0.142248368 + t * (0.7107068705 + t * (-0.7265760135 + t * 0.5307027145))))
    bell = jnp.exp2((-0.5 / math.log(2.0)) * (values * values))
    part = bell * ((1.0 / math.sqrt(2.0 * math.pi)) * size - poly)
    return jnp.where(values >= 0.0, 1.0 + part, -part)


def swap(values, first):
    lane = lax.broadcasted_iota(jnp.int32, (values.shape[0], 128), 1)
    sign = jnp.where(lane < 64, first, -first)
    parts = [
        pltpu.roll(values[:, at : at + 128], 64, 1) * sign for at in range(0, values.shape[1], 128)
    ]
    return parts[0] if len(parts) == 1 else jnp.concatenate(parts, 1)


def slot_of(shape):
    return lax.broadcasted_iota(jnp.int32, shape, len(shape) - 1) % 16


def spread_rows(block):
    slots = slot_of((16, 128))
    rows = lax.broadcasted_iota(jnp.int32, (16, 128), 0)
    parts = [jnp.where(slots == k, block, 0.0) for k in range(16)]
    parts.append(jnp.where(slots == rows, jnp.broadcast_to(block[12:13], (16, 128)), 0.0))
    return jnp.concatenate(parts, 0)


def gather_rows(values):
    slots = slot_of((16, 128))
    rows = lax.broadcasted_iota(jnp.int32, (16, 128), 0)
    total = jnp.where(slots == 0, values[0:16], 0.0)
    for k in range(1, 16):
        total = total + jnp.where(slots == k, values[16 * k : 16 * k + 16], 0.0)
    last = jnp.sum(jnp.where(slots == rows, values[256:272], 0.0), axis=0, keepdims=True)
    return jnp.where(rows == 12, jnp.broadcast_to(last, (16, 128)), total)


def split_mm(table, values):
    high, low = halves(values)
    return mm(table, high) + mm(table, low)


def body(
    pw, bias, wz, t1, a16, spread, gather, t1i, e1, r2,
    t2_hbm, t2i_hbm, zz_hbm, e2_hbm, rr_hbm, f_hbm, cot_hbm, w_hbm,
    ig_hbm, wg_hbm,
    t2, t2i, zz, e2, rr, f, cot, w_in, w, ig, wg_out, wg, pg, lin, kron,
    u, r0, vs, r1, rsb, r3a, md, xb, mexp, gexp, acc,
    mq, r3b, xb2, vs2, r1s, ys, r0s, zb,
    f_sem, local_sem, s1s, s1r, s2s, s2r, s3s, s3r, g3s, g3r, g2s, g2r, g1s, g1r, out_sem,
):
    gx = lax.axis_index("gx")
    gy = lax.axis_index("gy")
    zl, s = gx // 8, gx % 8
    zh, yy = gy // 4, gy % 4
    me = (zh * 4 + zl) * 4 + yy

    def y_id(to):
        return (gx, zh * 4 + to)

    def s_id(to):
        return (zl * 8 + to, gy)

    def m_id(to):
        return (((to // 4) % 4) * 8 + s, (to // 16) * 4 + to % 4)

    def each(low, high, fn):
        def step(d, carry):
            fn(d)
            return carry

        lax.fori_loop(low, high, step, 0)

    def f_load(to, h):
        return pltpu.make_async_copy(f_hbm.at[to, h], f.at[to, h], f_sem.at[to, h])

    for h in range(2):
        each(1, 5, lambda d, h=h: f_load((yy + d) % 4, h).start())

    barrier = pltpu.get_barrier_semaphore()

    def greet(device):
        pl.semaphore_signal(barrier, inc=1, device_id=device, device_id_type=MESH)

    each(1, 8, lambda d: greet(s_id((s + d) % 8)))
    each(1, 32, lambda d: greet(m_id((me + d) % 32)))

    loads = [
        pltpu.make_async_copy(src, dst, local_sem.at[n])
        for n, (src, dst) in enumerate(
            [
                (w_hbm, w_in),
                (t2_hbm.at[zl], t2),
                (rr_hbm, rr),
                (t2i_hbm.at[zl], t2i),
                (cot_hbm, cot),
                (zz_hbm, zz),
                (e2_hbm, e2),
            ]
        )
    ]
    for load in loads:
        load.start()
    pl.semaphore_wait(barrier, 38)

    def send(src, dst, send_sem, recv_sem, device):
        return pltpu.make_async_remote_copy(src, dst, send_sem, recv_sem, device_id=device, device_id_type=MESH)

    def c1(h, to):
        return send(u.at[h, to], r0.at[h, yy], s1s.at[h], s1r.at[h], y_id(to))

    def c2(h, to):
        return send(vs.at[h, to], r1.at[h, s], s2s.at[h], s2r.at[h], s_id(to))

    def c3(h, to):
        return send(rsb.at[h, to], r3a.at[h, me], s3s.at[h], s3r.at[h], m_id(to))

    def k3(h, to):
        return send(mq.at[h, to % 4], r3b.at[h, me], g3s.at[h], g3r.at[h], m_id(to))

    def k2(h, to):
        return send(vs2.at[h, to], r1s.at[h, s], g2s.at[h], g2r.at[h], s_id(to))

    def k1(h, to):
        return send(ys.at[h, to], r0s.at[h, yy], g1s.at[h], g1r.at[h, yy], y_id(to))

    def v1(h, fr):
        return send(ys.at[h, fr], r0s.at[h, fr], g1s.at[h], g1r.at[h, fr], y_id(fr))

    def all_of(buffer, h, count, sem):
        part = buffer.at[h, pl.ds(0, count)]
        pltpu.make_async_copy(part, part, sem.at[h]).wait()

    def z_analysis(source, h, to, dest):
        total = None
        for q in range(4):
            term = mm(source[to, h, q].reshape(192, 256), wz[q])
            total = term if total is None else total + term
        slots = slot_of((32, 128))
        last = None
        for x in range(6):
            rows = total[32 * x : 32 * x + 32]
            dest[:, 128 * x : 128 * x + 128] = rows[:, :128]
            part = jnp.where(slots == x, rows[:, 128:], 0.0)
            last = part if last is None else last + part
        dest[:, 768:896] = last

    def analysis_start(source, h):
        def one(d):
            to = (yy + d) % 4
            f_load(to, h).wait()
            z_analysis(source, h, to, u.at[h, to])
            c1(h, to).start()

        each(1, 4, one)
        f_load(yy, h).wait()
        z_analysis(source, h, yy, r0.at[h, yy])

    def y_analysis(h):
        table = t1.at[zh]
        for at, wide in ((0, 256), (256, 256), (512, 256), (768, 128)):
            high, low = halves(r0[h, :, :, at : at + wide].reshape(128, wide))
            both = jnp.concatenate([high, low], 0)
            out = mm(table[:, 0:256], both) + mm(table[:, 256:384], high)
            vs[h, :, :, at : at + wide] = (out[:64] + swap(out[64:], 1.0)).reshape(8, 8, wide)

    def x_analysis_load(h):
        last = r1[h, :, :, 768:896].reshape(64, 128).astype(BF16)
        last = mm(last, spread[...]).astype(BF16)
        for x in range(6):
            at = 128 * x
            xb[64 * x : 64 * x + 64, 0:128] = r1[h, :, :, at : at + 128].reshape(64, 128).astype(BF16)
            xb[64 * x : 64 * x + 64, 128:256] = last[:, at : at + 128]

    def x_analysis_store(out, h, z):
        out = out[:64] + swap(out[64:], 1.0)
        rows = lax.broadcasted_iota(jnp.int32, (64, 128), 0) % 16
        last = jnp.where(slot_of((64, 128)) == rows, out[:, 128:], 0.0)
        last = jnp.sum(last.reshape(4, 16, 128), axis=1, keepdims=True)
        last = jnp.broadcast_to(last, (4, 16, 128)).reshape(64, 128)
        rsb[h, pl.ds(4 * z, 4)] = jnp.where(rows == 12, last, out[:, :128]).reshape(4, 16, 128)

    def x_analysis(h):
        mine = me // 4
        for group in ((1, 2), (3, 4), (5, 6), (7, 8)):
            to = [(mine + d) % 8 for d in group]
            out = mm(jnp.concatenate([t2[z] for z in to], 0), xb[...])
            for n, d in enumerate(group):
                x_analysis_store(out[256 * n : 256 * n + 128] + out[256 * n + 128 : 256 * n + 256], h, to[n])
                each(0 if d < 8 else 1, 4, lambda y: c3(h, to[n] * 4 + (yy + y) % 4).start())
        r3a[h, me] = rsb[h, me]

    def analysis(first, second, received):
        first()
        for h in range(2):
            all_of(r0, h, 3, s1r)
            y_analysis(h)
            each(1, 8, lambda d: c2(h, (s + d) % 8).start())
            r1[h, s] = vs[h, s]
        for h in range(2):
            all_of(r1, h, 7, s2r)
            x_analysis_load(h)
            x_analysis(h)
        second()
        for h in range(2):
            all_of(r3a, h, 31, s3r)
            total = r3a[h, 0:4]
            for z in range(1, 8):
                total = total + r3a[h, 4 * z : 4 * z + 4]
            md[h] = total
            received(h)

    def analysis_end():
        for h in range(2):
            all_of(u, h, 3, s1s)
            all_of(vs, h, 7, s2s)
            all_of(rsb, h, 31, s3s)

    def x_synthesis_load(h):
        main = r3b[h]
        rows = lax.broadcasted_iota(jnp.int32, (512, 128), 0) % 16
        last = jnp.broadcast_to(main[:, 12:13], (32, 16, 128)).reshape(512, 128)
        xb2[:, 0:128] = main.reshape(512, 128).astype(BF16)
        xb2[:, 128:256] = jnp.where(slot_of((512, 128)) == rows, last, 0.0).astype(BF16)

    def x_synthesis(h):
        total = None
        for group in ((0, 1), (2, 3), (4, 5)):
            out = mm(jnp.concatenate([t2i[x] for x in group], 0), xb2[...])
            for n, x in enumerate(group):
                part = out[256 * n : 256 * n + 128] + out[256 * n + 128 : 256 * n + 256]
                part = part[:64] + swap(part[64:], -1.0)
                vs2[h, :, :, 128 * x : 128 * x + 128] = part[:, :128].reshape(8, 8, 128)
                high, low = halves(part[:, 128:])
                last = mm(high, gather[x]) + mm(low, gather[x])
                total = last if total is None else total + last
        vs2[h, :, :, 768:896] = total.reshape(8, 8, 128)

    def y_synthesis(h):
        table = t1i.at[zh]
        for at, wide in ((0, 256), (256, 256), (512, 256), (768, 128)):
            values = r1s[h, :, :, at : at + wide].reshape(64, wide)
            high, low = halves(jnp.concatenate([values, swap(values, -1.0)], 0))
            out = mm(table[:, 0:256], jnp.concatenate([high, low], 0)) + mm(table[:, 256:384], high)
            ys[h, :, :, at : at + wide] = out.reshape(4, 32, wide)

    def z_synthesis(h, fr, finish):
        slots = slot_of((32, 128))
        last = r0s[h, fr, :, 768:896]
        for x in range(6):
            zb[32 * x : 32 * x + 32, 0:128] = r0s[h, fr, :, 128 * x : 128 * x + 128].astype(BF16)
            zb[32 * x : 32 * x + 32, 128:256] = jnp.where(slots == x, last, 0.0).astype(BF16)

        def one(q):
            finish(fr, h, q, mm(zb[...], zz[q]).reshape(6, 32, 256))

        each(0, 4, one)

    def synthesis(meanwhile, finish, after):
        meanwhile()
        for h in range(2):
            all_of(r3b, h, 31, g3r)
            x_synthesis_load(h)
            x_synthesis(h)
            each(1, 8, lambda d: k2(h, (s + d) % 8).start())
            r1s[h, s] = vs2[h, s]
        for h in range(2):
            all_of(r1s, h, 7, g2r)
            y_synthesis(h)
            each(1, 4, lambda d: k1(h, (yy + d) % 4).start())
            r0s[h, yy] = ys[h, yy]
        for h in range(2):
            z_synthesis(h, yy, finish)
        for h in range(2):

            def one(d, h=h):
                fr = (yy + 2 * d - 1 - d // 3 * 3) % 4
                v1(h, fr).wait_recv()
                z_synthesis(h, fr, finish)
                after(h, fr)

            each(1, 4, one)
            after(h, yy)
        for h in range(2):
            all_of(r3b, h, 31, g3s)
            all_of(vs2, h, 7, g2s)
            all_of(ys, h, 3, g1s)

    def channel_map(wide, source):
        rows = lax.broadcasted_iota(jnp.int32, (512, 512), 0) % 16
        columns = lax.broadcasted_iota(jnp.int32, (512, 512), 1) % 16
        full = lax.dot_general(
            wide.astype(BF16), a16[...], (((1,), (1,)), ((), ())), preferred_element_type=F32
        )
        kron[...] = jnp.where(rows == columns, full, 0.0).astype(BF16)

        def one(x):
            for at in (0, 16):
                block = source[:, :, :, x, at : at + 16, :].reshape(512, 256)
                out = mm(kron[...], block)
                lin[:, :, :, x, at : at + 16, :] = out.reshape(4, 2, 4, 16, 256)

        each(0, 6, one)

    def lanes(b):
        return pl.ds(pl.multiple_of(b * 128, 128), 128)

    def weights_in():
        loads[0].wait()

        def one(k):
            for part in range(2):
                for i in range(6):
                    w[part, k, 2 * i : 2 * i + 2, :] = w_in[part, k, i]
                w[part, k, 12:16, :] = jnp.zeros((4, 1024), F32)

        each(0, KZ, one)

    def weight_grad_out():
        def one(k):
            for part in range(2):
                for i in range(6):
                    wg_out[part, k, i] = wg[part, k, 2 * i : 2 * i + 2, :]

        each(0, KZ, one)
        wg_copy.start()

    def w_at(part, b):
        return w[part, :, :, lanes(b)].reshape(272, 128)

    def mix_one(h):
        def one(y):
            b = 2 * y + h
            modes = split_left(spread_rows(md[h, y]), e1[...])
            mexp[b] = modes
            real, imag = modes[:, :128], modes[:, 128:]
            w_real, w_imag = w_at(0, b), w_at(1, b)
            acc[:, :128] += w_real * real - w_imag * imag
            acc[:, 128:] += w_real * imag + w_imag * real

        each(0, 4, one)

    def spread_out(h, y):
        each(0, 8, lambda z: pl.when(z * 4 + y != me)(lambda: k3(h, z * 4 + y).start()))

    def keep_own(h):
        r3b[h, me] = mq[h, yy]

    def mix_two():
        high, low = halves(acc[...])
        for h in range(2):
            for pair in range(2):
                table = rr[h, pair]
                out = mm(high, table) + mm(low, table)
                for n in range(2):
                    y = 2 * pair + n
                    mq[h, y] = gather_rows(out[:, 128 * n : 128 * n + 128])
                    spread_out(h, y)
            keep_own(h)

    def split_left(values, table):
        high, low = halves(values)
        return mm(high, table) + mm(low, table)

    def back_one(h):
        def one(y):
            gexp[...] += split_left(spread_rows(md[h, y]), e2[2 * y + h])

        each(0, 4, one)

    def back_two():
        for h in range(2):

            def two(y, h=h):
                b = 2 * y + h
                g_real, g_imag = gexp[:, :128], gexp[:, 128:]
                w_real, w_imag = w_at(0, b), w_at(1, b)
                real = w_real * g_real + w_imag * g_imag
                imag = w_real * g_imag - w_imag * g_real
                mq[h, y] = gather_rows(split_left(jnp.concatenate([real, imag], 1), r2[...]))
                spread_out(h, y)

            each(0, 4, two)
            keep_own(h)

    def weight_grad():
        def one(b):
            g_real, g_imag = gexp[:, :128], gexp[:, 128:]
            real, imag = mexp[b, :, :128], mexp[b, :, 128:]
            wg[0, :, :, lanes(b)] = (real * g_real + imag * g_imag).reshape(KZ, 16, 128)
            wg[1, :, :, lanes(b)] = (real * g_imag - imag * g_real).reshape(KZ, 16, 128)

        each(0, 8, one)
        weight_grad_out()

    def finish_pre(fr, h, q, spectral):
        pre = spectral + lin[fr, h, q] + bias[fr * 8 + h * 4 + q]
        pg[fr, h, q] = (cot[fr, h, q].astype(F32) * gelu_slope(pre)).astype(BF16)

    def finish_grad(fr, h, q, spectral):
        ig[fr, h, q] = (spectral + lin[fr, h, q]).astype(BF16)

    wg_copy = pltpu.make_async_copy(wg_out, wg_hbm, out_sem.at[0])

    def ig_copy(h):
        return pltpu.make_async_copy(ig.at[:, h], ig_hbm.at[:, h], out_sem.at[1 + h])

    def second_start(h, to):
        @pl.when(to != yy)
        def _():
            z_analysis(pg, h, to, u.at[h, to])
            c1(h, to).start()

        @pl.when(to == yy)
        def _():
            z_analysis(pg, h, yy, r0.at[h, yy])

    def last_copies(h, to):
        pl.when(to == yy)(lambda: ig_copy(h).start())

    def first_y_wait():
        channel_map(mm(a16[...], pw[...]), f)
        loads[1].wait()

    def first_z_wait():
        weights_in()
        acc[...] = jnp.zeros_like(acc)

    def second_z_wait():
        wide = lax.dot_general(a16[...], pw[...], (((1,), (1,)), ((), ())), preferred_element_type=F32)
        channel_map(wide, pg)
        gexp[...] = jnp.zeros_like(gexp)

    def wait_loads():
        for load in loads[3:]:
            load.wait()

    for h in range(2):
        analysis_start(f, h)
    analysis(first_y_wait, first_z_wait, mix_one)
    loads[2].wait()
    mix_two()
    analysis_end()
    synthesis(wait_loads, finish_pre, second_start)
    analysis(lambda: None, second_z_wait, back_one)
    back_two()
    synthesis(weight_grad, finish_grad, last_copies)
    analysis_end()
    wg_copy.wait()
    ig_copy(0).wait()
    ig_copy(1).wait()


def per_device(input_field, cotangent, spectral_weights, point_weight, point_bias):
    field_shape = (4, 2, 4, 6, 32, 256)
    w_shape = spectral_weights.shape
    tabs = {name: jnp.asarray(value) for name, value in TABLES.items()}
    vmem = pl.BlockSpec(memory_space=pltpu.VMEM)
    smem = pl.BlockSpec(memory_space=pltpu.SMEM)
    hbm = pl.BlockSpec(memory_space=pl.ANY)
    dma = pltpu.SemaphoreType.DMA
    scratch = [
        pltpu.VMEM((8, 256, 384), BF16),
        pltpu.VMEM((6, 256, 512), BF16),
        pltpu.VMEM((4, 256, 256), BF16),
        pltpu.VMEM((8, 128, 256), BF16),
        pltpu.VMEM((2, 2, 256, 256), BF16),
        pltpu.VMEM(field_shape, BF16),
        pltpu.VMEM(field_shape, BF16),
        pltpu.VMEM(w_shape, F32),
        pltpu.VMEM((2, KZ, 16, 1024), F32),
        pltpu.VMEM(field_shape, BF16),
        pltpu.VMEM(w_shape, F32),
        pltpu.VMEM((2, KZ, 16, 1024), F32),
        pltpu.VMEM(field_shape, BF16),
        pltpu.VMEM(field_shape, F32),
        pltpu.VMEM((512, 512), BF16),
        pltpu.VMEM((2, 4, 32, 896), F32),
        pltpu.VMEM((2, 4, 32, 896), F32),
        pltpu.VMEM((2, 8, 8, 896), F32),
        pltpu.VMEM((2, 8, 8, 896), F32),
        pltpu.VMEM((2, 32, 16, 128), F32),
        pltpu.VMEM((2, 32, 16, 128), F32),
        pltpu.VMEM((2, 4, 16, 128), F32),
        pltpu.VMEM((384, 256), BF16),
        pltpu.VMEM((8, 272, 256), F32),
        pltpu.VMEM((272, 256), F32),
        pltpu.VMEM((272, 256), F32),
        pltpu.VMEM((2, 4, 16, 128), F32),
        pltpu.VMEM((2, 32, 16, 128), F32),
        pltpu.VMEM((512, 256), BF16),
        pltpu.VMEM((2, 8, 8, 896), F32),
        pltpu.VMEM((2, 8, 8, 896), F32),
        pltpu.VMEM((2, 4, 32, 896), F32),
        pltpu.VMEM((2, 4, 32, 896), F32),
        pltpu.VMEM((192, 256), BF16),
        dma((4, 2)),
        dma((7,)),
        dma((2,)), dma((2,)), dma((2,)), dma((2,)), dma((2,)), dma((2,)),
        dma((2,)), dma((2,)), dma((2,)), dma((2,)), dma((2,)), dma((2, 4)),
        dma((3,)),
    ]
    ig, wg = pl.pallas_call(
        body,
        out_shape=(
            jax.ShapeDtypeStruct(field_shape, BF16),
            jax.ShapeDtypeStruct(w_shape, F32),
        ),
        in_specs=[vmem, smem] + [vmem] * len(IN_VMEM) + [hbm] * (len(IN_HBM) + 3),
        out_specs=(hbm, hbm),
        scratch_shapes=scratch,
        compiler_params=pltpu.CompilerParams(
            collective_id=0, has_side_effects=True, vmem_limit_bytes=58 * 1024 * 1024
        ),
        cost_estimate=pl.CostEstimate(flops=10**10, bytes_accessed=2 * 10**7, transcendentals=0),
    )(
        point_weight, point_bias,
        *[tabs[name] for name in IN_VMEM],
        *[tabs[name] for name in IN_HBM],
        input_field.reshape(field_shape), cotangent.reshape(field_shape), spectral_weights,
    )
    return (ig.reshape(input_field.shape), wg)


def solution(mesh):
    return jax.shard_map(
        per_device,
        mesh=mesh,
        in_specs=(
            P(None, None, "gx", "gy", None),
            P(None, None, "gx", "gy", None),
            P(None, None, "gy", "gx", None),
            P(),
            P(),
        ),
        out_specs=(P(None, None, "gx", "gy", None), P(None, None, "gy", "gx", None)),
        check_vma=False,
    )
```

```python
import math

import jax
import jax.numpy as jnp
import ml_dtypes
import numpy as np
from jax import lax
from jax.experimental import pallas as pl
from jax.experimental.pallas import tpu as pltpu
from jax.sharding import PartitionSpec as P

C = 32
NX = 192
NY = 256
NZ = 256
KX = 48
KY = 64
KZ = 17
SCALE = (NX * NY * NZ) ** (-0.5)
MESH = pl.DeviceIdType.MESH
F32 = jnp.float32
BF16 = jnp.bfloat16


def kept(count, number):
    half = number // 2
    return np.concatenate([np.arange(half), np.arange(half) + count - half])


def trig(points, freqs, count):
    angle = 2.0 * np.pi * ((points[:, None] * freqs[None, :]) % count) / count
    return np.cos(angle), np.sin(angle)


def hi_lo(table):
    table = np.asarray(table, np.float32)
    high = table.astype(ml_dtypes.bfloat16)
    low = (table - high.astype(np.float32)).astype(ml_dtypes.bfloat16)
    return high, low


def make_tables():
    z_cos, z_sin = trig(np.arange(NZ), np.arange(KZ), NZ)
    y_cos, y_sin = trig(np.arange(NY), kept(NY, KY), NY)
    x_cos, x_sin = trig(np.arange(NX), kept(NX, KX), NX)
    tabs = {}
    wz = np.zeros((4, NZ, 2, 2, 4, 16))
    zz = np.zeros((4, 2, 2, 4, 16, NZ))
    for c4 in range(4):
        wz[c4, :, 0, 0, c4, :] = z_cos[:, :16]
        wz[c4, :, 0, 1, c4, :] = -z_sin[:, :16]
        wz[c4, :, 1, 0, c4, :] = z_cos[:, 16:17]
        wz[c4, :, 1, 1, c4, :] = -z_sin[:, 16:17]
        zz[c4, 0, 0, c4] = z_cos[:, :16].T
        zz[c4, 0, 1, c4] = -z_sin[:, :16].T
        zz[c4, 1, 0, c4] = z_cos[:, 16:17].T
        zz[c4, 1, 1, c4] = -z_sin[:, 16:17].T
    tabs["wz"] = wz.reshape(4, NZ, 256).astype(np.float32).astype(ml_dtypes.bfloat16)
    tabs["zz"] = hi_lo(zz.reshape(4, 256, NZ))[0]
    s_at, zl_at, j_at = np.meshgrid(np.arange(8), np.arange(4), np.arange(2), indexing="ij")
    order = ((zl_at * 8 + s_at) * 2 + j_at).reshape(-1)
    yc = (y_cos * SCALE)[:, order].reshape(2, 128, 64)
    ys = (y_sin * SCALE)[:, order].reshape(2, 128, 64)
    inv = np.concatenate([yc, ys], 2)
    fwd = inv.transpose(0, 2, 1)
    tabs["t1"] = np.stack([np.concatenate([h, h, l], -1) for h, l in [hi_lo(fwd[0]), hi_lo(fwd[1])]])
    tabs["t1i"] = np.stack([np.concatenate([h, h, l], -1) for h, l in [hi_lo(inv[0]), hi_lo(inv[1])]])
    xt = np.stack([x_cos, x_sin]).reshape(2, 4, 8, 6, 2, 4, 6)
    t2 = np.zeros((4, 2, 4, 2, 4, 16, 6, 8, 8))
    for zl_to in range(4):
        for i in range(6):
            for j in range(2):
                block = xt[:, :, :, :, :, :, i]
                t2[:, :, zl_to, :, :, 2 * i + j, :, :, zl_to * 2 + j] = block.transpose(1, 4, 0, 5, 3, 2)
    fwd = t2.reshape(4, 8, 128, 384)
    tabs["t2"] = np.concatenate(hi_lo(fwd), 2)
    inv = t2.transpose(0, 6, 3, 7, 8, 1, 2, 4, 5).reshape(4, 6, 128, 512)
    tabs["t2i"] = np.concatenate(hi_lo(inv), 2)
    eye2, eye4 = np.eye(2), np.eye(4)
    ones16, ones32 = np.ones(16), np.ones(32)
    e1 = np.einsum("qr,cd,s,o->qcsrdo", eye2, eye4, ones16, ones32)
    tabs["e1"] = e1.reshape(128, 256)
    tabs["r2"] = e1.reshape(128, 256).T
    pick = np.eye(32).reshape(8, 4, 32)
    e2 = np.einsum("qr,bio,s,c->bqisrco", eye2, pick, ones16, np.ones(4)).reshape(8, 128, 256)
    tabs["e2"] = e2
    tabs["rr"] = e2.reshape(2, 2, 2, 128, 256).transpose(2, 0, 4, 1, 3).reshape(2, 2, 256, 256)
    slot = np.zeros((6, 16, 16))
    for x in range(6):
        slot[x, x, :] = 1.0
    spread = np.einsum("qr,cd,xst->xqcsrdt", eye2, eye4, slot).reshape(6, 128, 128)
    tabs["spread"] = spread.transpose(1, 0, 2).reshape(128, 768)
    tabs["gather"] = spread.transpose(0, 2, 1)
    tabs["a16"] = np.repeat(np.eye(32), 16, axis=0)
    for name in ("e1", "r2", "e2", "rr", "spread", "gather", "a16"):
        tabs[name] = tabs[name].astype(ml_dtypes.bfloat16)
    return tabs


TABLES = make_tables()
IN_VMEM = ("wz", "t1", "a16", "spread", "gather", "t1i", "e1", "r2")
IN_HBM = ("t2", "t2i", "zz", "e2", "rr")


def mm(left, right):
    return jnp.dot(left, right, preferred_element_type=F32)


def halves(values):
    high = values.astype(BF16)
    return high, (values - high.astype(F32)).astype(BF16)


def gelu_slope(values):
    size = jnp.abs(values)
    below = 1.0 + (0.3275911 / math.sqrt(2.0)) * size
    t = pl.reciprocal(below, approx=True)
    t = t * (2.0 - below * t)
    poly = t * (0.127414796 + t * (-0.142248368 + t * (0.7107068705 + t * (-0.7265760135 + t * 0.5307027145))))
    bell = jnp.exp2((-0.5 / math.log(2.0)) * (values * values))
    part = bell * (poly - (1.0 / math.sqrt(2.0 * math.pi)) * size)
    return jnp.where(values >= 0.0, 1.0 - part, part)


def swap(values, first):
    lane = lax.broadcasted_iota(jnp.int32, (values.shape[0], 128), 1)
    sign = jnp.where(lane < 64, first, -first)
    parts = [
        pltpu.roll(values[:, at : at + 128], 64, 1) * sign for at in range(0, values.shape[1], 128)
    ]
    return parts[0] if len(parts) == 1 else jnp.concatenate(parts, 1)


def slot_of(shape):
    return lax.broadcasted_iota(jnp.int32, shape, len(shape) - 1) % 16


def spread_rows(block):
    slots = slot_of((16, 128))
    rows = lax.broadcasted_iota(jnp.int32, (16, 128), 0)
    parts = [jnp.where(slots == k, block, 0.0) for k in range(16)]
    parts.append(jnp.where(slots == rows, jnp.broadcast_to(block[12:13], (16, 128)), 0.0))
    return jnp.concatenate(parts, 0)


def gather_rows(values):
    slots = slot_of((16, 128))
    rows = lax.broadcasted_iota(jnp.int32, (16, 128), 0)
    total = jnp.where(slots == 0, values[0:16], 0.0)
    for k in range(1, 16):
        total = total + jnp.where(slots == k, values[16 * k : 16 * k + 16], 0.0)
    last = jnp.sum(jnp.where(slots == rows, values[256:272], 0.0), axis=0, keepdims=True)
    return jnp.where(rows == 12, jnp.broadcast_to(last, (16, 128)), total)


def split_left(values, table):
    high, low = halves(values)
    out = mm(jnp.concatenate([high, low], 0), table)
    return out[: values.shape[0]] + out[values.shape[0] :]


GROUPS = ((0, 512), (512, 384))
CHUNKS = (((0, 256), (256, 256)), ((512, 256), (768, 128)))
ROWS = 13


def body(
    pw, bias, wz, t1, a16, spread, gather, t1i, e1, r2,
    t2_hbm, t2i_hbm, zz_hbm, e2_hbm, rr_hbm, f_hbm, cot_hbm, w_hbm,
    ig_hbm, wg_hbm,
    t2, t2i, zz, e2, rr, f, cot, w_in, w, ig, wg_out, wg, pg, lin, kron,
    u, r0, vs, r1, rsb, r3a, md, xb, mexp, gexp, acc,
    mq, r3b, xb2, vs2, r1s, ys, r0s, zb,
    f_sem, local_sem, s1s, s1r, s2s, s2r, s3s, s3r, g3s, g3r, g2s, g2r, g1s, g1r, out_sem,
):
    gx = lax.axis_index("gx")
    gy = lax.axis_index("gy")
    zl, s = gx // 8, gx % 8
    zh, yy = gy // 4, gy % 4
    me = (zh * 4 + zl) * 4 + yy

    def y_id(to):
        return (gx, zh * 4 + to)

    def s_id(to):
        return (zl * 8 + to, gy)

    def m_id(to):
        return (((to // 4) % 4) * 8 + s, (to // 16) * 4 + to % 4)

    def each(low, high, fn):
        def step(d, carry):
            fn(d)
            return carry

        lax.fori_loop(low, high, step, 0)

    def f_load(to, h):
        return pltpu.make_async_copy(f_hbm.at[to, h], f.at[to, h], f_sem.at[to, h])

    for h in range(2):
        each(1, 5, lambda d, h=h: f_load((yy + d) % 4, h).start())

    barrier = pltpu.get_barrier_semaphore()

    r3a[:, :, 8:16, :] = jnp.zeros((2, 32, 8, 128), F32)
    r3b[:, :, 8:16, :] = jnp.zeros((2, 32, 8, 128), F32)

    def greet(device):
        pl.semaphore_signal(barrier, inc=1, device_id=device, device_id_type=MESH)

    each(1, 8, lambda d: greet(s_id((s + d) % 8)))
    each(1, 32, lambda d: greet(m_id((me + d) % 32)))

    loads = [
        pltpu.make_async_copy(src, dst, local_sem.at[n])
        for n, (src, dst) in enumerate(
            [
                (w_hbm, w_in),
                (t2_hbm.at[zl], t2),
                (rr_hbm, rr),
                (t2i_hbm.at[zl], t2i),
                (cot_hbm, cot),
                (zz_hbm, zz),
                (e2_hbm, e2),
            ]
        )
    ]
    for load in loads:
        load.start()
    def send(src, dst, send_sem, recv_sem, device):
        return pltpu.make_async_remote_copy(src, dst, send_sem, recv_sem, device_id=device, device_id_type=MESH)

    def c1(h, to, g):
        cells = pl.ds(*GROUPS[g])
        return send(u.at[h, to, :, cells], r0.at[h, yy, :, cells], s1s.at[h], s1r.at[h, g], y_id(to))

    def c2(h, to, g):
        cells = pl.ds(*GROUPS[g])
        return send(vs.at[h, to, :, cells], r1.at[h, s, :, cells], s2s.at[h], s2r.at[h], s_id(to))

    def c3(h, to):
        rows = pl.ds(0, ROWS)
        return send(rsb.at[h, to, rows], r3a.at[h, me, rows], s3s.at[h], s3r.at[h], m_id(to))

    def k3(h, to):
        rows = pl.ds(0, ROWS)
        return send(mq.at[h, to % 4, rows], r3b.at[h, me, rows], g3s.at[h], g3r.at[h], m_id(to))

    def k2(h, to, g):
        cells = pl.ds(*GROUPS[g])
        return send(vs2.at[h, to, :, cells], r1s.at[h, s, :, cells], g2s.at[h], g2r.at[h, g], s_id(to))

    def k1(h, to, g):
        cells = pl.ds(*GROUPS[g])
        return send(ys.at[h, to, :, cells], r0s.at[h, yy, :, cells], g1s.at[h], g1r.at[h, yy], y_id(to))

    def whole(part, sem):
        pltpu.make_async_copy(part, part, sem).wait()

    def all_of(buffer, h, count, sem):
        whole(buffer.at[h, pl.ds(0, count)], sem.at[h])

    def all_of_group(buffer, h, count, sem, g):
        whole(buffer.at[h, pl.ds(0, count), :, pl.ds(*GROUPS[g])], sem.at[h, g])

    def all_modes(buffer, h, sem):
        whole(buffer.at[h, pl.ds(0, 31), pl.ds(0, ROWS)], sem.at[h])

    def z_analysis(source, h, to, dest):
        total = None
        for q in range(4):
            term = mm(source[to, h, q].reshape(192, 256), wz[q])
            total = term if total is None else total + term
        slots = slot_of((32, 128))
        last = None
        for x in range(6):
            rows = total[32 * x : 32 * x + 32]
            dest[:, 128 * x : 128 * x + 128] = rows[:, :128]
            part = jnp.where(slots == x, rows[:, 128:], 0.0)
            last = part if last is None else last + part
        dest[:, 768:896] = last

    def analysis_start(source, h, greeted):
        def one(d):
            to = (yy + d) % 4
            f_load(to, h).wait()
            z_analysis(source, h, to, u.at[h, to])
            if greeted:
                c1(h, to, 0).start()

        each(1, 4, one)
        if not greeted:
            pl.semaphore_wait(barrier, 38)
            each(1, 4, lambda d: c1(h, (yy + d) % 4, 0).start())
        each(1, 4, lambda d: c1(h, (yy + d) % 4, 1).start())
        f_load(yy, h).wait()
        z_analysis(source, h, yy, r0.at[h, yy])

    def y_analysis(h, g):
        table = t1.at[zh]
        for at, wide in CHUNKS[g]:
            high, low = halves(r0[h, :, :, at : at + wide].reshape(128, wide))
            both = jnp.concatenate([high, low], 0)
            out = mm(table[:, 0:256], both) + mm(table[:, 256:384], high)
            vs[h, :, :, at : at + wide] = (out[:64] + swap(out[64:], 1.0)).reshape(8, 8, wide)

    def x_analysis_load(h):
        last = r1[h, :, :, 768:896].reshape(64, 128).astype(BF16)
        last = mm(last, spread[...]).astype(BF16)
        for x in range(6):
            at = 128 * x
            xb[64 * x : 64 * x + 64, 0:128] = r1[h, :, :, at : at + 128].reshape(64, 128).astype(BF16)
            xb[64 * x : 64 * x + 64, 128:256] = last[:, at : at + 128]

    def x_analysis_store(out, h, z):
        out = out[:64] + swap(out[64:], 1.0)
        rows = lax.broadcasted_iota(jnp.int32, (64, 128), 0) % 16
        last = jnp.where(slot_of((64, 128)) == rows, out[:, 128:], 0.0)
        last = jnp.sum(last.reshape(4, 16, 128), axis=1, keepdims=True)
        last = jnp.broadcast_to(last, (4, 16, 128)).reshape(64, 128)
        rsb[h, pl.ds(4 * z, 4)] = jnp.where(rows == 12, last, out[:, :128]).reshape(4, 16, 128)

    def x_analysis(h):
        mine = me // 4
        for group in ((1, 2), (3, 4), (5, 6), (7, 8)):
            to = [(mine + d) % 8 for d in group]
            out = mm(jnp.concatenate([t2[z] for z in to], 0), xb[...])
            for n, d in enumerate(group):
                x_analysis_store(out[256 * n : 256 * n + 128] + out[256 * n + 128 : 256 * n + 256], h, to[n])
                each(0 if d < 8 else 1, 4, lambda y: c3(h, to[n] * 4 + (yy + y) % 4).start())
        r3a[h, me] = rsb[h, me]

    def analysis(first, second, received):
        first()
        for h in range(2):
            for g in range(2):
                all_of_group(r0, h, 3, s1r, g)
                y_analysis(h, g)
                each(1, 8, lambda d: c2(h, (s + d) % 8, g).start())
            r1[h, s] = vs[h, s]
        for h in range(2):
            all_of(r1, h, 7, s2r)
            x_analysis_load(h)
            x_analysis(h)
        second()
        for h in range(2):
            all_modes(r3a, h, s3r)
            total = r3a[h, 0:4]
            for z in range(1, 8):
                total = total + r3a[h, 4 * z : 4 * z + 4]
            md[h] = total
            received(h)

    def analysis_end():
        for h in range(2):
            all_of(u, h, 3, s1s)
            all_of(vs, h, 7, s2s)
            all_modes(rsb, h, s3s)

    def x_synthesis_load(h):
        main = r3b[h]
        rows = lax.broadcasted_iota(jnp.int32, (512, 128), 0) % 16
        last = jnp.broadcast_to(main[:, 12:13], (32, 16, 128)).reshape(512, 128)
        xb2[:, 0:128] = main.reshape(512, 128).astype(BF16)
        xb2[:, 128:256] = jnp.where(slot_of((512, 128)) == rows, last, 0.0).astype(BF16)

    def x_synthesis(h):
        total = None
        for group in ((0, 1), (2, 3), (4, 5)):
            out = mm(jnp.concatenate([t2i[x] for x in group], 0), xb2[...])
            for n, x in enumerate(group):
                part = out[256 * n : 256 * n + 128] + out[256 * n + 128 : 256 * n + 256]
                part = part[:64] + swap(part[64:], -1.0)
                vs2[h, :, :, 128 * x : 128 * x + 128] = part[:, :128].reshape(8, 8, 128)
                high, low = halves(part[:, 128:])
                last = mm(high, gather[x]) + mm(low, gather[x])
                total = last if total is None else total + last
            if group == (2, 3):
                each(1, 8, lambda d: k2(h, (s + d) % 8, 0).start())
        vs2[h, :, :, 768:896] = total.reshape(8, 8, 128)
        each(1, 8, lambda d: k2(h, (s + d) % 8, 1).start())

    def y_synthesis(h, g):
        table = t1i.at[zh]
        for at, wide in CHUNKS[g]:
            values = r1s[h, :, :, at : at + wide].reshape(64, wide)
            high, low = halves(jnp.concatenate([values, swap(values, -1.0)], 0))
            out = mm(table[:, 0:256], jnp.concatenate([high, low], 0)) + mm(table[:, 256:384], high)
            ys[h, :, :, at : at + wide] = out.reshape(4, 32, wide)

    def z_synthesis(h, fr, finish):
        slots = slot_of((32, 128))
        last = r0s[h, fr, :, 768:896]
        for x in range(6):
            zb[32 * x : 32 * x + 32, 0:128] = r0s[h, fr, :, 128 * x : 128 * x + 128].astype(BF16)
            zb[32 * x : 32 * x + 32, 128:256] = jnp.where(slots == x, last, 0.0).astype(BF16)

        def one(q):
            finish(fr, h, q, mm(zb[...], zz[q]).reshape(6, 32, 256))

        each(0, 4, one)

    def synthesis(meanwhile, finish, own, after):
        meanwhile()
        for h in range(2):
            all_modes(r3b, h, g3r)
            x_synthesis_load(h)
            x_synthesis(h)
            r1s[h, s] = vs2[h, s]
        for h in range(2):
            for g in range(2):
                all_of_group(r1s, h, 7, g2r, g)
                y_synthesis(h, g)
                each(1, 4, lambda d: k1(h, (yy + d) % 4, g).start())
            r0s[h, yy] = ys[h, yy]
        for h in range(2):
            z_synthesis(h, yy, finish)
            own(h)
        for h in range(2):

            def one(d, h=h):
                fr = (yy + 2 * d - 1 - d // 3 * 3) % 4
                whole(r0s.at[h, fr], g1r.at[h, fr])
                z_synthesis(h, fr, finish)
                after(h, fr)

            each(1, 4, one)
        for h in range(2):
            all_modes(r3b, h, g3s)
            all_of(vs2, h, 7, g2s)
            all_of(ys, h, 3, g1s)

    def channel_map(wide, source):
        rows = lax.broadcasted_iota(jnp.int32, (512, 512), 0) % 16
        columns = lax.broadcasted_iota(jnp.int32, (512, 512), 1) % 16
        full = lax.dot_general(
            wide.astype(BF16), a16[...], (((1,), (1,)), ((), ())), preferred_element_type=F32
        )
        kron[...] = jnp.where(rows == columns, full, 0.0).astype(BF16)

        def one(x):
            for at in (0, 16):
                block = source[:, :, :, x, at : at + 16, :].reshape(512, 256)
                out = mm(kron[...], block)
                lin[:, :, :, x, at : at + 16, :] = out.reshape(4, 2, 4, 16, 256)

        each(0, 6, one)

    def lanes(b):
        return pl.ds(pl.multiple_of(b * 128, 128), 128)

    def weights_in():
        loads[0].wait()

        def one(k):
            for part in range(2):
                for i in range(6):
                    w[part, k, 2 * i : 2 * i + 2, :] = w_in[part, k, i]
                w[part, k, 12:16, :] = jnp.zeros((4, 1024), F32)

        each(0, KZ, one)

    def weight_grad_out():
        def one(k):
            for part in range(2):
                for i in range(6):
                    wg_out[part, k, i] = wg[part, k, 2 * i : 2 * i + 2, :]

        each(0, KZ, one)
        wg_copy.start()

    def w_at(part, b):
        return w[part, :, :, lanes(b)].reshape(272, 128)

    def mix_one(h):
        def one(y):
            b = 2 * y + h
            modes = split_left(spread_rows(md[h, y]), e1[...])
            mexp[b] = modes
            real, imag = modes[:, :128], modes[:, 128:]
            w_real, w_imag = w_at(0, b), w_at(1, b)
            acc[:, :128] += w_real * real - w_imag * imag
            acc[:, 128:] += w_real * imag + w_imag * real

        each(0, 4, one)

    def spread_out(h, y):
        each(0, 8, lambda z: pl.when(z * 4 + y != me)(lambda: k3(h, z * 4 + y).start()))

    def keep_own(h):
        r3b[h, me] = mq[h, yy]

    def mix_two():
        for h in range(2):
            for pair in range(2):
                out = split_left(acc[...], rr[h, pair])
                for n in range(2):
                    y = 2 * pair + n
                    mq[h, y] = gather_rows(out[:, 128 * n : 128 * n + 128])
                    spread_out(h, y)
            keep_own(h)

    def back_one(h):
        def one(y):
            gexp[...] += split_left(spread_rows(md[h, y]), e2[2 * y + h])

        each(0, 4, one)

    def back_two():
        for h in range(2):

            def two(y, h=h):
                b = 2 * y + h
                g_real, g_imag = gexp[:, :128], gexp[:, 128:]
                w_real, w_imag = w_at(0, b), w_at(1, b)
                real = w_real * g_real + w_imag * g_imag
                imag = w_real * g_imag - w_imag * g_real
                mq[h, y] = gather_rows(split_left(jnp.concatenate([real, imag], 1), r2[...]))
                spread_out(h, y)

            each(0, 4, two)
            keep_own(h)

    def weight_grad():
        def one(b):
            g_real, g_imag = gexp[:, :128], gexp[:, 128:]
            real, imag = mexp[b, :, :128], mexp[b, :, 128:]
            wg[0, :, :, lanes(b)] = (real * g_real + imag * g_imag).reshape(KZ, 16, 128)
            wg[1, :, :, lanes(b)] = (real * g_imag - imag * g_real).reshape(KZ, 16, 128)

        each(0, 8, one)
        weight_grad_out()

    def finish_pre(fr, h, q, spectral):
        pre = spectral + lin[fr, h, q] + bias[fr * 8 + h * 4 + q]
        pg[fr, h, q] = (cot[fr, h, q].astype(F32) * gelu_slope(pre)).astype(BF16)

    def finish_grad(fr, h, q, spectral):
        ig[fr, h, q] = spectral + lin[fr, h, q]

    wg_copy = pltpu.make_async_copy(wg_out, wg_hbm, out_sem.at[0])

    def ig_copy(h, fr):
        return pltpu.make_async_copy(ig.at[fr, h], ig_hbm.at[fr, h], out_sem.at[1])

    def second_own(h):
        z_analysis(pg, h, yy, r0.at[h, yy])

    def second_start(h, to):
        z_analysis(pg, h, to, u.at[h, to])
        for g in range(2):
            c1(h, to, g).start()

    def first_y_wait():
        channel_map(mm(a16[...], pw[...]), f)
        loads[1].wait()

    def first_z_wait():
        weights_in()
        acc[...] = jnp.zeros_like(acc)

    def second_z_wait():
        wide = lax.dot_general(a16[...], pw[...], (((1,), (1,)), ((), ())), preferred_element_type=F32)
        channel_map(wide, pg)
        gexp[...] = jnp.zeros_like(gexp)

    def wait_loads():
        for load in loads[3:]:
            load.wait()

    for h in range(2):
        analysis_start(f, h, h == 1)
    analysis(first_y_wait, first_z_wait, mix_one)
    loads[2].wait()
    mix_two()
    analysis_end()
    synthesis(wait_loads, finish_pre, second_own, second_start)
    analysis(lambda: None, second_z_wait, back_one)
    back_two()
    synthesis(weight_grad, finish_grad, lambda h: ig_copy(h, yy).start(), lambda h, fr: ig_copy(h, fr).start())
    analysis_end()
    wg_copy.wait()
    whole(ig, out_sem.at[1])


def per_device(input_field, cotangent, spectral_weights, point_weight, point_bias):
    field_shape = (4, 2, 4, 6, 32, 256)
    w_shape = spectral_weights.shape
    tabs = {name: jnp.asarray(value) for name, value in TABLES.items()}
    vmem = pl.BlockSpec(memory_space=pltpu.VMEM)
    smem = pl.BlockSpec(memory_space=pltpu.SMEM)
    hbm = pl.BlockSpec(memory_space=pl.ANY)
    dma = pltpu.SemaphoreType.DMA
    scratch = [
        pltpu.VMEM((8, 256, 384), BF16),
        pltpu.VMEM((6, 256, 512), BF16),
        pltpu.VMEM((4, 256, 256), BF16),
        pltpu.VMEM((8, 128, 256), BF16),
        pltpu.VMEM((2, 2, 256, 256), BF16),
        pltpu.VMEM(field_shape, BF16),
        pltpu.VMEM(field_shape, BF16),
        pltpu.VMEM(w_shape, F32),
        pltpu.VMEM((2, KZ, 16, 1024), F32),
        pltpu.VMEM(field_shape, F32),
        pltpu.VMEM(w_shape, F32),
        pltpu.VMEM((2, KZ, 16, 1024), F32),
        pltpu.VMEM(field_shape, BF16),
        pltpu.VMEM(field_shape, F32),
        pltpu.VMEM((512, 512), BF16),
        pltpu.VMEM((2, 4, 32, 896), F32),
        pltpu.VMEM((2, 4, 32, 896), F32),
        pltpu.VMEM((2, 8, 8, 896), F32),
        pltpu.VMEM((2, 8, 8, 896), F32),
        pltpu.VMEM((2, 32, 16, 128), F32),
        pltpu.VMEM((2, 32, 16, 128), F32),
        pltpu.VMEM((2, 4, 16, 128), F32),
        pltpu.VMEM((384, 256), BF16),
        pltpu.VMEM((8, 272, 256), F32),
        pltpu.VMEM((272, 256), F32),
        pltpu.VMEM((272, 256), F32),
        pltpu.VMEM((2, 4, 16, 128), F32),
        pltpu.VMEM((2, 32, 16, 128), F32),
        pltpu.VMEM((512, 256), BF16),
        pltpu.VMEM((2, 8, 8, 896), F32),
        pltpu.VMEM((2, 8, 8, 896), F32),
        pltpu.VMEM((2, 4, 32, 896), F32),
        pltpu.VMEM((2, 4, 32, 896), F32),
        pltpu.VMEM((192, 256), BF16),
        dma((4, 2)),
        dma((7,)),
        dma((2,)), dma((2, 2)), dma((2,)), dma((2,)), dma((2,)), dma((2,)),
        dma((2,)), dma((2,)), dma((2,)), dma((2, 2)), dma((2,)), dma((2, 4)),
        dma((2,)),
    ]
    ig, wg = pl.pallas_call(
        body,
        out_shape=(
            jax.ShapeDtypeStruct(field_shape, F32),
            jax.ShapeDtypeStruct(w_shape, F32),
        ),
        in_specs=[vmem, smem] + [vmem] * len(IN_VMEM) + [hbm] * (len(IN_HBM) + 3),
        out_specs=(hbm, hbm),
        scratch_shapes=scratch,
        compiler_params=pltpu.CompilerParams(
            collective_id=0, has_side_effects=True, vmem_limit_bytes=58 * 1024 * 1024
        ),
        cost_estimate=pl.CostEstimate(flops=10**10, bytes_accessed=2 * 10**7, transcendentals=0),
    )(
        point_weight, point_bias,
        *[tabs[name] for name in IN_VMEM],
        *[tabs[name] for name in IN_HBM],
        input_field.reshape(field_shape), cotangent.reshape(field_shape), spectral_weights,
    )
    return (ig.reshape(input_field.shape).astype(BF16), wg)


def solution(mesh):
    return jax.shard_map(
        per_device,
        mesh=mesh,
        in_specs=(
            P(None, None, "gx", "gy", None),
            P(None, None, "gx", "gy", None),
            P(None, None, "gy", "gx", None),
            P(),
            P(),
        ),
        out_specs=(P(None, None, "gx", "gy", None), P(None, None, "gy", "gx", None)),
        check_vma=False,
    )
```

```python
import math

import jax
import jax.numpy as jnp
import ml_dtypes
import numpy as np
from jax import lax
from jax.experimental import pallas as pl
from jax.experimental.pallas import tpu as pltpu
from jax.sharding import PartitionSpec as P

C = 32
NX = 192
NY = 256
NZ = 256
KX = 48
KY = 64
KZ = 17
SCALE = (NX * NY * NZ) ** (-0.5)
MESH = pl.DeviceIdType.MESH
F32 = jnp.float32
BF16 = jnp.bfloat16


def kept(count, number):
    half = number // 2
    return np.concatenate([np.arange(half), np.arange(half) + count - half])


def trig(points, freqs, count):
    angle = 2.0 * np.pi * ((points[:, None] * freqs[None, :]) % count) / count
    return np.cos(angle), np.sin(angle)


def hi_lo(table):
    table = np.asarray(table, np.float32)
    high = table.astype(ml_dtypes.bfloat16)
    low = (table - high.astype(np.float32)).astype(ml_dtypes.bfloat16)
    return high, low


def make_tables():
    z_cos, z_sin = trig(np.arange(NZ), np.arange(KZ), NZ)
    y_cos, y_sin = trig(np.arange(NY), kept(NY, KY), NY)
    x_cos, x_sin = trig(np.arange(NX), kept(NX, KX), NX)
    tabs = {}
    wz = np.zeros((4, NZ, 2, 2, 4, 16))
    zz = np.zeros((4, 2, 2, 4, 16, NZ))
    for c4 in range(4):
        wz[c4, :, 0, 0, c4, :] = z_cos[:, :16]
        wz[c4, :, 0, 1, c4, :] = -z_sin[:, :16]
        wz[c4, :, 1, 0, c4, :] = z_cos[:, 16:17]
        wz[c4, :, 1, 1, c4, :] = -z_sin[:, 16:17]
        zz[c4, 0, 0, c4] = z_cos[:, :16].T
        zz[c4, 0, 1, c4] = -z_sin[:, :16].T
        zz[c4, 1, 0, c4] = z_cos[:, 16:17].T
        zz[c4, 1, 1, c4] = -z_sin[:, 16:17].T
    tabs["wz"] = wz.reshape(4, NZ, 256).astype(np.float32).astype(ml_dtypes.bfloat16)
    tabs["zz"] = hi_lo(zz.reshape(4, 256, NZ))[0]
    s_at, zl_at, j_at = np.meshgrid(np.arange(8), np.arange(4), np.arange(2), indexing="ij")
    order = ((zl_at * 8 + s_at) * 2 + j_at).reshape(-1)
    yc = (y_cos * SCALE)[:, order].reshape(2, 128, 64)
    ys = (y_sin * SCALE)[:, order].reshape(2, 128, 64)
    inv = np.concatenate([yc, ys], 2)
    fwd = inv.transpose(0, 2, 1)
    tabs["t1"] = np.stack([np.concatenate([h, h, l], -1) for h, l in [hi_lo(fwd[0]), hi_lo(fwd[1])]])
    tabs["t1i"] = np.stack([np.concatenate([h, h, l], -1) for h, l in [hi_lo(inv[0]), hi_lo(inv[1])]])
    xt = np.stack([x_cos, x_sin]).reshape(2, 4, 8, 6, 2, 4, 6)
    t2 = np.zeros((4, 2, 4, 2, 4, 16, 6, 8, 8))
    for zl_to in range(4):
        for i in range(6):
            for j in range(2):
                block = xt[:, :, :, :, :, :, i]
                t2[:, :, zl_to, :, :, 2 * i + j, :, :, zl_to * 2 + j] = block.transpose(1, 4, 0, 5, 3, 2)
    fwd = t2.reshape(4, 8, 128, 384)
    tabs["t2"] = np.concatenate(hi_lo(fwd), 2)
    inv = t2.transpose(0, 6, 3, 7, 8, 1, 2, 4, 5).reshape(4, 6, 128, 512)
    tabs["t2i"] = np.concatenate(hi_lo(inv), 2)
    eye2, eye4 = np.eye(2), np.eye(4)
    ones16, ones32 = np.ones(16), np.ones(32)
    e1 = np.einsum("qr,cd,s,o->qcsrdo", eye2, eye4, ones16, ones32)
    tabs["e1"] = e1.reshape(128, 256)
    tabs["r2"] = e1.reshape(128, 256).T
    pick = np.eye(32).reshape(8, 4, 32)
    e2 = np.einsum("qr,bio,s,c->bqisrco", eye2, pick, ones16, np.ones(4)).reshape(8, 128, 256)
    tabs["e2"] = e2
    tabs["rr"] = e2.reshape(2, 2, 2, 128, 256).transpose(2, 0, 4, 1, 3).reshape(2, 2, 256, 256)
    slot = np.zeros((6, 16, 16))
    for x in range(6):
        slot[x, x, :] = 1.0
    spread = np.einsum("qr,cd,xst->xqcsrdt", eye2, eye4, slot).reshape(6, 128, 128)
    tabs["spread"] = spread.transpose(1, 0, 2).reshape(128, 768)
    tabs["gather"] = spread.transpose(0, 2, 1)
    tabs["a16"] = np.repeat(np.eye(32), 16, axis=0)
    for name in ("e1", "r2", "e2", "rr", "spread", "gather", "a16"):
        tabs[name] = tabs[name].astype(ml_dtypes.bfloat16)
    return tabs


TABLES = make_tables()
IN_VMEM = ("wz", "t1", "a16", "spread", "gather", "t1i", "e1", "r2")
IN_HBM = ("t2", "t2i", "zz", "e2", "rr")


def mm(left, right):
    return jnp.dot(left, right, preferred_element_type=F32)


def halves(values):
    high = values.astype(BF16)
    return high, (values - high.astype(F32)).astype(BF16)


def gelu_slope(values):
    size = jnp.abs(values)
    below = 1.0 + (0.3275911 / math.sqrt(2.0)) * size
    t = pl.reciprocal(below, approx=True)
    t = t * (2.0 - below * t)
    poly = t * (0.127414796 + t * (-0.142248368 + t * (0.7107068705 + t * (-0.7265760135 + t * 0.5307027145))))
    bell = jnp.exp2((-0.5 / math.log(2.0)) * (values * values))
    part = bell * (poly - (1.0 / math.sqrt(2.0 * math.pi)) * size)
    return jnp.where(values >= 0.0, 1.0 - part, part)


def swap(values, first):
    lane = lax.broadcasted_iota(jnp.int32, (values.shape[0], 128), 1)
    sign = jnp.where(lane < 64, first, -first)
    parts = [
        pltpu.roll(values[:, at : at + 128], 64, 1) * sign for at in range(0, values.shape[1], 128)
    ]
    return parts[0] if len(parts) == 1 else jnp.concatenate(parts, 1)


def slot_of(shape):
    return lax.broadcasted_iota(jnp.int32, shape, len(shape) - 1) % 16


def spread_rows(block):
    slots = slot_of((16, 128))
    rows = lax.broadcasted_iota(jnp.int32, (16, 128), 0)
    parts = [jnp.where(slots == k, block, 0.0) for k in range(16)]
    parts.append(jnp.where(slots == rows, jnp.broadcast_to(block[12:13], (16, 128)), 0.0))
    return jnp.concatenate(parts, 0)


def gather_rows(values):
    slots = slot_of((16, 128))
    rows = lax.broadcasted_iota(jnp.int32, (16, 128), 0)
    total = jnp.where(slots == 0, values[0:16], 0.0)
    for k in range(1, 16):
        total = total + jnp.where(slots == k, values[16 * k : 16 * k + 16], 0.0)
    last = jnp.sum(jnp.where(slots == rows, values[256:272], 0.0), axis=0, keepdims=True)
    return jnp.where(rows == 12, jnp.broadcast_to(last, (16, 128)), total)


def split_left(values, table):
    high, low = halves(values)
    out = mm(jnp.concatenate([high, low], 0), table)
    return out[: values.shape[0]] + out[values.shape[0] :]


GROUPS = ((0, 512), (512, 384))
CHUNKS = (((0, 256), (256, 256)), ((512, 256), (768, 128)))
ROWS = 13


def body(
    pw, bias, wz, t1, a16, spread, gather, t1i, e1, r2,
    t2_hbm, t2i_hbm, zz_hbm, e2_hbm, rr_hbm, f_hbm, cot_hbm, w_hbm,
    ig, wg_out,
    t2, t2i, zz, e2, rr, f, cot, w_in, w, wg, pg, lin, kron,
    u, r0, vs, r1, rsb, r3a, md, xb, mexp, gexp, acc,
    mq, r3b, xb2, vs2, r1s, ys, r0s, zb, rel, rel_g,
    f_sem, local_sem, s1s, s1r, s2s, s2r, s3s, s3r, g3s, g3r, g2s, g2r, g1s, g1r, rel_r, rel_s, rel_gr, rel_gs,
):
    gx = lax.axis_index("gx")
    gy = lax.axis_index("gy")
    zl, s = gx // 8, gx % 8
    zh, yy = gy // 4, gy % 4
    me = (zh * 4 + zl) * 4 + yy

    def y_id(to):
        return (gx, zh * 4 + to)

    def s_id(to):
        return (zl * 8 + to, gy)

    def m_id(to):
        return (((to // 4) % 4) * 8 + s, (to // 16) * 4 + to % 4)

    def each(low, high, fn):
        def step(d, carry):
            fn(d)
            return carry

        lax.fori_loop(low, high, step, 0)

    def f_load(to, h):
        return pltpu.make_async_copy(f_hbm.at[to, h], f.at[to, h], f_sem.at[to, h])

    for h in range(2):
        each(1, 5, lambda d, h=h: f_load((yy + d) % 4, h).start())

    barrier = pltpu.get_barrier_semaphore()

    r3a[:, :, 8:16, :] = jnp.zeros((2, 32, 8, 128), F32)
    r3b[:, :, 8:16, :] = jnp.zeros((2, 32, 8, 128), F32)

    def greet(device):
        pl.semaphore_signal(barrier, inc=1, device_id=device, device_id_type=MESH)

    each(1, 8, lambda d: greet(s_id((s + d) % 8)))
    each(1, 32, lambda d: greet(m_id((me + d) % 32)))

    loads = [
        pltpu.make_async_copy(src, dst, local_sem.at[n])
        for n, (src, dst) in enumerate(
            [
                (w_hbm, w_in),
                (t2_hbm.at[zl], t2),
                (rr_hbm, rr),
                (t2i_hbm.at[zl], t2i),
                (cot_hbm, cot),
                (zz_hbm, zz),
                (e2_hbm, e2),
            ]
        )
    ]
    for load in loads:
        load.start()
    def send(src, dst, send_sem, recv_sem, device):
        return pltpu.make_async_remote_copy(src, dst, send_sem, recv_sem, device_id=device, device_id_type=MESH)

    def c1(h, to, g):
        cells = pl.ds(*GROUPS[g])
        return send(u.at[h, to, :, cells], r0.at[h, yy, :, cells], s1s.at[h], s1r.at[h, g], y_id(to))

    def c2(h, to, g):
        cells = pl.ds(*GROUPS[g])
        return send(vs.at[h, to, :, cells], r1.at[h, s, :, cells], s2s.at[h], s2r.at[h], s_id(to))

    def c3(h, to):
        rows = pl.ds(0, ROWS)
        return send(rsb.at[h, to, rows], r3a.at[h, me, rows], s3s.at[h], s3r.at[h], m_id(to))

    def k3(h, to):
        rows = pl.ds(0, ROWS)
        return send(mq.at[h, to % 4, rows], r3b.at[h, me, rows], g3s.at[h], g3r.at[h], m_id(to))

    def k2(h, to, g):
        cells = pl.ds(*GROUPS[g])
        return send(vs2.at[h, to, :, cells], r1s.at[h, s, :, cells], g2s.at[h], g2r.at[h, g], s_id(to))

    def k1(h, to, g):
        cells = pl.ds(*GROUPS[g])
        return send(ys.at[h, to, :, cells], r0s.at[h, yy, :, cells], g1s.at[h], g1r.at[h, yy], y_id(to))

    def far_f(h, g):
        cells = pl.ds(*GROUPS[g])
        return send(
            u.at[h, (yy + 2) % 4, :, cells],
            rel.at[h, :, cells],
            s1s.at[h],
            rel_r.at[h, g],
            y_id((yy + 1 + 2 * g) % 4),
        )

    def far_g(h, g):
        cells = pl.ds(*GROUPS[g])
        return send(
            ys.at[h, (yy + 2) % 4, :, cells],
            rel_g.at[h, :, cells],
            g1s.at[h],
            rel_gr.at[h, g],
            y_id((yy + 1 + 2 * g) % 4),
        )

    def forward_f(h, g):
        cells = pl.ds(*GROUPS[g])
        part = rel.at[h, :, cells]
        whole(part, rel_r.at[h, g])
        dest = r0.at[h, (yy + 3 + 2 * g) % 4, :, cells]
        send(part, dest, rel_s.at[h], s1r.at[h, g], y_id((yy + 1 + 2 * g) % 4)).start()

    def forward_g(h, g):
        cells = pl.ds(*GROUPS[g])
        part = rel_g.at[h, :, cells]
        whole(part, rel_gr.at[h, g])
        fr = (yy + 3 + 2 * g) % 4
        send(part, r0s.at[h, fr, :, cells], rel_gs.at[h], g1r.at[h, fr], y_id((yy + 1 + 2 * g) % 4)).start()

    def whole(part, sem):
        pltpu.make_async_copy(part, part, sem).wait()

    def all_of(buffer, h, count, sem):
        whole(buffer.at[h, pl.ds(0, count)], sem.at[h])

    def all_of_group(buffer, h, count, sem, g):
        whole(buffer.at[h, pl.ds(0, count), :, pl.ds(*GROUPS[g])], sem.at[h, g])

    def all_modes(buffer, h, sem):
        whole(buffer.at[h, pl.ds(0, 31), pl.ds(0, ROWS)], sem.at[h])

    def z_analysis(source, h, to, dest):
        total = None
        for q in range(4):
            term = mm(source[to, h, q].reshape(192, 256), wz[q])
            total = term if total is None else total + term
        slots = slot_of((32, 128))
        last = None
        for x in range(6):
            rows = total[32 * x : 32 * x + 32]
            dest[:, 128 * x : 128 * x + 128] = rows[:, :128]
            part = jnp.where(slots == x, rows[:, 128:], 0.0)
            last = part if last is None else last + part
        dest[:, 768:896] = last

    def analysis_load(h, d):
        to = (yy + d) % 4
        f_load(to, h).wait()
        z_analysis(f, h, to, u.at[h, to])

    def analysis_near(h):
        for g in range(2):
            for d in (1, 3):
                c1(h, (yy + d) % 4, g).start()

    def analysis_own(h):
        f_load(yy, h).wait()
        z_analysis(f, h, yy, r0.at[h, yy])

    def analysis_start():
        each(1, 4, lambda d: analysis_load(0, d))
        pl.semaphore_wait(barrier, 38)
        for g in range(2):
            far_f(0, g).start()
        analysis_near(0)
        analysis_load(1, 2)
        for g in range(2):
            far_f(1, g).start()
        each(0, 2, lambda n: analysis_load(1, 1 + 2 * n))
        analysis_own(0)
        for g in range(2):
            forward_f(0, g)
        analysis_near(1)
        analysis_own(1)

    def y_analysis(h, g):
        table = t1.at[zh]
        for at, wide in CHUNKS[g]:
            high, low = halves(r0[h, :, :, at : at + wide].reshape(128, wide))
            both = jnp.concatenate([high, low], 0)
            out = mm(table[:, 0:256], both) + mm(table[:, 256:384], high)
            vs[h, :, :, at : at + wide] = (out[:64] + swap(out[64:], 1.0)).reshape(8, 8, wide)

    def x_analysis_load(h):
        last = r1[h, :, :, 768:896].reshape(64, 128).astype(BF16)
        last = mm(last, spread[...]).astype(BF16)
        for x in range(6):
            at = 128 * x
            xb[64 * x : 64 * x + 64, 0:128] = r1[h, :, :, at : at + 128].reshape(64, 128).astype(BF16)
            xb[64 * x : 64 * x + 64, 128:256] = last[:, at : at + 128]

    def x_analysis_store(out, h, z):
        out = out[:64] + swap(out[64:], 1.0)
        rows = lax.broadcasted_iota(jnp.int32, (64, 128), 0) % 16
        last = jnp.where(slot_of((64, 128)) == rows, out[:, 128:], 0.0)
        last = jnp.sum(last.reshape(4, 16, 128), axis=1, keepdims=True)
        last = jnp.broadcast_to(last, (4, 16, 128)).reshape(64, 128)
        rsb[h, pl.ds(4 * z, 4)] = jnp.where(rows == 12, last, out[:, :128]).reshape(4, 16, 128)

    def x_analysis(h):
        mine = me // 4
        for group in ((1, 2), (3, 4), (5, 6), (7, 8)):
            to = [(mine + d) % 8 for d in group]
            out = mm(jnp.concatenate([t2[z] for z in to], 0), xb[...])
            for n, d in enumerate(group):
                x_analysis_store(out[256 * n : 256 * n + 128] + out[256 * n + 128 : 256 * n + 256], h, to[n])
                each(0 if d < 8 else 1, 4, lambda y: c3(h, to[n] * 4 + (yy + y) % 4).start())
        r3a[h, me] = rsb[h, me]

    def analysis(first, second, received):
        first()
        for h in range(2):
            for g in range(2):
                all_of_group(r0, h, 3, s1r, g)
                y_analysis(h, g)
                each(1, 8, lambda d: c2(h, (s + d) % 8, g).start())
            r1[h, s] = vs[h, s]
        for h in range(2):
            all_of(r1, h, 7, s2r)
            x_analysis_load(h)
            x_analysis(h)
        second()
        for h in range(2):
            all_modes(r3a, h, s3r)
            total = r3a[h, 0:4]
            for z in range(1, 8):
                total = total + r3a[h, 4 * z : 4 * z + 4]
            md[h] = total
            received(h)

    def analysis_end():
        for h in range(2):
            all_of(u, h, 3, s1s)
            all_of(vs, h, 7, s2s)
            all_modes(rsb, h, s3s)

    def x_synthesis_load(h):
        main = r3b[h]
        rows = lax.broadcasted_iota(jnp.int32, (512, 128), 0) % 16
        last = jnp.broadcast_to(main[:, 12:13], (32, 16, 128)).reshape(512, 128)
        xb2[:, 0:128] = main.reshape(512, 128).astype(BF16)
        xb2[:, 128:256] = jnp.where(slot_of((512, 128)) == rows, last, 0.0).astype(BF16)

    def x_synthesis(h):
        total = None
        for group in ((0, 1), (2, 3), (4, 5)):
            out = mm(jnp.concatenate([t2i[x] for x in group], 0), xb2[...])
            for n, x in enumerate(group):
                part = out[256 * n : 256 * n + 128] + out[256 * n + 128 : 256 * n + 256]
                part = part[:64] + swap(part[64:], -1.0)
                vs2[h, :, :, 128 * x : 128 * x + 128] = part[:, :128].reshape(8, 8, 128)
                high, low = halves(part[:, 128:])
                last = mm(high, gather[x]) + mm(low, gather[x])
                total = last if total is None else total + last
            if group == (2, 3):
                each(1, 8, lambda d: k2(h, (s + d) % 8, 0).start())
        vs2[h, :, :, 768:896] = total.reshape(8, 8, 128)
        each(1, 8, lambda d: k2(h, (s + d) % 8, 1).start())

    def y_synthesis(h, g):
        table = t1i.at[zh]
        for at, wide in CHUNKS[g]:
            values = r1s[h, :, :, at : at + wide].reshape(64, wide)
            high, low = halves(jnp.concatenate([values, swap(values, -1.0)], 0))
            out = mm(table[:, 0:256], jnp.concatenate([high, low], 0)) + mm(table[:, 256:384], high)
            ys[h, :, :, at : at + wide] = out.reshape(4, 32, wide)

    def z_synthesis(h, fr, finish):
        slots = slot_of((32, 128))
        last = r0s[h, fr, :, 768:896]
        for x in range(6):
            zb[32 * x : 32 * x + 32, 0:128] = r0s[h, fr, :, 128 * x : 128 * x + 128].astype(BF16)
            zb[32 * x : 32 * x + 32, 128:256] = jnp.where(slots == x, last, 0.0).astype(BF16)

        def one(q):
            finish(fr, h, q, mm(zb[...], zz[q]).reshape(6, 32, 256))

        each(0, 4, one)

    def synthesis(meanwhile, finish, own, after):
        meanwhile()
        for h in range(2):
            all_modes(r3b, h, g3r)
            x_synthesis_load(h)
            x_synthesis(h)
            r1s[h, s] = vs2[h, s]
        for h in range(2):
            for g in range(2):
                all_of_group(r1s, h, 7, g2r, g)
                y_synthesis(h, g)
                far_g(h, g).start()
                for d in (1, 3):
                    k1(h, (yy + d) % 4, g).start()
                if h == 1:
                    forward_g(0, g)
            r0s[h, yy] = ys[h, yy]
        for h in range(2):
            z_synthesis(h, yy, finish)
            own(h)
        for g in range(2):
            forward_g(1, g)
        for h in range(2):

            def one(d, h=h):
                fr = (yy + 2 * d - 1 - d // 3 * 3) % 4
                whole(r0s.at[h, fr], g1r.at[h, fr])
                z_synthesis(h, fr, finish)
                after(h, fr)

            each(1, 4, one)
        for h in range(2):
            all_modes(r3b, h, g3s)
            all_of(vs2, h, 7, g2s)
            all_of(ys, h, 3, g1s)
            whole(rel_g.at[h], rel_gs.at[h])

    def channel_map(wide, source):
        rows = lax.broadcasted_iota(jnp.int32, (512, 512), 0) % 16
        columns = lax.broadcasted_iota(jnp.int32, (512, 512), 1) % 16
        full = lax.dot_general(
            wide.astype(BF16), a16[...], (((1,), (1,)), ((), ())), preferred_element_type=F32
        )
        kron[...] = jnp.where(rows == columns, full, 0.0).astype(BF16)

        def one(x):
            for at in (0, 16):
                block = source[:, :, :, x, at : at + 16, :].reshape(512, 256)
                out = mm(kron[...], block)
                lin[:, :, :, x, at : at + 16, :] = out.reshape(4, 2, 4, 16, 256)

        each(0, 6, one)

    def lanes(b):
        return pl.ds(pl.multiple_of(b * 128, 128), 128)

    def weights_in():
        loads[0].wait()

        def one(k):
            for part in range(2):
                for i in range(6):
                    w[part, k, 2 * i : 2 * i + 2, :] = w_in[part, k, i]
                w[part, k, 12:16, :] = jnp.zeros((4, 1024), F32)

        each(0, KZ, one)

    def weight_grad_out():
        def one(k):
            for part in range(2):
                for i in range(6):
                    wg_out[part, k, i] = wg[part, k, 2 * i : 2 * i + 2, :]

        each(0, KZ, one)

    def w_at(part, b):
        return w[part, :, :, lanes(b)].reshape(272, 128)

    def mix_one(h):
        def one(y):
            b = 2 * y + h
            modes = split_left(spread_rows(md[h, y]), e1[...])
            mexp[b] = modes
            real, imag = modes[:, :128], modes[:, 128:]
            w_real, w_imag = w_at(0, b), w_at(1, b)
            acc[:, :128] += w_real * real - w_imag * imag
            acc[:, 128:] += w_real * imag + w_imag * real

        each(0, 4, one)

    def spread_out(h, y):
        each(0, 8, lambda z: pl.when(z * 4 + y != me)(lambda: k3(h, z * 4 + y).start()))

    def keep_own(h):
        r3b[h, me] = mq[h, yy]

    def mix_two():
        for h in range(2):
            for pair in range(2):
                out = split_left(acc[...], rr[h, pair])
                for n in range(2):
                    y = 2 * pair + n
                    mq[h, y] = gather_rows(out[:, 128 * n : 128 * n + 128])
                    spread_out(h, y)
            keep_own(h)

    def back_one(h):
        def one(y):
            gexp[...] += split_left(spread_rows(md[h, y]), e2[2 * y + h])

        each(0, 4, one)

    def back_two():
        for h in range(2):

            def two(y, h=h):
                b = 2 * y + h
                g_real, g_imag = gexp[:, :128], gexp[:, 128:]
                w_real, w_imag = w_at(0, b), w_at(1, b)
                real = w_real * g_real + w_imag * g_imag
                imag = w_real * g_imag - w_imag * g_real
                mq[h, y] = gather_rows(split_left(jnp.concatenate([real, imag], 1), r2[...]))
                spread_out(h, y)

            each(0, 4, two)
            keep_own(h)

    def weight_grad():
        def one(b):
            g_real, g_imag = gexp[:, :128], gexp[:, 128:]
            real, imag = mexp[b, :, :128], mexp[b, :, 128:]
            wg[0, :, :, lanes(b)] = (real * g_real + imag * g_imag).reshape(KZ, 16, 128)
            wg[1, :, :, lanes(b)] = (real * g_imag - imag * g_real).reshape(KZ, 16, 128)

        each(0, 8, one)
        weight_grad_out()

    def finish_pre(fr, h, q, spectral):
        pre = spectral + lin[fr, h, q] + bias[fr * 8 + h * 4 + q]
        pg[fr, h, q] = (cot[fr, h, q].astype(F32) * gelu_slope(pre)).astype(BF16)

    def finish_grad(fr, h, q, spectral):
        ig[fr, h, q] = (spectral + lin[fr, h, q]).astype(BF16)

    def second_own(h):
        z_analysis(pg, h, yy, r0.at[h, yy])

    def second_start(h, to):
        z_analysis(pg, h, to, u.at[h, to])
        for g in range(2):
            c1(h, to, g).start()

    def first_y_wait():
        channel_map(mm(a16[...], pw[...]), f)
        for g in range(2):
            forward_f(1, g)
        loads[1].wait()

    def first_z_wait():
        weights_in()
        acc[...] = jnp.zeros_like(acc)

    def second_z_wait():
        wide = lax.dot_general(a16[...], pw[...], (((1,), (1,)), ((), ())), preferred_element_type=F32)
        channel_map(wide, pg)
        gexp[...] = jnp.zeros_like(gexp)

    def wait_loads():
        for load in loads[3:]:
            load.wait()

    analysis_start()
    analysis(first_y_wait, first_z_wait, mix_one)
    loads[2].wait()
    mix_two()
    analysis_end()
    for h in range(2):
        whole(rel.at[h], rel_s.at[h])
    synthesis(wait_loads, finish_pre, second_own, second_start)
    analysis(lambda: None, second_z_wait, back_one)
    back_two()
    synthesis(weight_grad, finish_grad, lambda h: None, lambda h, fr: None)
    analysis_end()


def per_device(input_field, cotangent, spectral_weights, point_weight, point_bias):
    field_shape = (4, 2, 4, 6, 32, 256)
    w_shape = spectral_weights.shape
    tabs = {name: jnp.asarray(value) for name, value in TABLES.items()}
    vmem = pl.BlockSpec(memory_space=pltpu.VMEM)
    smem = pl.BlockSpec(memory_space=pltpu.SMEM)
    hbm = pl.BlockSpec(memory_space=pl.ANY)
    dma = pltpu.SemaphoreType.DMA
    scratch = [
        pltpu.VMEM((8, 256, 384), BF16),
        pltpu.VMEM((6, 256, 512), BF16),
        pltpu.VMEM((4, 256, 256), BF16),
        pltpu.VMEM((8, 128, 256), BF16),
        pltpu.VMEM((2, 2, 256, 256), BF16),
        pltpu.VMEM(field_shape, BF16),
        pltpu.VMEM(field_shape, BF16),
        pltpu.VMEM(w_shape, F32),
        pltpu.VMEM((2, KZ, 16, 1024), F32),
        pltpu.VMEM((2, KZ, 16, 1024), F32),
        pltpu.VMEM(field_shape, BF16),
        pltpu.VMEM(field_shape, F32),
        pltpu.VMEM((512, 512), BF16),
        pltpu.VMEM((2, 4, 32, 896), F32),
        pltpu.VMEM((2, 4, 32, 896), F32),
        pltpu.VMEM((2, 8, 8, 896), F32),
        pltpu.VMEM((2, 8, 8, 896), F32),
        pltpu.VMEM((2, 32, 16, 128), F32),
        pltpu.VMEM((2, 32, 16, 128), F32),
        pltpu.VMEM((2, 4, 16, 128), F32),
        pltpu.VMEM((384, 256), BF16),
        pltpu.VMEM((8, 272, 256), F32),
        pltpu.VMEM((272, 256), F32),
        pltpu.VMEM((272, 256), F32),
        pltpu.VMEM((2, 4, 16, 128), F32),
        pltpu.VMEM((2, 32, 16, 128), F32),
        pltpu.VMEM((512, 256), BF16),
        pltpu.VMEM((2, 8, 8, 896), F32),
        pltpu.VMEM((2, 8, 8, 896), F32),
        pltpu.VMEM((2, 4, 32, 896), F32),
        pltpu.VMEM((2, 4, 32, 896), F32),
        pltpu.VMEM((192, 256), BF16),
        pltpu.VMEM((2, 32, 896), F32),
        pltpu.VMEM((2, 32, 896), F32),
        dma((4, 2)),
        dma((7,)),
        dma((2,)), dma((2, 2)), dma((2,)), dma((2,)), dma((2,)), dma((2,)),
        dma((2,)), dma((2,)), dma((2,)), dma((2, 2)), dma((2,)), dma((2, 4)),
        dma((2, 2)), dma((2,)), dma((2, 2)), dma((2,)),
    ]
    ig, wg = pl.pallas_call(
        body,
        out_shape=(
            pltpu.VMEM(field_shape, BF16),
            pltpu.VMEM(w_shape, F32),
        ),
        in_specs=[vmem, smem] + [vmem] * len(IN_VMEM) + [hbm] * (len(IN_HBM) + 3),
        out_specs=(vmem, vmem),
        scratch_shapes=scratch,
        compiler_params=pltpu.CompilerParams(
            collective_id=0, has_side_effects=True, vmem_limit_bytes=50 * 1024 * 1024
        ),
        cost_estimate=pl.CostEstimate(flops=10**10, bytes_accessed=2 * 10**7, transcendentals=0),
    )(
        point_weight, point_bias,
        *[tabs[name] for name in IN_VMEM],
        *[tabs[name] for name in IN_HBM],
        input_field.reshape(field_shape), cotangent.reshape(field_shape), spectral_weights,
    )
    return (ig.reshape(input_field.shape), wg)


def solution(mesh):
    return jax.shard_map(
        per_device,
        mesh=mesh,
        in_specs=(
            P(None, None, "gx", "gy", None),
            P(None, None, "gx", "gy", None),
            P(None, None, "gy", "gx", None),
            P(),
            P(),
        ),
        out_specs=(P(None, None, "gx", "gy", None), P(None, None, "gy", "gx", None)),
        check_vma=False,
    )
```

```python
import math

import jax
import jax.numpy as jnp
import ml_dtypes
import numpy as np
from jax import lax
from jax.experimental import pallas as pl
from jax.experimental.pallas import tpu as pltpu
from jax.sharding import PartitionSpec as P

C = 32
NX = 192
NY = 256
NZ = 256
KX = 48
KY = 64
KZ = 17
SCALE = (NX * NY * NZ) ** (-0.5)
MESH = pl.DeviceIdType.MESH
F32 = jnp.float32
BF16 = jnp.bfloat16


def kept(count, number):
    half = number // 2
    return np.concatenate([np.arange(half), np.arange(half) + count - half])


def trig(points, freqs, count):
    angle = 2.0 * np.pi * ((points[:, None] * freqs[None, :]) % count) / count
    return np.cos(angle), np.sin(angle)


def hi_lo(table):
    table = np.asarray(table, np.float32)
    high = table.astype(ml_dtypes.bfloat16)
    low = (table - high.astype(np.float32)).astype(ml_dtypes.bfloat16)
    return high, low


def make_tables():
    z_cos, z_sin = trig(np.arange(NZ), np.arange(KZ), NZ)
    y_cos, y_sin = trig(np.arange(NY), kept(NY, KY), NY)
    x_cos, x_sin = trig(np.arange(NX), kept(NX, KX), NX)
    tabs = {}
    wz = np.zeros((4, NZ, 2, 2, 4, 16))
    zz = np.zeros((4, 2, 2, 4, 16, NZ))
    for c4 in range(4):
        wz[c4, :, 0, 0, c4, :] = z_cos[:, :16]
        wz[c4, :, 0, 1, c4, :] = -z_sin[:, :16]
        wz[c4, :, 1, 0, c4, :] = z_cos[:, 16:17]
        wz[c4, :, 1, 1, c4, :] = -z_sin[:, 16:17]
        zz[c4, 0, 0, c4] = z_cos[:, :16].T
        zz[c4, 0, 1, c4] = -z_sin[:, :16].T
        zz[c4, 1, 0, c4] = z_cos[:, 16:17].T
        zz[c4, 1, 1, c4] = -z_sin[:, 16:17].T
    tabs["wz"] = wz.reshape(4, NZ, 256).astype(np.float32).astype(ml_dtypes.bfloat16)
    tabs["zz"] = hi_lo(zz.reshape(4, 256, NZ))[0]
    s_at, zl_at, j_at = np.meshgrid(np.arange(8), np.arange(4), np.arange(2), indexing="ij")
    order = ((zl_at * 8 + s_at) * 2 + j_at).reshape(-1)
    yc = (y_cos * SCALE)[:, order].reshape(2, 128, 64)
    ys = (y_sin * SCALE)[:, order].reshape(2, 128, 64)
    inv = np.concatenate([yc, ys], 2)
    fwd = inv.transpose(0, 2, 1)
    tabs["t1"] = np.stack([np.concatenate([h, h, l], -1) for h, l in [hi_lo(fwd[0]), hi_lo(fwd[1])]])
    tabs["t1i"] = np.stack([np.concatenate([h, h, l], -1) for h, l in [hi_lo(inv[0]), hi_lo(inv[1])]])
    xt = np.stack([x_cos, x_sin]).reshape(2, 4, 8, 6, 2, 4, 6)
    t2 = np.zeros((4, 2, 4, 2, 4, 16, 6, 8, 8))
    for zl_to in range(4):
        for i in range(6):
            for j in range(2):
                block = xt[:, :, :, :, :, :, i]
                t2[:, :, zl_to, :, :, 2 * i + j, :, :, zl_to * 2 + j] = block.transpose(1, 4, 0, 5, 3, 2)
    fwd = t2.reshape(4, 8, 128, 384)
    tabs["t2"] = np.concatenate(hi_lo(fwd), 2)
    inv = t2.transpose(0, 6, 3, 7, 8, 1, 2, 4, 5).reshape(4, 6, 128, 512)
    tabs["t2i"] = np.concatenate(hi_lo(inv), 2)
    eye2, eye4 = np.eye(2), np.eye(4)
    ones16, ones32 = np.ones(16), np.ones(32)
    e1 = np.einsum("qr,cd,s,o->qcsrdo", eye2, eye4, ones16, ones32)
    tabs["e1"] = e1.reshape(128, 256)
    tabs["r2"] = e1.reshape(128, 256).T
    pick = np.eye(32).reshape(8, 4, 32)
    e2 = np.einsum("qr,bio,s,c->bqisrco", eye2, pick, ones16, np.ones(4)).reshape(8, 128, 256)
    tabs["e2"] = e2
    tabs["rr"] = e2.reshape(2, 2, 2, 128, 256).transpose(2, 0, 4, 1, 3).reshape(2, 2, 256, 256)
    slot = np.zeros((6, 16, 16))
    for x in range(6):
        slot[x, x, :] = 1.0
    spread = np.einsum("qr,cd,xst->xqcsrdt", eye2, eye4, slot).reshape(6, 128, 128)
    tabs["spread"] = spread.transpose(1, 0, 2).reshape(128, 768)
    tabs["gather"] = spread.transpose(0, 2, 1)
    tabs["a16"] = np.repeat(np.eye(32), 16, axis=0)
    for name in ("e1", "r2", "e2", "rr", "spread", "gather", "a16"):
        tabs[name] = tabs[name].astype(ml_dtypes.bfloat16)
    return tabs


TABLES = make_tables()
IN_VMEM = ("wz", "t1", "a16", "spread", "gather", "t1i", "e1", "r2")
IN_HBM = ("t2", "t2i", "zz", "e2", "rr")


def mm(left, right):
    return jnp.dot(left, right, preferred_element_type=F32)


def halves(values):
    high = values.astype(BF16)
    return high, (values - high.astype(F32)).astype(BF16)


def gelu_slope(values):
    size = jnp.abs(values)
    below = 1.0 + (0.3275911 / math.sqrt(2.0)) * size
    t = pl.reciprocal(below, approx=True)
    t = t * (2.0 - below * t)
    poly = t * (0.127414796 + t * (-0.142248368 + t * (0.7107068705 + t * (-0.7265760135 + t * 0.5307027145))))
    bell = jnp.exp2((-0.5 / math.log(2.0)) * (values * values))
    part = bell * (poly - (1.0 / math.sqrt(2.0 * math.pi)) * size)
    return jnp.where(values >= 0.0, 1.0 - part, part)


def swap(values, first):
    lane = lax.broadcasted_iota(jnp.int32, (values.shape[0], 128), 1)
    sign = jnp.where(lane < 64, first, -first)
    parts = [
        pltpu.roll(values[:, at : at + 128], 64, 1) * sign for at in range(0, values.shape[1], 128)
    ]
    return parts[0] if len(parts) == 1 else jnp.concatenate(parts, 1)


def slot_of(shape):
    return lax.broadcasted_iota(jnp.int32, shape, len(shape) - 1) % 16


def spread_rows(block):
    slots = slot_of((16, 128))
    rows = lax.broadcasted_iota(jnp.int32, (16, 128), 0)
    parts = [jnp.where(slots == k, block, 0.0) for k in range(16)]
    parts.append(jnp.where(slots == rows, jnp.broadcast_to(block[12:13], (16, 128)), 0.0))
    return jnp.concatenate(parts, 0)


def gather_rows(values):
    slots = slot_of((16, 128))
    rows = lax.broadcasted_iota(jnp.int32, (16, 128), 0)
    total = jnp.where(slots == 0, values[0:16], 0.0)
    for k in range(1, 16):
        total = total + jnp.where(slots == k, values[16 * k : 16 * k + 16], 0.0)
    last = jnp.sum(jnp.where(slots == rows, values[256:272], 0.0), axis=0, keepdims=True)
    return jnp.where(rows == 12, jnp.broadcast_to(last, (16, 128)), total)


def split_left(values, table):
    high, low = halves(values)
    out = mm(jnp.concatenate([high, low], 0), table)
    return out[: values.shape[0]] + out[values.shape[0] :]


GROUPS = ((0, 512), (512, 384))
CHUNKS = (((0, 256), (256, 256)), ((512, 256), (768, 128)))
ROWS = 13


def body(
    pw, bias, wz, t1, a16, spread, gather, t1i, e1, r2,
    t2_hbm, t2i_hbm, zz_hbm, e2_hbm, rr_hbm, f_hbm, cot_hbm, w_hbm,
    ig, wg_out,
    t2, t2i, zz, e2, rr, f, cot, w_in, w, wg, pg, lin, kron,
    u, r0, vs, r1, rsb, r3a, md, xb, mexp, gexp, acc,
    mq, r3b, xb2, vs2, r1s, ys, r0s, zb,
    f_sem, local_sem, s1s, s1r, s2s, s2r, s3s, s3r, g3s, g3r, g2s, g2r, g1s, g1r,
):
    gx = lax.axis_index("gx")
    gy = lax.axis_index("gy")
    zl, s = lax.div(gx, 8), lax.rem(gx, 8)
    zh, yy = lax.div(gy, 4), lax.rem(gy, 4)
    me = (zh * 4 + zl) * 4 + yy

    def y_id(to):
        return (gx, zh * 4 + to)

    def s_id(to):
        return (zl * 8 + to, gy)

    def m_id(zl_to, zh_to, y_to):
        return (zl_to * 8 + s, zh_to * 4 + y_to)

    def others(first):
        def one(z, y):
            pl.when(me != z * 4 + y)(lambda: first(z, z % 4, z // 4, y))

        for z in range(8):
            for y in range(4):
                one(z, y)

    def y_at(d):
        return lax.rem(yy + d, 4)

    def s_at(d):
        return lax.rem(s + d, 8)

    def each(low, high, fn):
        def step(d, carry):
            fn(d)
            return carry

        lax.fori_loop(low, high, step, 0)

    def f_load(to, h):
        return pltpu.make_async_copy(f_hbm.at[to, h], f.at[to, h], f_sem.at[to, h])

    for h in range(2):
        each(1, 5, lambda d, h=h: f_load(y_at(d), h).start())

    barrier = pltpu.get_barrier_semaphore()

    r3a[:, :, 8:16, :] = jnp.zeros((2, 32, 8, 128), F32)
    r3b[:, :, 8:16, :] = jnp.zeros((2, 32, 8, 128), F32)

    def greet(device):
        pl.semaphore_signal(barrier, inc=1, device_id=device, device_id_type=MESH)

    for d in range(1, 8):
        greet(s_id(s_at(d)))
    others(lambda z, zl_to, zh_to, y: greet(m_id(zl_to, zh_to, y)))

    loads = [
        pltpu.make_async_copy(src, dst, local_sem.at[n])
        for n, (src, dst) in enumerate(
            [
                (w_hbm, w_in),
                (t2_hbm.at[zl], t2),
                (rr_hbm, rr),
                (t2i_hbm.at[zl], t2i),
                (cot_hbm, cot),
                (zz_hbm, zz),
                (e2_hbm, e2),
            ]
        )
    ]
    for load in loads:
        load.start()
    def send(src, dst, send_sem, recv_sem, device):
        return pltpu.make_async_remote_copy(src, dst, send_sem, recv_sem, device_id=device, device_id_type=MESH)

    def c1(h, to, g):
        cells = pl.ds(*GROUPS[g])
        return send(u.at[h, to, :, cells], r0.at[h, yy, :, cells], s1s.at[h], s1r.at[h, g], y_id(to))

    def c2(h, to, g):
        cells = pl.ds(*GROUPS[g])
        return send(vs.at[h, to, :, cells], r1.at[h, s, :, cells], s2s.at[h], s2r.at[h], s_id(to))

    def c3(h, z, device_y):
        rows = pl.ds(0, ROWS)
        device = m_id(lax.rem(z, 4), lax.div(z, 4), device_y)
        return send(rsb.at[h, z * 4 + device_y, rows], r3a.at[h, me, rows], s3s.at[h], s3r.at[h], device)

    def k3(h, zl_to, zh_to, y):
        rows = pl.ds(0, ROWS)
        device = m_id(zl_to, zh_to, y)
        return send(mq.at[h, y, rows], r3b.at[h, me, rows], g3s.at[h], g3r.at[h], device)

    def k2(h, to, g):
        cells = pl.ds(*GROUPS[g])
        return send(vs2.at[h, to, :, cells], r1s.at[h, s, :, cells], g2s.at[h], g2r.at[h, g], s_id(to))

    def k1(h, to, g):
        cells = pl.ds(*GROUPS[g])
        return send(ys.at[h, to, :, cells], r0s.at[h, yy, :, cells], g1s.at[h], g1r.at[h, yy], y_id(to))

    def whole(part, sem):
        pltpu.make_async_copy(part, part, sem).wait()

    def all_of(buffer, h, count, sem):
        whole(buffer.at[h, pl.ds(0, count)], sem.at[h])

    def all_of_group(buffer, h, count, sem, g):
        whole(buffer.at[h, pl.ds(0, count), :, pl.ds(*GROUPS[g])], sem.at[h, g])

    def all_modes(buffer, h, sem):
        whole(buffer.at[h, pl.ds(0, 31), pl.ds(0, ROWS)], sem.at[h])

    def z_analysis(source, h, to, dest):
        total = None
        for q in range(4):
            term = mm(source[to, h, q].reshape(192, 256), wz[q])
            total = term if total is None else total + term
        slots = slot_of((32, 128))
        last = None
        for x in range(6):
            rows = total[32 * x : 32 * x + 32]
            dest[:, 128 * x : 128 * x + 128] = rows[:, :128]
            part = jnp.where(slots == x, rows[:, 128:], 0.0)
            last = part if last is None else last + part
        dest[:, 768:896] = last

    def analysis_start(source, h, greeted):
        def one(d):
            to = y_at(d)
            f_load(to, h).wait()
            z_analysis(source, h, to, u.at[h, to])
            if greeted:
                c1(h, to, 0).start()

        each(1, 4, one)
        if not greeted:
            pl.semaphore_wait(barrier, 38)
            for d in range(1, 4):
                c1(h, y_at(d), 0).start()
        for d in range(1, 4):
            c1(h, y_at(d), 1).start()
        f_load(yy, h).wait()
        z_analysis(source, h, yy, r0.at[h, yy])

    def y_analysis(h, g):
        table = t1.at[zh]
        for at, wide in CHUNKS[g]:
            high, low = halves(r0[h, :, :, at : at + wide].reshape(128, wide))
            both = jnp.concatenate([high, low], 0)
            out = mm(table[:, 0:256], both) + mm(table[:, 256:384], high)
            vs[h, :, :, at : at + wide] = (out[:64] + swap(out[64:], 1.0)).reshape(8, 8, wide)

    def x_analysis_load(h):
        last = r1[h, :, :, 768:896].reshape(64, 128).astype(BF16)
        last = mm(last, spread[...]).astype(BF16)
        for x in range(6):
            at = 128 * x
            xb[64 * x : 64 * x + 64, 0:128] = r1[h, :, :, at : at + 128].reshape(64, 128).astype(BF16)
            xb[64 * x : 64 * x + 64, 128:256] = last[:, at : at + 128]

    def x_analysis_store(out, h, z):
        out = out[:64] + swap(out[64:], 1.0)
        rows = lax.broadcasted_iota(jnp.int32, (64, 128), 0) % 16
        last = jnp.where(slot_of((64, 128)) == rows, out[:, 128:], 0.0)
        last = jnp.sum(last.reshape(4, 16, 128), axis=1, keepdims=True)
        last = jnp.broadcast_to(last, (4, 16, 128)).reshape(64, 128)
        rsb[h, pl.ds(4 * z, 4)] = jnp.where(rows == 12, last, out[:, :128]).reshape(4, 16, 128)

    def x_analysis(h):
        mine = zh * 4 + zl
        for group in ((1, 2), (3, 4), (5, 6), (7, 8)):
            to = [lax.rem(mine + d, 8) for d in group]
            out = mm(jnp.concatenate([t2[z] for z in to], 0), xb[...])
            for n, d in enumerate(group):
                x_analysis_store(out[256 * n : 256 * n + 128] + out[256 * n + 128 : 256 * n + 256], h, to[n])
                for y in range(4 if d < 8 else 3):
                    c3(h, to[n], y if d < 8 else y_at(y + 1)).start()
        r3a[h, me] = rsb[h, me]

    def analysis(first, second, received):
        first()
        for h in range(2):
            for g in range(2):
                all_of_group(r0, h, 3, s1r, g)
                y_analysis(h, g)
                for d in range(1, 8):
                    c2(h, s_at(d), g).start()
            r1[h, s] = vs[h, s]
        for h in range(2):
            all_of(r1, h, 7, s2r)
            x_analysis_load(h)
            x_analysis(h)
        second()
        for h in range(2):
            all_modes(r3a, h, s3r)
            total = r3a[h, 0:4]
            for z in range(1, 8):
                total = total + r3a[h, 4 * z : 4 * z + 4]
            md[h] = total
            received(h)

    def analysis_end():
        for h in range(2):
            all_of(u, h, 3, s1s)
            all_of(vs, h, 7, s2s)
            all_modes(rsb, h, s3s)

    def x_synthesis_load(h):
        main = r3b[h]
        rows = lax.broadcasted_iota(jnp.int32, (512, 128), 0) % 16
        last = jnp.broadcast_to(main[:, 12:13], (32, 16, 128)).reshape(512, 128)
        xb2[:, 0:128] = main.reshape(512, 128).astype(BF16)
        xb2[:, 128:256] = jnp.where(slot_of((512, 128)) == rows, last, 0.0).astype(BF16)

    def x_synthesis(h):
        total = None
        for group in ((0, 1), (2, 3), (4, 5)):
            out = mm(jnp.concatenate([t2i[x] for x in group], 0), xb2[...])
            for n, x in enumerate(group):
                part = out[256 * n : 256 * n + 128] + out[256 * n + 128 : 256 * n + 256]
                part = part[:64] + swap(part[64:], -1.0)
                vs2[h, :, :, 128 * x : 128 * x + 128] = part[:, :128].reshape(8, 8, 128)
                high, low = halves(part[:, 128:])
                last = mm(high, gather[x]) + mm(low, gather[x])
                total = last if total is None else total + last
            if group == (2, 3):
                for d in range(1, 8):
                    k2(h, s_at(d), 0).start()
        vs2[h, :, :, 768:896] = total.reshape(8, 8, 128)
        for d in range(1, 8):
            k2(h, s_at(d), 1).start()

    def y_synthesis(h, g):
        table = t1i.at[zh]
        for at, wide in CHUNKS[g]:
            values = r1s[h, :, :, at : at + wide].reshape(64, wide)
            high, low = halves(jnp.concatenate([values, swap(values, -1.0)], 0))
            out = mm(table[:, 0:256], jnp.concatenate([high, low], 0)) + mm(table[:, 256:384], high)
            ys[h, :, :, at : at + wide] = out.reshape(4, 32, wide)

    def z_synthesis(h, fr, finish):
        slots = slot_of((32, 128))
        last = r0s[h, fr, :, 768:896]
        for x in range(6):
            zb[32 * x : 32 * x + 32, 0:128] = r0s[h, fr, :, 128 * x : 128 * x + 128].astype(BF16)
            zb[32 * x : 32 * x + 32, 128:256] = jnp.where(slots == x, last, 0.0).astype(BF16)

        def one(q):
            finish(fr, h, q, mm(zb[...], zz[q]).reshape(6, 32, 256))

        each(0, 4, one)

    def synthesis(meanwhile, finish, own, after):
        meanwhile()
        for h in range(2):
            all_modes(r3b, h, g3r)
            x_synthesis_load(h)
            x_synthesis(h)
            r1s[h, s] = vs2[h, s]
        for h in range(2):
            for g in range(2):
                all_of_group(r1s, h, 7, g2r, g)
                y_synthesis(h, g)
                for d in range(1, 4):
                    k1(h, y_at(d), g).start()
            r0s[h, yy] = ys[h, yy]
        for h in range(2):
            z_synthesis(h, yy, finish)
            own(h)
        for h in range(2):

            def one(d, h=h):
                fr = y_at(2 * d - 1 - lax.div(d, 3) * 3)
                whole(r0s.at[h, fr], g1r.at[h, fr])
                z_synthesis(h, fr, finish)
                after(h, fr)

            each(1, 4, one)
        for h in range(2):
            all_modes(r3b, h, g3s)
            all_of(vs2, h, 7, g2s)
            all_of(ys, h, 3, g1s)

    def channel_map(wide, source):
        rows = lax.broadcasted_iota(jnp.int32, (512, 512), 0) % 16
        columns = lax.broadcasted_iota(jnp.int32, (512, 512), 1) % 16
        full = lax.dot_general(
            wide.astype(BF16), a16[...], (((1,), (1,)), ((), ())), preferred_element_type=F32
        )
        kron[...] = jnp.where(rows == columns, full, 0.0).astype(BF16)

        def one(x):
            for at in (0, 16):
                block = source[:, :, :, x, at : at + 16, :].reshape(512, 256)
                out = mm(kron[...], block)
                lin[:, :, :, x, at : at + 16, :] = out.reshape(4, 2, 4, 16, 256)

        each(0, 6, one)

    def lanes(b):
        return pl.ds(pl.multiple_of(b * 128, 128), 128)

    def weights_in():
        loads[0].wait()

        def one(k):
            for part in range(2):
                for i in range(6):
                    w[part, k, 2 * i : 2 * i + 2, :] = w_in[part, k, i]
                w[part, k, 12:16, :] = jnp.zeros((4, 1024), F32)

        each(0, KZ, one)

    def weight_grad_out():
        def one(k):
            for part in range(2):
                for i in range(6):
                    wg_out[part, k, i] = wg[part, k, 2 * i : 2 * i + 2, :]

        each(0, KZ, one)

    def w_at(part, b):
        return w[part, :, :, lanes(b)].reshape(272, 128)

    def mix_one(h):
        def one(y):
            b = 2 * y + h
            modes = split_left(spread_rows(md[h, y]), e1[...])
            mexp[b] = modes
            real, imag = modes[:, :128], modes[:, 128:]
            w_real, w_imag = w_at(0, b), w_at(1, b)
            acc[:, :128] += w_real * real - w_imag * imag
            acc[:, 128:] += w_real * imag + w_imag * real

        each(0, 4, one)

    def spread_out(h, y):
        def one(z):
            pl.when(me != z * 4 + y)(lambda: k3(h, z % 4, z // 4, y).start())

        for z in range(8):
            one(z)

    def keep_own(h):
        r3b[h, me] = mq[h, yy]

    def mix_two():
        for h in range(2):
            for pair in range(2):
                out = split_left(acc[...], rr[h, pair])
                for n in range(2):
                    y = 2 * pair + n
                    mq[h, y] = gather_rows(out[:, 128 * n : 128 * n + 128])
                    spread_out(h, y)
            keep_own(h)

    def back_one(h):
        def one(y):
            gexp[...] += split_left(spread_rows(md[h, y]), e2[2 * y + h])

        each(0, 4, one)

    def back_two():
        for h in range(2):

            def two(y, h=h):
                b = 2 * y + h
                g_real, g_imag = gexp[:, :128], gexp[:, 128:]
                w_real, w_imag = w_at(0, b), w_at(1, b)
                real = w_real * g_real + w_imag * g_imag
                imag = w_real * g_imag - w_imag * g_real
                mq[h, y] = gather_rows(split_left(jnp.concatenate([real, imag], 1), r2[...]))
                spread_out(h, y)

            each(0, 4, two)
            keep_own(h)

    def weight_grad():
        def one(b):
            g_real, g_imag = gexp[:, :128], gexp[:, 128:]
            real, imag = mexp[b, :, :128], mexp[b, :, 128:]
            wg[0, :, :, lanes(b)] = (real * g_real + imag * g_imag).reshape(KZ, 16, 128)
            wg[1, :, :, lanes(b)] = (real * g_imag - imag * g_real).reshape(KZ, 16, 128)

        each(0, 8, one)
        weight_grad_out()

    def finish_pre(fr, h, q, spectral):
        pre = spectral + lin[fr, h, q] + bias[fr * 8 + h * 4 + q]
        pg[fr, h, q] = (cot[fr, h, q].astype(F32) * gelu_slope(pre)).astype(BF16)

    def finish_grad(fr, h, q, spectral):
        ig[fr, h, q] = (spectral + lin[fr, h, q]).astype(BF16)

    def second_own(h):
        z_analysis(pg, h, yy, r0.at[h, yy])

    def second_start(h, to):
        z_analysis(pg, h, to, u.at[h, to])
        for g in range(2):
            c1(h, to, g).start()

    def first_y_wait():
        channel_map(mm(a16[...], pw[...]), f)
        loads[1].wait()

    def first_z_wait():
        weights_in()
        acc[...] = jnp.zeros_like(acc)

    def second_z_wait():
        wide = lax.dot_general(a16[...], pw[...], (((1,), (1,)), ((), ())), preferred_element_type=F32)
        channel_map(wide, pg)
        gexp[...] = jnp.zeros_like(gexp)

    def wait_loads():
        for load in loads[3:]:
            load.wait()

    for h in range(2):
        analysis_start(f, h, h == 1)
    analysis(first_y_wait, first_z_wait, mix_one)
    loads[2].wait()
    mix_two()
    analysis_end()
    synthesis(wait_loads, finish_pre, second_own, second_start)
    analysis(lambda: None, second_z_wait, back_one)
    back_two()
    synthesis(weight_grad, finish_grad, lambda h: None, lambda h, fr: None)
    analysis_end()


def per_device(input_field, cotangent, spectral_weights, point_weight, point_bias):
    field_shape = (4, 2, 4, 6, 32, 256)
    w_shape = spectral_weights.shape
    tabs = {name: jnp.asarray(value) for name, value in TABLES.items()}
    vmem = pl.BlockSpec(memory_space=pltpu.VMEM)
    smem = pl.BlockSpec(memory_space=pltpu.SMEM)
    hbm = pl.BlockSpec(memory_space=pl.ANY)
    dma = pltpu.SemaphoreType.DMA
    scratch = [
        pltpu.VMEM((8, 256, 384), BF16),
        pltpu.VMEM((6, 256, 512), BF16),
        pltpu.VMEM((4, 256, 256), BF16),
        pltpu.VMEM((8, 128, 256), BF16),
        pltpu.VMEM((2, 2, 256, 256), BF16),
        pltpu.VMEM(field_shape, BF16),
        pltpu.VMEM(field_shape, BF16),
        pltpu.VMEM(w_shape, F32),
        pltpu.VMEM((2, KZ, 16, 1024), F32),
        pltpu.VMEM((2, KZ, 16, 1024), F32),
        pltpu.VMEM(field_shape, BF16),
        pltpu.VMEM(field_shape, F32),
        pltpu.VMEM((512, 512), BF16),
        pltpu.VMEM((2, 4, 32, 896), F32),
        pltpu.VMEM((2, 4, 32, 896), F32),
        pltpu.VMEM((2, 8, 8, 896), F32),
        pltpu.VMEM((2, 8, 8, 896), F32),
        pltpu.VMEM((2, 32, 16, 128), F32),
        pltpu.VMEM((2, 32, 16, 128), F32),
        pltpu.VMEM((2, 4, 16, 128), F32),
        pltpu.VMEM((384, 256), BF16),
        pltpu.VMEM((8, 272, 256), F32),
        pltpu.VMEM((272, 256), F32),
        pltpu.VMEM((272, 256), F32),
        pltpu.VMEM((2, 4, 16, 128), F32),
        pltpu.VMEM((2, 32, 16, 128), F32),
        pltpu.VMEM((512, 256), BF16),
        pltpu.VMEM((2, 8, 8, 896), F32),
        pltpu.VMEM((2, 8, 8, 896), F32),
        pltpu.VMEM((2, 4, 32, 896), F32),
        pltpu.VMEM((2, 4, 32, 896), F32),
        pltpu.VMEM((192, 256), BF16),
        dma((4, 2)),
        dma((7,)),
        dma((2,)), dma((2, 2)), dma((2,)), dma((2,)), dma((2,)), dma((2,)),
        dma((2,)), dma((2,)), dma((2,)), dma((2, 2)), dma((2,)), dma((2, 4)),
    ]
    ig, wg = pl.pallas_call(
        body,
        out_shape=(
            pltpu.VMEM(field_shape, BF16),
            pltpu.VMEM(w_shape, F32),
        ),
        in_specs=[vmem, smem] + [vmem] * len(IN_VMEM) + [hbm] * (len(IN_HBM) + 3),
        out_specs=(vmem, vmem),
        scratch_shapes=scratch,
        compiler_params=pltpu.CompilerParams(
            collective_id=0, has_side_effects=True, vmem_limit_bytes=50 * 1024 * 1024
        ),
        cost_estimate=pl.CostEstimate(flops=10**10, bytes_accessed=2 * 10**7, transcendentals=0),
    )(
        point_weight, point_bias,
        *[tabs[name] for name in IN_VMEM],
        *[tabs[name] for name in IN_HBM],
        input_field.reshape(field_shape), cotangent.reshape(field_shape), spectral_weights,
    )
    return (ig.reshape(input_field.shape), wg)


def solution(mesh):
    return jax.shard_map(
        per_device,
        mesh=mesh,
        in_specs=(
            P(None, None, "gx", "gy", None),
            P(None, None, "gx", "gy", None),
            P(None, None, "gy", "gx", None),
            P(),
            P(),
        ),
        out_specs=(P(None, None, "gx", "gy", None), P(None, None, "gy", "gx", None)),
        check_vma=False,
    )
```

```python
import math

import jax
import jax.numpy as jnp
import ml_dtypes
import numpy as np
from jax import lax
from jax.experimental import pallas as pl
from jax.experimental.pallas import tpu as pltpu
from jax.sharding import PartitionSpec as P

C = 32
NX = 192
NY = 256
NZ = 256
KX = 48
KY = 64
KZ = 17
SCALE = (NX * NY * NZ) ** (-0.5)
MESH = pl.DeviceIdType.MESH
F32 = jnp.float32
BF16 = jnp.bfloat16


def kept(count, number):
    half = number // 2
    return np.concatenate([np.arange(half), np.arange(half) + count - half])


def trig(points, freqs, count):
    angle = 2.0 * np.pi * ((points[:, None] * freqs[None, :]) % count) / count
    return np.cos(angle), np.sin(angle)


def hi_lo(table):
    table = np.asarray(table, np.float32)
    high = table.astype(ml_dtypes.bfloat16)
    low = (table - high.astype(np.float32)).astype(ml_dtypes.bfloat16)
    return high, low


def make_tables():
    z_cos, z_sin = trig(np.arange(NZ), np.arange(KZ), NZ)
    y_cos, y_sin = trig(np.arange(NY), kept(NY, KY), NY)
    x_cos, x_sin = trig(np.arange(NX), kept(NX, KX), NX)
    tabs = {}
    wz = np.zeros((4, NZ, 2, 2, 4, 16))
    zz = np.zeros((4, 2, 2, 4, 16, NZ))
    for c4 in range(4):
        wz[c4, :, 0, 0, c4, :] = z_cos[:, :16]
        wz[c4, :, 0, 1, c4, :] = -z_sin[:, :16]
        wz[c4, :, 1, 0, c4, :] = z_cos[:, 16:17]
        wz[c4, :, 1, 1, c4, :] = -z_sin[:, 16:17]
        zz[c4, 0, 0, c4] = z_cos[:, :16].T
        zz[c4, 0, 1, c4] = -z_sin[:, :16].T
        zz[c4, 1, 0, c4] = z_cos[:, 16:17].T
        zz[c4, 1, 1, c4] = -z_sin[:, 16:17].T
    tabs["wz"] = wz.reshape(4, NZ, 256).astype(np.float32).astype(ml_dtypes.bfloat16)
    tabs["zz"] = hi_lo(zz.reshape(4, 256, NZ))[0]
    s_at, zl_at, j_at = np.meshgrid(np.arange(8), np.arange(4), np.arange(2), indexing="ij")
    order = ((zl_at * 8 + s_at) * 2 + j_at).reshape(-1)
    yc = (y_cos * SCALE)[:, order].reshape(2, 128, 64)
    ys = (y_sin * SCALE)[:, order].reshape(2, 128, 64)
    inv = np.concatenate([yc, ys], 2)
    fwd = inv.transpose(0, 2, 1)
    tabs["t1"] = np.stack([np.concatenate([h, h, l], -1) for h, l in [hi_lo(fwd[0]), hi_lo(fwd[1])]])
    tabs["t1i"] = np.stack([np.concatenate([h, h, l], -1) for h, l in [hi_lo(inv[0]), hi_lo(inv[1])]])
    xt = np.stack([x_cos, x_sin]).reshape(2, 4, 8, 6, 2, 4, 6)
    t2 = np.zeros((4, 2, 4, 2, 4, 16, 6, 8, 8))
    for zl_to in range(4):
        for i in range(6):
            for j in range(2):
                block = xt[:, :, :, :, :, :, i]
                t2[:, :, zl_to, :, :, 2 * i + j, :, :, zl_to * 2 + j] = block.transpose(1, 4, 0, 5, 3, 2)
    fwd = t2.reshape(4, 8, 128, 384)
    tabs["t2"] = np.concatenate(hi_lo(fwd), 2)
    inv = t2.transpose(0, 6, 3, 7, 8, 1, 2, 4, 5).reshape(4, 6, 128, 512)
    tabs["t2i"] = np.concatenate(hi_lo(inv), 2)
    eye2, eye4 = np.eye(2), np.eye(4)
    ones16, ones32 = np.ones(16), np.ones(32)
    e1 = np.einsum("qr,cd,s,o->qcsrdo", eye2, eye4, ones16, ones32)
    tabs["e1"] = e1.reshape(128, 256)
    tabs["r2"] = e1.reshape(128, 256).T
    pick = np.eye(32).reshape(8, 4, 32)
    e2 = np.einsum("qr,bio,s,c->bqisrco", eye2, pick, ones16, np.ones(4)).reshape(8, 128, 256)
    tabs["e2"] = e2
    tabs["rr"] = e2.reshape(2, 2, 2, 128, 256).transpose(2, 0, 4, 1, 3).reshape(2, 2, 256, 256)
    slot = np.zeros((6, 16, 16))
    for x in range(6):
        slot[x, x, :] = 1.0
    spread = np.einsum("qr,cd,xst->xqcsrdt", eye2, eye4, slot).reshape(6, 128, 128)
    tabs["spread"] = spread.transpose(1, 0, 2).reshape(128, 768)
    tabs["gather"] = spread.transpose(0, 2, 1)
    tabs["a16"] = np.repeat(np.eye(32), 16, axis=0)
    for name in ("e1", "r2", "e2", "rr", "spread", "gather", "a16"):
        tabs[name] = tabs[name].astype(ml_dtypes.bfloat16)
    return tabs


TABLES = make_tables()
IN_VMEM = ("wz", "t1", "a16", "spread", "gather", "t1i", "e1", "r2")
IN_HBM = ("t2", "t2i", "zz", "e2", "rr")


def mm(left, right):
    return jnp.dot(left, right, preferred_element_type=F32)


def halves(values):
    high = values.astype(BF16)
    return high, (values - high.astype(F32)).astype(BF16)


def gelu_slope(values):
    size = jnp.abs(values)
    below = 1.0 + (0.3275911 / math.sqrt(2.0)) * size
    t = pl.reciprocal(below, approx=True)
    t = t * (2.0 - below * t)
    poly = t * (0.127414796 + t * (-0.142248368 + t * (0.7107068705 + t * (-0.7265760135 + t * 0.5307027145))))
    bell = jnp.exp2((-0.5 / math.log(2.0)) * (values * values))
    part = bell * (poly - (1.0 / math.sqrt(2.0 * math.pi)) * size)
    return jnp.where(values >= 0.0, 1.0 - part, part)


def swap(values, first):
    lane = lax.broadcasted_iota(jnp.int32, (values.shape[0], 128), 1)
    sign = jnp.where(lane < 64, first, -first)
    parts = [
        pltpu.roll(values[:, at : at + 128], 64, 1) * sign for at in range(0, values.shape[1], 128)
    ]
    return parts[0] if len(parts) == 1 else jnp.concatenate(parts, 1)


def slot_of(shape):
    return jnp.bitwise_and(lax.broadcasted_iota(jnp.int32, shape, len(shape) - 1), 15)


def row_of(shape):
    return jnp.bitwise_and(lax.broadcasted_iota(jnp.int32, shape, 0), 15)


def spread_rows(block):
    slots = slot_of((16, 128))
    rows = lax.broadcasted_iota(jnp.int32, (16, 128), 0)
    parts = [jnp.where(slots == k, block, 0.0) for k in range(16)]
    parts.append(jnp.where(slots == rows, jnp.broadcast_to(block[12:13], (16, 128)), 0.0))
    return jnp.concatenate(parts, 0)


def gather_rows(values):
    slots = slot_of((16, 128))
    rows = lax.broadcasted_iota(jnp.int32, (16, 128), 0)
    total = jnp.where(slots == 0, values[0:16], 0.0)
    for k in range(1, 16):
        total = total + jnp.where(slots == k, values[16 * k : 16 * k + 16], 0.0)
    last = jnp.sum(jnp.where(slots == rows, values[256:272], 0.0), axis=0, keepdims=True)
    return jnp.where(rows == 12, jnp.broadcast_to(last, (16, 128)), total)


def split_left(values, table):
    high, low = halves(values)
    out = mm(jnp.concatenate([high, low], 0), table)
    return out[: values.shape[0]] + out[values.shape[0] :]


GROUPS = ((0, 512), (512, 384))
CHUNKS = (((0, 256), (256, 256)), ((512, 256), (768, 128)))
ROWS = 13


def body(
    pw, bias, wz, t1, a16, spread, gather, t1i, e1, r2,
    t2_hbm, t2i_hbm, zz_hbm, e2_hbm, rr_hbm, f_hbm, cot_hbm, w_hbm,
    ig, wg_out,
    t2, t2i, zz, e2, rr, f, cot, w_in, w, wg, pg, lin, kron,
    u, r0, vs, r1, rsb, r3a, md, xb, mexp, gexp, acc,
    mq, r3b, xb2, vs2, r1s, ys, r0s, zb,
    f_sem, local_sem, s1s, s1r, s2s, s2r, s3s, s3r, g3s, g3r, g2s, g2r, g1s, g1r,
):
    gx = lax.axis_index("gx")
    gy = lax.axis_index("gy")
    zl, s = lax.div(gx, 8), lax.rem(gx, 8)
    zh, yy = lax.div(gy, 4), lax.rem(gy, 4)
    me = (zh * 4 + zl) * 4 + yy

    def y_id(to):
        return (gx, zh * 4 + to)

    def s_id(to):
        return (zl * 8 + to, gy)

    def m_id(zl_to, zh_to, y_to):
        return (zl_to * 8 + s, zh_to * 4 + y_to)

    def others(first):
        def one(z, y):
            pl.when(me != z * 4 + y)(lambda: first(z, z % 4, z // 4, y))

        for z in range(8):
            for y in range(4):
                one(z, y)

    def y_at(d):
        return lax.rem(yy + d, 4)

    def s_at(d):
        return lax.rem(s + d, 8)

    def each(low, high, fn):
        def step(d, carry):
            fn(d)
            return carry

        lax.fori_loop(low, high, step, 0)

    def f_load(to, h):
        return pltpu.make_async_copy(f_hbm.at[to, h], f.at[to, h], f_sem.at[to, h])

    for h in range(2):
        each(1, 5, lambda d, h=h: f_load(y_at(d), h).start())

    barrier = pltpu.get_barrier_semaphore()

    r3a[:, :, 8:16, :] = jnp.zeros((2, 32, 8, 128), F32)
    r3b[:, :, 8:16, :] = jnp.zeros((2, 32, 8, 128), F32)

    def greet(device):
        pl.semaphore_signal(barrier, inc=1, device_id=device, device_id_type=MESH)

    for d in range(1, 8):
        greet(s_id(s_at(d)))
    others(lambda z, zl_to, zh_to, y: greet(m_id(zl_to, zh_to, y)))

    loads = [
        pltpu.make_async_copy(src, dst, local_sem.at[n])
        for n, (src, dst) in enumerate(
            [
                (w_hbm, w_in),
                (t2_hbm.at[zl], t2),
                (rr_hbm, rr),
                (t2i_hbm.at[zl], t2i),
                (cot_hbm, cot),
                (zz_hbm, zz),
                (e2_hbm, e2),
            ]
        )
    ]
    for load in loads:
        load.start()
    def send(src, dst, send_sem, recv_sem, device):
        return pltpu.make_async_remote_copy(src, dst, send_sem, recv_sem, device_id=device, device_id_type=MESH)

    def c1(h, to, g):
        cells = pl.ds(*GROUPS[g])
        return send(u.at[h, to, :, cells], r0.at[h, yy, :, cells], s1s.at[h], s1r.at[h, g], y_id(to))

    def c2(h, to, g):
        cells = pl.ds(*GROUPS[g])
        return send(vs.at[h, to, :, cells], r1.at[h, s, :, cells], s2s.at[h], s2r.at[h], s_id(to))

    def c3(h, z, device_y):
        rows = pl.ds(0, ROWS)
        device = m_id(lax.rem(z, 4), lax.div(z, 4), device_y)
        return send(rsb.at[h, z * 4 + device_y, rows], r3a.at[h, me, rows], s3s.at[h], s3r.at[h], device)

    def k3(h, zl_to, zh_to, y):
        rows = pl.ds(0, ROWS)
        device = m_id(zl_to, zh_to, y)
        return send(mq.at[h, y, rows], r3b.at[h, me, rows], g3s.at[h], g3r.at[h], device)

    def k2(h, to, g):
        cells = pl.ds(*GROUPS[g])
        return send(vs2.at[h, to, :, cells], r1s.at[h, s, :, cells], g2s.at[h], g2r.at[h, g], s_id(to))

    def k1(h, to, g):
        cells = pl.ds(*GROUPS[g])
        return send(ys.at[h, to, :, cells], r0s.at[h, yy, :, cells], g1s.at[h], g1r.at[h, yy], y_id(to))

    def whole(part, sem):
        pltpu.make_async_copy(part, part, sem).wait()

    def all_of(buffer, h, count, sem):
        whole(buffer.at[h, pl.ds(0, count)], sem.at[h])

    def all_of_group(buffer, h, count, sem, g):
        whole(buffer.at[h, pl.ds(0, count), :, pl.ds(*GROUPS[g])], sem.at[h, g])

    def all_modes(buffer, h, sem):
        whole(buffer.at[h, pl.ds(0, 31), pl.ds(0, ROWS)], sem.at[h])

    def z_analysis(source, h, to, dest):
        total = None
        for q in range(4):
            term = mm(source[to, h, q].reshape(192, 256), wz[q])
            total = term if total is None else total + term
        slots = slot_of((32, 128))
        last = None
        for x in range(6):
            rows = total[32 * x : 32 * x + 32]
            dest[:, 128 * x : 128 * x + 128] = rows[:, :128]
            part = jnp.where(slots == x, rows[:, 128:], 0.0)
            last = part if last is None else last + part
        dest[:, 768:896] = last

    def analysis_start(source, h, greeted):
        def one(d):
            to = y_at(d)
            f_load(to, h).wait()
            z_analysis(source, h, to, u.at[h, to])
            if greeted:
                c1(h, to, 0).start()

        each(1, 4, one)
        if not greeted:
            pl.semaphore_wait(barrier, 38)
            for d in range(1, 4):
                c1(h, y_at(d), 0).start()
        for d in range(1, 4):
            c1(h, y_at(d), 1).start()
        f_load(yy, h).wait()
        z_analysis(source, h, yy, r0.at[h, yy])

    def y_analysis(h, g):
        table = t1.at[zh]
        for at, wide in CHUNKS[g]:
            high, low = halves(r0[h, :, :, at : at + wide].reshape(128, wide))
            both = jnp.concatenate([high, low], 0)
            out = mm(table[:, 0:256], both) + mm(table[:, 256:384], high)
            vs[h, :, :, at : at + wide] = (out[:64] + swap(out[64:], 1.0)).reshape(8, 8, wide)

    def x_analysis_load(h):
        last = r1[h, :, :, 768:896].reshape(64, 128).astype(BF16)
        last = mm(last, spread[...]).astype(BF16)
        for x in range(6):
            at = 128 * x
            xb[64 * x : 64 * x + 64, 0:128] = r1[h, :, :, at : at + 128].reshape(64, 128).astype(BF16)
            xb[64 * x : 64 * x + 64, 128:256] = last[:, at : at + 128]

    def x_analysis_store(out, h, z):
        out = out[:64] + swap(out[64:], 1.0)
        rows = row_of((64, 128))
        last = jnp.where(slot_of((64, 128)) == rows, out[:, 128:], 0.0)
        last = jnp.sum(last.reshape(4, 16, 128), axis=1, keepdims=True)
        last = jnp.broadcast_to(last, (4, 16, 128)).reshape(64, 128)
        rsb[h, pl.ds(4 * z, 4)] = jnp.where(rows == 12, last, out[:, :128]).reshape(4, 16, 128)

    def x_analysis(h):
        mine = zh * 4 + zl
        for group in ((1, 2), (3, 4), (5, 6), (7, 8)):
            to = [lax.rem(mine + d, 8) for d in group]
            out = mm(jnp.concatenate([t2[z] for z in to], 0), xb[...])
            for n, d in enumerate(group):
                x_analysis_store(out[256 * n : 256 * n + 128] + out[256 * n + 128 : 256 * n + 256], h, to[n])
                for y in range(4 if d < 8 else 3):
                    c3(h, to[n], y if d < 8 else y_at(y + 1)).start()
        r3a[h, me] = rsb[h, me]

    def analysis(first, second, received):
        first()
        for h in range(2):
            for g in range(2):
                all_of_group(r0, h, 3, s1r, g)
                y_analysis(h, g)
                for d in range(1, 8):
                    c2(h, s_at(d), g).start()
            r1[h, s] = vs[h, s]
        for h in range(2):
            all_of(r1, h, 7, s2r)
            x_analysis_load(h)
            x_analysis(h)
        second()
        for h in range(2):
            all_modes(r3a, h, s3r)
            total = r3a[h, 0:4]
            for z in range(1, 8):
                total = total + r3a[h, 4 * z : 4 * z + 4]
            md[h] = total
            received(h)

    def analysis_end():
        for h in range(2):
            all_of(u, h, 3, s1s)
            all_of(vs, h, 7, s2s)
            all_modes(rsb, h, s3s)

    def x_synthesis_load(h):
        main = r3b[h]
        rows = row_of((512, 128))
        last = jnp.broadcast_to(main[:, 12:13], (32, 16, 128)).reshape(512, 128)
        xb2[:, 0:128] = main.reshape(512, 128).astype(BF16)
        xb2[:, 128:256] = jnp.where(slot_of((512, 128)) == rows, last, 0.0).astype(BF16)

    def x_synthesis(h):
        total = None
        for group in ((0, 1), (2, 3), (4, 5)):
            out = mm(jnp.concatenate([t2i[x] for x in group], 0), xb2[...])
            for n, x in enumerate(group):
                part = out[256 * n : 256 * n + 128] + out[256 * n + 128 : 256 * n + 256]
                part = part[:64] + swap(part[64:], -1.0)
                vs2[h, :, :, 128 * x : 128 * x + 128] = part[:, :128].reshape(8, 8, 128)
                high, low = halves(part[:, 128:])
                last = mm(high, gather[x]) + mm(low, gather[x])
                total = last if total is None else total + last
            if group == (2, 3):
                for d in range(1, 8):
                    k2(h, s_at(d), 0).start()
        vs2[h, :, :, 768:896] = total.reshape(8, 8, 128)
        for d in range(1, 8):
            k2(h, s_at(d), 1).start()

    def y_synthesis(h, g):
        table = t1i.at[zh]
        for at, wide in CHUNKS[g]:
            values = r1s[h, :, :, at : at + wide].reshape(64, wide)
            high, low = halves(jnp.concatenate([values, swap(values, -1.0)], 0))
            out = mm(table[:, 0:256], jnp.concatenate([high, low], 0)) + mm(table[:, 256:384], high)
            ys[h, :, :, at : at + wide] = out.reshape(4, 32, wide)

    def z_synthesis(h, fr, finish):
        slots = slot_of((32, 128))
        last = r0s[h, fr, :, 768:896]
        for x in range(6):
            zb[32 * x : 32 * x + 32, 0:128] = r0s[h, fr, :, 128 * x : 128 * x + 128].astype(BF16)
            zb[32 * x : 32 * x + 32, 128:256] = jnp.where(slots == x, last, 0.0).astype(BF16)

        def one(q):
            finish(fr, h, q, mm(zb[...], zz[q]).reshape(6, 32, 256))

        each(0, 4, one)

    def synthesis(meanwhile, finish, own, after):
        meanwhile()
        for h in range(2):
            all_modes(r3b, h, g3r)
            x_synthesis_load(h)
            x_synthesis(h)
            r1s[h, s] = vs2[h, s]
            for g in range(2):
                all_of_group(r1s, h, 7, g2r, g)
                y_synthesis(h, g)
                for d in range(1, 4):
                    k1(h, y_at(d), g).start()
            r0s[h, yy] = ys[h, yy]
        for h in range(2):
            z_synthesis(h, yy, finish)
            own(h)
        for h in range(2):

            def one(d, h=h):
                fr = y_at(2 * d - 1 - lax.div(d, 3) * 3)
                whole(r0s.at[h, fr], g1r.at[h, fr])
                z_synthesis(h, fr, finish)
                after(h, fr)

            each(1, 4, one)
        for h in range(2):
            all_modes(r3b, h, g3s)
            all_of(vs2, h, 7, g2s)
            all_of(ys, h, 3, g1s)

    def channel_map(wide, source):
        rows = row_of((512, 512))
        columns = slot_of((512, 512))
        full = lax.dot_general(
            wide.astype(BF16), a16[...], (((1,), (1,)), ((), ())), preferred_element_type=F32
        )
        kron[...] = jnp.where(rows == columns, full, 0.0).astype(BF16)

        def one(x):
            for at in (0, 16):
                block = source[:, :, :, x, at : at + 16, :].reshape(512, 256)
                out = mm(kron[...], block)
                lin[:, :, :, x, at : at + 16, :] = out.reshape(4, 2, 4, 16, 256)

        each(0, 6, one)

    def lanes(b):
        return pl.ds(pl.multiple_of(b * 128, 128), 128)

    def weights_in():
        loads[0].wait()

        def one(k):
            for part in range(2):
                for i in range(6):
                    w[part, k, 2 * i : 2 * i + 2, :] = w_in[part, k, i]
                w[part, k, 12:16, :] = jnp.zeros((4, 1024), F32)

        each(0, KZ, one)

    def weight_grad_out():
        def one(k):
            for part in range(2):
                for i in range(6):
                    wg_out[part, k, i] = wg[part, k, 2 * i : 2 * i + 2, :]

        each(0, KZ, one)

    def w_at(part, b):
        return w[part, :, :, lanes(b)].reshape(272, 128)

    def mix_one(h):
        def one(y):
            b = 2 * y + h
            modes = split_left(spread_rows(md[h, y]), e1[...])
            mexp[b] = modes
            real, imag = modes[:, :128], modes[:, 128:]
            w_real, w_imag = w_at(0, b), w_at(1, b)
            acc[:, :128] += w_real * real - w_imag * imag
            acc[:, 128:] += w_real * imag + w_imag * real

        each(0, 4, one)

    def spread_out(h, y):
        def one(z):
            pl.when(me != z * 4 + y)(lambda: k3(h, z % 4, z // 4, y).start())

        for z in range(8):
            one(z)

    def keep_own(h):
        r3b[h, me] = mq[h, yy]

    def mix_two():
        for h in range(2):
            for pair in range(2):
                out = split_left(acc[...], rr[h, pair])
                for n in range(2):
                    y = 2 * pair + n
                    mq[h, y] = gather_rows(out[:, 128 * n : 128 * n + 128])
                    spread_out(h, y)
            keep_own(h)

    def back_one(h):
        def one(y):
            gexp[...] += split_left(spread_rows(md[h, y]), e2[2 * y + h])

        each(0, 4, one)

    def back_two():
        for h in range(2):

            def two(y, h=h):
                b = 2 * y + h
                g_real, g_imag = gexp[:, :128], gexp[:, 128:]
                w_real, w_imag = w_at(0, b), w_at(1, b)
                real = w_real * g_real + w_imag * g_imag
                imag = w_real * g_imag - w_imag * g_real
                mq[h, y] = gather_rows(split_left(jnp.concatenate([real, imag], 1), r2[...]))
                spread_out(h, y)

            each(0, 4, two)
            keep_own(h)

    def weight_grad():
        def one(b):
            g_real, g_imag = gexp[:, :128], gexp[:, 128:]
            real, imag = mexp[b, :, :128], mexp[b, :, 128:]
            wg[0, :, :, lanes(b)] = (real * g_real + imag * g_imag).reshape(KZ, 16, 128)
            wg[1, :, :, lanes(b)] = (real * g_imag - imag * g_real).reshape(KZ, 16, 128)

        each(0, 8, one)
        weight_grad_out()

    def finish_pre(fr, h, q, spectral):
        pre = spectral + lin[fr, h, q] + bias[fr * 8 + h * 4 + q]
        pg[fr, h, q] = (cot[fr, h, q].astype(F32) * gelu_slope(pre)).astype(BF16)

    def finish_grad(fr, h, q, spectral):
        ig[fr, h, q] = (spectral + lin[fr, h, q]).astype(BF16)

    def second_own(h):
        z_analysis(pg, h, yy, r0.at[h, yy])

    def second_start(h, to):
        z_analysis(pg, h, to, u.at[h, to])
        for g in range(2):
            c1(h, to, g).start()

    def first_y_wait():
        channel_map(mm(a16[...], pw[...]), f)
        loads[1].wait()

    def first_z_wait():
        weights_in()
        acc[...] = jnp.zeros_like(acc)

    def second_z_wait():
        wide = lax.dot_general(a16[...], pw[...], (((1,), (1,)), ((), ())), preferred_element_type=F32)
        channel_map(wide, pg)
        gexp[...] = jnp.zeros_like(gexp)

    def wait_loads():
        for load in loads[3:]:
            load.wait()

    for h in range(2):
        analysis_start(f, h, h == 1)
    analysis(first_y_wait, first_z_wait, mix_one)
    loads[2].wait()
    mix_two()
    analysis_end()
    synthesis(wait_loads, finish_pre, second_own, second_start)
    analysis(lambda: None, second_z_wait, back_one)
    back_two()
    synthesis(weight_grad, finish_grad, lambda h: None, lambda h, fr: None)
    analysis_end()


def per_device(input_field, cotangent, spectral_weights, point_weight, point_bias):
    field_shape = (4, 2, 4, 6, 32, 256)
    w_shape = spectral_weights.shape
    tabs = {name: jnp.asarray(value) for name, value in TABLES.items()}
    vmem = pl.BlockSpec(memory_space=pltpu.VMEM)
    smem = pl.BlockSpec(memory_space=pltpu.SMEM)
    hbm = pl.BlockSpec(memory_space=pl.ANY)
    dma = pltpu.SemaphoreType.DMA
    scratch = [
        pltpu.VMEM((8, 256, 384), BF16),
        pltpu.VMEM((6, 256, 512), BF16),
        pltpu.VMEM((4, 256, 256), BF16),
        pltpu.VMEM((8, 128, 256), BF16),
        pltpu.VMEM((2, 2, 256, 256), BF16),
        pltpu.VMEM(field_shape, BF16),
        pltpu.VMEM(field_shape, BF16),
        pltpu.VMEM(w_shape, F32),
        pltpu.VMEM((2, KZ, 16, 1024), F32),
        pltpu.VMEM((2, KZ, 16, 1024), F32),
        pltpu.VMEM(field_shape, BF16),
        pltpu.VMEM(field_shape, F32),
        pltpu.VMEM((512, 512), BF16),
        pltpu.VMEM((2, 4, 32, 896), F32),
        pltpu.VMEM((2, 4, 32, 896), F32),
        pltpu.VMEM((2, 8, 8, 896), F32),
        pltpu.VMEM((2, 8, 8, 896), F32),
        pltpu.VMEM((2, 32, 16, 128), F32),
        pltpu.VMEM((2, 32, 16, 128), F32),
        pltpu.VMEM((2, 4, 16, 128), F32),
        pltpu.VMEM((384, 256), BF16),
        pltpu.VMEM((8, 272, 256), F32),
        pltpu.VMEM((272, 256), F32),
        pltpu.VMEM((272, 256), F32),
        pltpu.VMEM((2, 4, 16, 128), F32),
        pltpu.VMEM((2, 32, 16, 128), F32),
        pltpu.VMEM((512, 256), BF16),
        pltpu.VMEM((2, 8, 8, 896), F32),
        pltpu.VMEM((2, 8, 8, 896), F32),
        pltpu.VMEM((2, 4, 32, 896), F32),
        pltpu.VMEM((2, 4, 32, 896), F32),
        pltpu.VMEM((192, 256), BF16),
        dma((4, 2)),
        dma((7,)),
        dma((2,)), dma((2, 2)), dma((2,)), dma((2,)), dma((2,)), dma((2,)),
        dma((2,)), dma((2,)), dma((2,)), dma((2, 2)), dma((2,)), dma((2, 4)),
    ]
    ig, wg = pl.pallas_call(
        body,
        out_shape=(
            pltpu.VMEM(field_shape, BF16),
            pltpu.VMEM(w_shape, F32),
        ),
        in_specs=[vmem, smem] + [vmem] * len(IN_VMEM) + [hbm] * (len(IN_HBM) + 3),
        out_specs=(vmem, vmem),
        scratch_shapes=scratch,
        compiler_params=pltpu.CompilerParams(
            collective_id=0, has_side_effects=True, vmem_limit_bytes=50 * 1024 * 1024
        ),
        cost_estimate=pl.CostEstimate(flops=10**10, bytes_accessed=2 * 10**7, transcendentals=0),
    )(
        point_weight, point_bias,
        *[tabs[name] for name in IN_VMEM],
        *[tabs[name] for name in IN_HBM],
        input_field.reshape(field_shape), cotangent.reshape(field_shape), spectral_weights,
    )
    return (ig.reshape(input_field.shape), wg)


def solution(mesh):
    return jax.shard_map(
        per_device,
        mesh=mesh,
        in_specs=(
            P(None, None, "gx", "gy", None),
            P(None, None, "gx", "gy", None),
            P(None, None, "gy", "gx", None),
            P(),
            P(),
        ),
        out_specs=(P(None, None, "gx", "gy", None), P(None, None, "gy", "gx", None)),
        check_vma=False,
    )
```

```python
import math

import jax
import jax.numpy as jnp
import ml_dtypes
import numpy as np
from jax import lax
from jax.experimental import pallas as pl
from jax.experimental.pallas import tpu as pltpu
from jax.sharding import PartitionSpec as P

C = 32
NX = 192
NY = 256
NZ = 256
KX = 48
KY = 64
KZ = 17
SCALE = (NX * NY * NZ) ** (-0.5)
MESH = pl.DeviceIdType.MESH
F32 = jnp.float32
BF16 = jnp.bfloat16


def kept(count, number):
    half = number // 2
    return np.concatenate([np.arange(half), np.arange(half) + count - half])


def trig(points, freqs, count):
    angle = 2.0 * np.pi * ((points[:, None] * freqs[None, :]) % count) / count
    return np.cos(angle), np.sin(angle)


def hi_lo(table):
    table = np.asarray(table, np.float32)
    high = table.astype(ml_dtypes.bfloat16)
    low = (table - high.astype(np.float32)).astype(ml_dtypes.bfloat16)
    return high, low


def make_tables():
    z_cos, z_sin = trig(np.arange(NZ), np.arange(KZ), NZ)
    y_cos, y_sin = trig(np.arange(NY), kept(NY, KY), NY)
    x_cos, x_sin = trig(np.arange(NX), kept(NX, KX), NX)
    tabs = {}
    wz = np.zeros((4, NZ, 2, 2, 4, 16))
    zz = np.zeros((4, 2, 2, 4, 16, NZ))
    for c4 in range(4):
        wz[c4, :, 0, 0, c4, :] = z_cos[:, :16]
        wz[c4, :, 0, 1, c4, :] = -z_sin[:, :16]
        wz[c4, :, 1, 0, c4, :] = z_cos[:, 16:17]
        wz[c4, :, 1, 1, c4, :] = -z_sin[:, 16:17]
        zz[c4, 0, 0, c4] = z_cos[:, :16].T
        zz[c4, 0, 1, c4] = -z_sin[:, :16].T
        zz[c4, 1, 0, c4] = z_cos[:, 16:17].T
        zz[c4, 1, 1, c4] = -z_sin[:, 16:17].T
    tabs["wz"] = wz.reshape(4 * NZ, 256).astype(np.float32).astype(ml_dtypes.bfloat16)
    tabs["zz"] = hi_lo(zz.reshape(4, 256, NZ))[0]
    s_at, zl_at, j_at = np.meshgrid(np.arange(8), np.arange(4), np.arange(2), indexing="ij")
    order = ((zl_at * 8 + s_at) * 2 + j_at).reshape(-1)
    yc = (y_cos * SCALE)[:, order].reshape(2, 128, 64)
    ys = (y_sin * SCALE)[:, order].reshape(2, 128, 64)
    inv = np.concatenate([yc, ys], 2)
    fwd = inv.transpose(0, 2, 1)
    tabs["t1"] = np.stack([np.concatenate([h, h, l], -1) for h, l in [hi_lo(fwd[0]), hi_lo(fwd[1])]])
    tabs["t1i"] = np.stack([np.concatenate([h, h, l], -1) for h, l in [hi_lo(inv[0]), hi_lo(inv[1])]])
    xt = np.stack([x_cos, x_sin]).reshape(2, 4, 8, 6, 2, 4, 6)
    t2 = np.zeros((4, 2, 4, 2, 4, 16, 6, 8, 8))
    for zl_to in range(4):
        for i in range(6):
            for j in range(2):
                block = xt[:, :, :, :, :, :, i]
                t2[:, :, zl_to, :, :, 2 * i + j, :, :, zl_to * 2 + j] = block.transpose(1, 4, 0, 5, 3, 2)
    fwd = t2.reshape(4, 8, 128, 384)
    tabs["t2"] = np.concatenate(hi_lo(fwd), 3)
    inv = t2.transpose(0, 6, 3, 7, 8, 1, 2, 4, 5).reshape(4, 6, 128, 512)
    tabs["t2i"] = np.concatenate(hi_lo(inv), 2)
    eye2, eye4 = np.eye(2), np.eye(4)
    ones16, ones32 = np.ones(16), np.ones(32)
    e1 = np.einsum("qr,cd,s,o->qcsrdo", eye2, eye4, ones16, ones32)
    tabs["e1"] = e1.reshape(128, 256)
    tabs["r2"] = e1.reshape(128, 256).T
    pick = np.eye(32).reshape(8, 4, 32)
    e2 = np.einsum("qr,bio,s,c->bqisrco", eye2, pick, ones16, np.ones(4)).reshape(8, 128, 256)
    tabs["e2"] = e2
    tabs["rr"] = e2.reshape(2, 2, 2, 128, 256).transpose(2, 0, 4, 1, 3).reshape(2, 2, 256, 256)
    slot = np.zeros((6, 16, 16))
    for x in range(6):
        slot[x, x, :] = 1.0
    spread = np.einsum("qr,cd,xst->xqcsrdt", eye2, eye4, slot).reshape(6, 128, 128)
    tabs["spread"] = spread.transpose(1, 0, 2).reshape(128, 768)
    tabs["gather"] = spread.transpose(0, 2, 1)
    tabs["a16"] = np.repeat(np.eye(32), 16, axis=0)
    for name in ("e1", "r2", "e2", "rr", "spread", "gather", "a16"):
        tabs[name] = tabs[name].astype(ml_dtypes.bfloat16)
    return tabs


TABLES = make_tables()
IN_VMEM = ("wz", "t1", "a16", "spread", "gather", "t1i", "e1", "r2")
IN_HBM = ("t2", "t2i", "zz", "e2", "rr")


def mm(left, right):
    return jnp.dot(left, right, preferred_element_type=F32)


def halves(values):
    high = values.astype(BF16)
    return high, (values - high.astype(F32)).astype(BF16)


def gelu_slope(values):
    size = jnp.abs(values)
    below = 1.0 + (0.3275911 / math.sqrt(2.0)) * size
    t = pl.reciprocal(below, approx=True)
    t = t * (2.0 - below * t)
    poly = t * (0.127414796 + t * (-0.142248368 + t * (0.7107068705 + t * (-0.7265760135 + t * 0.5307027145))))
    bell = jnp.exp2((-0.5 / math.log(2.0)) * (values * values))
    part = bell * (poly - (1.0 / math.sqrt(2.0 * math.pi)) * size)
    return jnp.where(values >= 0.0, 1.0 - part, part)


def swap(values, first):
    lane = lax.broadcasted_iota(jnp.int32, (values.shape[0], 128), 1)
    sign = jnp.where(lane < 64, first, -first)
    parts = [
        pltpu.roll(values[:, at : at + 128], 64, 1) * sign for at in range(0, values.shape[1], 128)
    ]
    return parts[0] if len(parts) == 1 else jnp.concatenate(parts, 1)


def slot_of(shape):
    return jnp.bitwise_and(lax.broadcasted_iota(jnp.int32, shape, len(shape) - 1), 15)


def row_of(shape):
    return jnp.bitwise_and(lax.broadcasted_iota(jnp.int32, shape, 0), 15)


def spread_rows(block):
    slots = slot_of((16, 128))
    rows = lax.broadcasted_iota(jnp.int32, (16, 128), 0)
    parts = [jnp.where(slots == k, block, 0.0) for k in range(16)]
    parts.append(jnp.where(slots == rows, jnp.broadcast_to(block[12:13], (16, 128)), 0.0))
    return jnp.concatenate(parts, 0)


def gather_rows(values):
    slots = slot_of((16, 128))
    rows = lax.broadcasted_iota(jnp.int32, (16, 128), 0)
    total = jnp.where(slots == 0, values[0:16], 0.0)
    for k in range(1, 16):
        total = total + jnp.where(slots == k, values[16 * k : 16 * k + 16], 0.0)
    last = jnp.sum(jnp.where(slots == rows, values[256:272], 0.0), axis=0, keepdims=True)
    return jnp.where(rows == 12, jnp.broadcast_to(last, (16, 128)), total)


def split_left(values, table):
    high, low = halves(values)
    out = mm(jnp.concatenate([high, low], 0), table)
    return out[: values.shape[0]] + out[values.shape[0] :]


GROUPS = ((0, 512), (512, 384))
CHUNKS = (((0, 256), (256, 256)), ((512, 256), (768, 128)))
ROWS = 13


def body(
    pw, bias, wz, t1, a16, spread, gather, t1i, e1, r2,
    t2_hbm, t2i_hbm, zz_hbm, e2_hbm, rr_hbm, f_hbm, cot_hbm, w_hbm,
    ig, wg_out,
    t2, t2i, zz, e2, rr, f, cot, w_in, w, wg, pg, lin, kron,
    u, r0, vs, r1, rsb, r3a, md, xb, mexp, gexp, acc,
    mq, r3b, xb2, vs2, r1s, ys, r0s, zb,
    f_sem, local_sem, s1s, s1r, s2s, s2r, s3s, s3r, g3s, g3r, g2s, g2r, g1s, g1r,
):
    gx = lax.axis_index("gx")
    gy = lax.axis_index("gy")
    zl, s = lax.div(gx, 8), lax.rem(gx, 8)
    zh, yy = lax.div(gy, 4), lax.rem(gy, 4)
    me = (zh * 4 + zl) * 4 + yy

    def y_id(to):
        return (gx, zh * 4 + to)

    def s_id(to):
        return (zl * 8 + to, gy)

    def m_id(zl_to, zh_to, y_to):
        return (zl_to * 8 + s, zh_to * 4 + y_to)

    def others(first):
        def one(z, y):
            pl.when(me != z * 4 + y)(lambda: first(z, z % 4, z // 4, y))

        for z in range(8):
            for y in range(4):
                one(z, y)

    def y_at(d):
        return lax.rem(yy + d, 4)

    def s_at(d):
        return lax.rem(s + d, 8)

    def each(low, high, fn):
        def step(d, carry):
            fn(d)
            return carry

        lax.fori_loop(low, high, step, 0)

    def f_load(to, h):
        return pltpu.make_async_copy(f_hbm.at[to, h], f.at[to, h], f_sem.at[to, h])

    for h in range(2):
        each(1, 5, lambda d, h=h: f_load(y_at(d), h).start())

    barrier = pltpu.get_barrier_semaphore()

    r3a[:, :, 8:16, :] = jnp.zeros((2, 32, 8, 128), F32)
    r3b[:, :, 8:16, :] = jnp.zeros((2, 32, 8, 128), F32)

    def greet(device):
        pl.semaphore_signal(barrier, inc=1, device_id=device, device_id_type=MESH)

    for d in range(1, 8):
        greet(s_id(s_at(d)))
    others(lambda z, zl_to, zh_to, y: greet(m_id(zl_to, zh_to, y)))

    loads = [
        pltpu.make_async_copy(src, dst, local_sem.at[n])
        for n, (src, dst) in enumerate(
            [
                (w_hbm, w_in),
                (t2_hbm.at[zl], t2),
                (rr_hbm, rr),
                (t2i_hbm.at[zl], t2i),
                (cot_hbm, cot),
                (zz_hbm, zz),
                (e2_hbm, e2),
            ]
        )
    ]
    for load in loads:
        load.start()
    def send(src, dst, send_sem, recv_sem, device):
        return pltpu.make_async_remote_copy(src, dst, send_sem, recv_sem, device_id=device, device_id_type=MESH)

    def c1(h, to, g):
        cells = pl.ds(*GROUPS[g])
        return send(u.at[h, to, :, cells], r0.at[h, yy, :, cells], s1s.at[h], s1r.at[h, g], y_id(to))

    def c2(h, to, g):
        cells = pl.ds(*GROUPS[g])
        return send(vs.at[h, to, :, cells], r1.at[h, s, :, cells], s2s.at[h], s2r.at[h], s_id(to))

    def c3(h, z, device_y):
        rows = pl.ds(0, ROWS)
        device = m_id(lax.rem(z, 4), lax.div(z, 4), device_y)
        return send(rsb.at[h, z * 4 + device_y, rows], r3a.at[h, me, rows], s3s.at[h], s3r.at[h], device)

    def k3(h, zl_to, zh_to, y):
        rows = pl.ds(0, ROWS)
        device = m_id(zl_to, zh_to, y)
        return send(mq.at[h, y, rows], r3b.at[h, me, rows], g3s.at[h], g3r.at[h], device)

    def k2(h, to, g):
        cells = pl.ds(*GROUPS[g])
        return send(vs2.at[h, to, :, cells], r1s.at[h, s, :, cells], g2s.at[h], g2r.at[h, g], s_id(to))

    def k1(h, to, g):
        cells = pl.ds(*GROUPS[g])
        return send(ys.at[h, to, :, cells], r0s.at[h, yy, :, cells], g1s.at[h], g1r.at[h, yy], y_id(to))

    def whole(part, sem):
        pltpu.make_async_copy(part, part, sem).wait()

    def all_of(buffer, h, count, sem):
        whole(buffer.at[h, pl.ds(0, count)], sem.at[h])

    def all_of_group(buffer, h, count, sem, g):
        whole(buffer.at[h, pl.ds(0, count), :, pl.ds(*GROUPS[g])], sem.at[h, g])

    def all_modes(buffer, h, sem):
        whole(buffer.at[h, pl.ds(0, 31), pl.ds(0, ROWS)], sem.at[h])

    def z_analysis(source, h, to, dest):
        total = mm(jnp.concatenate([source[to, h, q].reshape(192, 256) for q in range(4)], 1), wz[...])
        slots = slot_of((32, 128))
        last = None
        for x in range(6):
            rows = total[32 * x : 32 * x + 32]
            dest[:, 128 * x : 128 * x + 128] = rows[:, :128]
            part = jnp.where(slots == x, rows[:, 128:], 0.0)
            last = part if last is None else last + part
        dest[:, 768:896] = last

    def analysis_start(source, h, greeted):
        def one(d):
            to = y_at(d)
            f_load(to, h).wait()
            z_analysis(source, h, to, u.at[h, to])
            if greeted:
                c1(h, to, 0).start()

        each(1, 4, one)
        if not greeted:
            pl.semaphore_wait(barrier, 38)
            for d in range(1, 4):
                c1(h, y_at(d), 0).start()
        for d in range(1, 4):
            c1(h, y_at(d), 1).start()
        f_load(yy, h).wait()
        z_analysis(source, h, yy, r0.at[h, yy])

    def y_analysis(h, g):
        table = t1.at[zh]
        for at, wide in CHUNKS[g]:
            high, low = halves(r0[h, :, :, at : at + wide].reshape(128, wide))
            out = mm(table[...], jnp.concatenate([high, low, high], 0))
            vs[h, :, :, at : at + wide] = (out[:64] + swap(out[64:], 1.0)).reshape(8, 8, wide)

    def x_analysis_load(h):
        last = r1[h, :, :, 768:896].reshape(64, 128).astype(BF16)
        last = mm(last, spread[...]).astype(BF16)
        for x in range(6):
            at = 128 * x
            xb[64 * x : 64 * x + 64, 0:128] = r1[h, :, :, at : at + 128].reshape(64, 128).astype(BF16)
            xb[64 * x : 64 * x + 64, 128:256] = last[:, at : at + 128]

    def x_analysis_store(out, h, z):
        out = out[:64] + swap(out[64:], 1.0)
        rows = row_of((64, 128))
        last = jnp.where(slot_of((64, 128)) == rows, out[:, 128:], 0.0)
        last = jnp.sum(last.reshape(4, 16, 128), axis=1, keepdims=True)
        last = jnp.broadcast_to(last, (4, 16, 128)).reshape(64, 128)
        rsb[h, pl.ds(4 * z, 4)] = jnp.where(rows == 12, last, out[:, :128]).reshape(4, 16, 128)

    def x_analysis(h):
        mine = zh * 4 + zl
        for group in ((1, 2, 3, 4), (5, 6, 7, 8)):
            to = [lax.rem(mine + d, 8) for d in group]
            values = xb[...]
            out = mm(jnp.concatenate([t2[z] for z in to], 0), jnp.concatenate([values, values], 0))
            for n, d in enumerate(group):
                x_analysis_store(out[128 * n : 128 * n + 128], h, to[n])
                for y in range(4 if d < 8 else 3):
                    c3(h, to[n], y if d < 8 else y_at(y + 1)).start()
        r3a[h, me] = rsb[h, me]

    def analysis(first, second, received):
        first()
        for h in range(2):
            for g in range(2):
                all_of_group(r0, h, 3, s1r, g)
                y_analysis(h, g)
                for d in range(1, 8):
                    c2(h, s_at(d), g).start()
            r1[h, s] = vs[h, s]
        for h in range(2):
            all_of(r1, h, 7, s2r)
            x_analysis_load(h)
            x_analysis(h)
        second()
        for h in range(2):
            all_modes(r3a, h, s3r)
            total = r3a[h, 0:4]
            for z in range(1, 8):
                total = total + r3a[h, 4 * z : 4 * z + 4]
            md[h] = total
            received(h)

    def analysis_end():
        for h in range(2):
            all_of(u, h, 3, s1s)
            all_of(vs, h, 7, s2s)
            all_modes(rsb, h, s3s)

    def x_synthesis_load(h):
        main = r3b[h]
        rows = row_of((512, 128))
        last = jnp.broadcast_to(main[:, 12:13], (32, 16, 128)).reshape(512, 128)
        xb2[:, 0:128] = main.reshape(512, 128).astype(BF16)
        xb2[:, 128:256] = jnp.where(slot_of((512, 128)) == rows, last, 0.0).astype(BF16)

    def x_synthesis(h):
        total = None
        for group in ((0, 1), (2, 3), (4, 5)):
            out = mm(jnp.concatenate([t2i[x] for x in group], 0), xb2[...])
            for n, x in enumerate(group):
                part = out[256 * n : 256 * n + 128] + out[256 * n + 128 : 256 * n + 256]
                part = part[:64] + swap(part[64:], -1.0)
                vs2[h, :, :, 128 * x : 128 * x + 128] = part[:, :128].reshape(8, 8, 128)
                high, low = halves(part[:, 128:])
                last = mm(high, gather[x]) + mm(low, gather[x])
                total = last if total is None else total + last
            if group == (2, 3):
                for d in range(1, 8):
                    k2(h, s_at(d), 0).start()
        vs2[h, :, :, 768:896] = total.reshape(8, 8, 128)
        for d in range(1, 8):
            k2(h, s_at(d), 1).start()

    def y_synthesis(h, g):
        table = t1i.at[zh]
        for at, wide in CHUNKS[g]:
            values = r1s[h, :, :, at : at + wide].reshape(64, wide)
            high, low = halves(jnp.concatenate([values, swap(values, -1.0)], 0))
            out = mm(table[...], jnp.concatenate([high, low, high], 0))
            ys[h, :, :, at : at + wide] = out.reshape(4, 32, wide)

    def z_synthesis(h, fr, finish):
        slots = slot_of((32, 128))
        last = r0s[h, fr, :, 768:896]
        for x in range(6):
            zb[32 * x : 32 * x + 32, 0:128] = r0s[h, fr, :, 128 * x : 128 * x + 128].astype(BF16)
            zb[32 * x : 32 * x + 32, 128:256] = jnp.where(slots == x, last, 0.0).astype(BF16)

        def one(pair):
            for n in range(2):
                q = 2 * pair + n
                finish(fr, h, q, mm(zb[...], zz[q]).reshape(6, 32, 256))

        each(0, 2, one)

    def synthesis(meanwhile, finish, own, after):
        meanwhile()
        for h in range(2):
            all_modes(r3b, h, g3r)
            x_synthesis_load(h)
            x_synthesis(h)
            r1s[h, s] = vs2[h, s]
        for h in range(2):
            for g in range(2):
                all_of_group(r1s, h, 7, g2r, g)
                y_synthesis(h, g)
                for d in range(1, 4):
                    k1(h, y_at(d), g).start()
            r0s[h, yy] = ys[h, yy]
        for h in range(2):
            z_synthesis(h, yy, finish)
            own(h)
        for h in range(2):

            def one(d, h=h):
                fr = y_at(2 * d - 1 - lax.div(d, 3) * 3)
                whole(r0s.at[h, fr], g1r.at[h, fr])
                z_synthesis(h, fr, finish)
                after(h, fr)

            each(1, 4, one)
        for h in range(2):
            all_modes(r3b, h, g3s)
            all_of(vs2, h, 7, g2s)
            all_of(ys, h, 3, g1s)

    def channel_map(wide, source):
        rows = row_of((512, 512))
        columns = slot_of((512, 512))
        full = lax.dot_general(
            wide.astype(BF16), a16[...], (((1,), (1,)), ((), ())), preferred_element_type=F32
        )
        kron[...] = jnp.where(rows == columns, full, 0.0).astype(BF16)

        def one(x):
            for at in (0, 16):
                block = source[:, :, :, x, at : at + 16, :].reshape(512, 256)
                out = mm(kron[...], block)
                lin[:, :, :, x, at : at + 16, :] = out.reshape(4, 2, 4, 16, 256)

        each(0, 6, one)

    def lanes(b):
        return pl.ds(pl.multiple_of(b * 128, 128), 128)

    def weights_in():
        loads[0].wait()

        def one(k):
            for part in range(2):
                for i in range(6):
                    w[part, k, 2 * i : 2 * i + 2, :] = w_in[part, k, i]
                w[part, k, 12:16, :] = jnp.zeros((4, 1024), F32)

        each(0, KZ, one)

    def weight_grad_out():
        def one(k):
            for part in range(2):
                for i in range(6):
                    wg_out[part, k, i] = wg[part, k, 2 * i : 2 * i + 2, :]

        each(0, KZ, one)

    def w_at(part, b):
        return w[part, :, :, lanes(b)].reshape(272, 128)

    def mix_one(h):
        def one(y):
            b = 2 * y + h
            modes = split_left(spread_rows(md[h, y]), e1[...])
            mexp[b] = modes
            real, imag = modes[:, :128], modes[:, 128:]
            w_real, w_imag = w_at(0, b), w_at(1, b)
            acc[:, :128] += w_real * real - w_imag * imag
            acc[:, 128:] += w_real * imag + w_imag * real

        each(0, 4, one)

    def spread_out(h, y):
        def one(z):
            pl.when(me != z * 4 + y)(lambda: k3(h, z % 4, z // 4, y).start())

        for z in range(8):
            one(z)

    def keep_own(h):
        r3b[h, me] = mq[h, yy]

    def mix_two():
        for h in range(2):
            for pair in range(2):
                out = split_left(acc[...], rr[h, pair])
                for n in range(2):
                    y = 2 * pair + n
                    mq[h, y] = gather_rows(out[:, 128 * n : 128 * n + 128])
                    spread_out(h, y)
            keep_own(h)

    def back_one(h):
        def one(y):
            gexp[...] += split_left(spread_rows(md[h, y]), e2[2 * y + h])

        each(0, 4, one)

    def back_two():
        for h in range(2):

            def two(y, h=h):
                b = 2 * y + h
                g_real, g_imag = gexp[:, :128], gexp[:, 128:]
                w_real, w_imag = w_at(0, b), w_at(1, b)
                real = w_real * g_real + w_imag * g_imag
                imag = w_real * g_imag - w_imag * g_real
                mq[h, y] = gather_rows(split_left(jnp.concatenate([real, imag], 1), r2[...]))
                spread_out(h, y)

            each(0, 4, two)
            keep_own(h)

    def weight_grad():
        def one(b):
            g_real, g_imag = gexp[:, :128], gexp[:, 128:]
            real, imag = mexp[b, :, :128], mexp[b, :, 128:]
            wg[0, :, :, lanes(b)] = (real * g_real + imag * g_imag).reshape(KZ, 16, 128)
            wg[1, :, :, lanes(b)] = (real * g_imag - imag * g_real).reshape(KZ, 16, 128)

        each(0, 8, one)
        weight_grad_out()

    def finish_pre(fr, h, q, spectral):
        pre = spectral + lin[fr, h, q] + bias[fr * 8 + h * 4 + q]
        pg[fr, h, q] = (cot[fr, h, q].astype(F32) * gelu_slope(pre)).astype(BF16)

    def finish_grad(fr, h, q, spectral):
        ig[fr, h, q] = (spectral + lin[fr, h, q]).astype(BF16)

    def second_own(h):
        z_analysis(pg, h, yy, r0.at[h, yy])

    def second_start(h, to):
        z_analysis(pg, h, to, u.at[h, to])
        for g in range(2):
            c1(h, to, g).start()

    def first_y_wait():
        channel_map(mm(a16[...], pw[...]), f)
        loads[1].wait()

    def first_z_wait():
        weights_in()
        acc[...] = jnp.zeros_like(acc)

    def second_z_wait():
        wide = lax.dot_general(a16[...], pw[...], (((1,), (1,)), ((), ())), preferred_element_type=F32)
        channel_map(wide, pg)
        gexp[...] = jnp.zeros_like(gexp)

    def wait_loads():
        for load in loads[3:]:
            load.wait()

    for h in range(2):
        analysis_start(f, h, h == 1)
    analysis(first_y_wait, first_z_wait, mix_one)
    loads[2].wait()
    mix_two()
    analysis_end()
    synthesis(wait_loads, finish_pre, second_own, second_start)
    analysis(lambda: None, second_z_wait, back_one)
    back_two()
    synthesis(weight_grad, finish_grad, lambda h: None, lambda h, fr: None)
    analysis_end()


def per_device(input_field, cotangent, spectral_weights, point_weight, point_bias):
    field_shape = (4, 2, 4, 6, 32, 256)
    w_shape = spectral_weights.shape
    tabs = {name: jnp.asarray(value) for name, value in TABLES.items()}
    vmem = pl.BlockSpec(memory_space=pltpu.VMEM)
    smem = pl.BlockSpec(memory_space=pltpu.SMEM)
    hbm = pl.BlockSpec(memory_space=pl.ANY)
    dma = pltpu.SemaphoreType.DMA
    scratch = [
        pltpu.VMEM((8, 128, 768), BF16),
        pltpu.VMEM((6, 256, 512), BF16),
        pltpu.VMEM((4, 256, 256), BF16),
        pltpu.VMEM((8, 128, 256), BF16),
        pltpu.VMEM((2, 2, 256, 256), BF16),
        pltpu.VMEM(field_shape, BF16),
        pltpu.VMEM(field_shape, BF16),
        pltpu.VMEM(w_shape, F32),
        pltpu.VMEM((2, KZ, 16, 1024), F32),
        pltpu.VMEM((2, KZ, 16, 1024), F32),
        pltpu.VMEM(field_shape, BF16),
        pltpu.VMEM(field_shape, F32),
        pltpu.VMEM((512, 512), BF16),
        pltpu.VMEM((2, 4, 32, 896), F32),
        pltpu.VMEM((2, 4, 32, 896), F32),
        pltpu.VMEM((2, 8, 8, 896), F32),
        pltpu.VMEM((2, 8, 8, 896), F32),
        pltpu.VMEM((2, 32, 16, 128), F32),
        pltpu.VMEM((2, 32, 16, 128), F32),
        pltpu.VMEM((2, 4, 16, 128), F32),
        pltpu.VMEM((384, 256), BF16),
        pltpu.VMEM((8, 272, 256), F32),
        pltpu.VMEM((272, 256), F32),
        pltpu.VMEM((272, 256), F32),
        pltpu.VMEM((2, 4, 16, 128), F32),
        pltpu.VMEM((2, 32, 16, 128), F32),
        pltpu.VMEM((512, 256), BF16),
        pltpu.VMEM((2, 8, 8, 896), F32),
        pltpu.VMEM((2, 8, 8, 896), F32),
        pltpu.VMEM((2, 4, 32, 896), F32),
        pltpu.VMEM((2, 4, 32, 896), F32),
        pltpu.VMEM((192, 256), BF16),
        dma((4, 2)),
        dma((7,)),
        dma((2,)), dma((2, 2)), dma((2,)), dma((2,)), dma((2,)), dma((2,)),
        dma((2,)), dma((2,)), dma((2,)), dma((2, 2)), dma((2,)), dma((2, 4)),
    ]
    ig, wg = pl.pallas_call(
        body,
        out_shape=(
            pltpu.VMEM(field_shape, BF16),
            pltpu.VMEM(w_shape, F32),
        ),
        in_specs=[vmem, smem] + [vmem] * len(IN_VMEM) + [hbm] * (len(IN_HBM) + 3),
        out_specs=(vmem, vmem),
        scratch_shapes=scratch,
        compiler_params=pltpu.CompilerParams(
            collective_id=0, has_side_effects=True, vmem_limit_bytes=50 * 1024 * 1024
        ),
        cost_estimate=pl.CostEstimate(flops=10**10, bytes_accessed=2 * 10**7, transcendentals=0),
    )(
        point_weight, point_bias,
        *[tabs[name] for name in IN_VMEM],
        *[tabs[name] for name in IN_HBM],
        input_field.reshape(field_shape), cotangent.reshape(field_shape), spectral_weights,
    )
    return (ig.reshape(input_field.shape), wg)


def solution(mesh):
    return jax.shard_map(
        per_device,
        mesh=mesh,
        in_specs=(
            P(None, None, "gx", "gy", None),
            P(None, None, "gx", "gy", None),
            P(None, None, "gy", "gx", None),
            P(),
            P(),
        ),
        out_specs=(P(None, None, "gx", "gy", None), P(None, None, "gy", "gx", None)),
        check_vma=False,
    )
```

```python
import math

import jax
import jax.numpy as jnp
import ml_dtypes
import numpy as np
from jax import lax
from jax.experimental import pallas as pl
from jax.experimental.pallas import tpu as pltpu
from jax.sharding import PartitionSpec as P

C = 32
NX = 192
NY = 256
NZ = 256
KX = 48
KY = 64
KZ = 17
SCALE = (NX * NY * NZ) ** (-0.5)
MESH = pl.DeviceIdType.MESH
F32 = jnp.float32
BF16 = jnp.bfloat16


def kept(count, number):
    half = number // 2
    return np.concatenate([np.arange(half), np.arange(half) + count - half])


def trig(points, freqs, count):
    angle = 2.0 * np.pi * ((points[:, None] * freqs[None, :]) % count) / count
    return np.cos(angle), np.sin(angle)


def hi_lo(table):
    table = np.asarray(table, np.float32)
    high = table.astype(ml_dtypes.bfloat16)
    low = (table - high.astype(np.float32)).astype(ml_dtypes.bfloat16)
    return high, low


def make_tables():
    z_cos, z_sin = trig(np.arange(NZ), np.arange(KZ), NZ)
    y_cos, y_sin = trig(np.arange(NY), kept(NY, KY), NY)
    x_cos, x_sin = trig(np.arange(NX), kept(NX, KX), NX)
    tabs = {}
    wz = np.zeros((4, NZ, 2, 2, 4, 16))
    zz = np.zeros((4, 2, 2, 4, 16, NZ))
    for c4 in range(4):
        wz[c4, :, 0, 0, c4, :] = z_cos[:, :16]
        wz[c4, :, 0, 1, c4, :] = -z_sin[:, :16]
        wz[c4, :, 1, 0, c4, :] = z_cos[:, 16:17]
        wz[c4, :, 1, 1, c4, :] = -z_sin[:, 16:17]
        zz[c4, 0, 0, c4] = z_cos[:, :16].T
        zz[c4, 0, 1, c4] = -z_sin[:, :16].T
        zz[c4, 1, 0, c4] = z_cos[:, 16:17].T
        zz[c4, 1, 1, c4] = -z_sin[:, 16:17].T
    tabs["wz"] = wz.reshape(4 * NZ, 256).astype(np.float32).astype(ml_dtypes.bfloat16)
    tabs["zz"] = hi_lo(zz.reshape(4, 256, NZ))[0]
    s_at, zl_at, j_at = np.meshgrid(np.arange(8), np.arange(4), np.arange(2), indexing="ij")
    order = ((zl_at * 8 + s_at) * 2 + j_at).reshape(-1)
    yc = (y_cos * SCALE)[:, order].reshape(2, 128, 64)
    ys = (y_sin * SCALE)[:, order].reshape(2, 128, 64)
    inv = np.concatenate([yc, ys], 2)
    fwd = inv.transpose(0, 2, 1)
    tabs["t1"] = np.stack([np.concatenate([h, h, l], -1) for h, l in [hi_lo(fwd[0]), hi_lo(fwd[1])]])
    tabs["t1i"] = np.stack([np.concatenate([h, h, l], -1) for h, l in [hi_lo(inv[0]), hi_lo(inv[1])]])
    xt = np.stack([x_cos, x_sin]).reshape(2, 4, 8, 6, 2, 4, 6)
    t2 = np.zeros((4, 2, 4, 2, 4, 16, 6, 8, 8))
    for zl_to in range(4):
        for i in range(6):
            for j in range(2):
                block = xt[:, :, :, :, :, :, i]
                t2[:, :, zl_to, :, :, 2 * i + j, :, :, zl_to * 2 + j] = block.transpose(1, 4, 0, 5, 3, 2)
    fwd = t2.reshape(4, 8, 128, 384)
    tabs["t2"] = hi_lo(fwd)[0]
    inv = t2.transpose(0, 6, 3, 7, 8, 1, 2, 4, 5).reshape(4, 6, 128, 512)
    tabs["t2i"] = hi_lo(inv)[0]
    eye2, eye4 = np.eye(2), np.eye(4)
    ones16, ones32 = np.ones(16), np.ones(32)
    e1 = np.einsum("qr,cd,s,o->qcsrdo", eye2, eye4, ones16, ones32)
    tabs["e1"] = e1.reshape(128, 256)
    tabs["r2"] = e1.reshape(128, 256).T
    pick = np.eye(32).reshape(8, 4, 32)
    e2 = np.einsum("qr,bio,s,c->bqisrco", eye2, pick, ones16, np.ones(4)).reshape(8, 128, 256)
    tabs["e2"] = e2
    tabs["rr"] = e2.reshape(2, 2, 2, 128, 256).transpose(2, 0, 4, 1, 3).reshape(2, 2, 256, 256)
    slot = np.zeros((6, 16, 16))
    for x in range(6):
        slot[x, x, :] = 1.0
    spread = np.einsum("qr,cd,xst->xqcsrdt", eye2, eye4, slot).reshape(6, 128, 128)
    tabs["spread"] = spread.transpose(1, 0, 2).reshape(128, 768)
    tabs["gather"] = spread.transpose(0, 2, 1)
    tabs["a16"] = np.repeat(np.eye(32), 16, axis=0)
    for name in ("e1", "r2", "e2", "rr", "spread", "gather", "a16"):
        tabs[name] = tabs[name].astype(ml_dtypes.bfloat16)
    return tabs


TABLES = make_tables()
IN_VMEM = ("wz", "t1", "a16", "spread", "gather", "t1i", "e1", "r2")
IN_HBM = ("t2", "t2i", "zz", "e2", "rr")


def mm(left, right):
    return jnp.dot(left, right, preferred_element_type=F32)


def halves(values):
    high = values.astype(BF16)
    return high, (values - high.astype(F32)).astype(BF16)


def gelu_slope(values):
    size = jnp.abs(values)
    below = 1.0 + (0.3275911 / math.sqrt(2.0)) * size
    t = pl.reciprocal(below, approx=True)
    t = t * (2.0 - below * t)
    poly = t * (0.127414796 + t * (-0.142248368 + t * (0.7107068705 + t * (-0.7265760135 + t * 0.5307027145))))
    bell = jnp.exp2((-0.5 / math.log(2.0)) * (values * values))
    part = bell * (poly - (1.0 / math.sqrt(2.0 * math.pi)) * size)
    return jnp.where(values >= 0.0, 1.0 - part, part)


def swap(values, first):
    lane = lax.broadcasted_iota(jnp.int32, (values.shape[0], 128), 1)
    sign = jnp.where(lane < 64, first, -first)
    parts = [
        pltpu.roll(values[:, at : at + 128], 64, 1) * sign for at in range(0, values.shape[1], 128)
    ]
    return parts[0] if len(parts) == 1 else jnp.concatenate(parts, 1)


def slot_of(shape):
    return jnp.bitwise_and(lax.broadcasted_iota(jnp.int32, shape, len(shape) - 1), 15)


def row_of(shape):
    return jnp.bitwise_and(lax.broadcasted_iota(jnp.int32, shape, 0), 15)


def spread_rows(block):
    slots = slot_of((16, 128))
    rows = lax.broadcasted_iota(jnp.int32, (16, 128), 0)
    parts = [jnp.where(slots == k, block, 0.0) for k in range(16)]
    parts.append(jnp.where(slots == rows, jnp.broadcast_to(block[12:13], (16, 128)), 0.0))
    return jnp.concatenate(parts, 0)


def gather_rows(values):
    slots = slot_of((16, 128))
    rows = lax.broadcasted_iota(jnp.int32, (16, 128), 0)
    total = jnp.where(slots == 0, values[0:16], 0.0)
    for k in range(1, 16):
        total = total + jnp.where(slots == k, values[16 * k : 16 * k + 16], 0.0)
    last = jnp.sum(jnp.where(slots == rows, values[256:272], 0.0), axis=0, keepdims=True)
    return jnp.where(rows == 12, jnp.broadcast_to(last, (16, 128)), total)


def split_left(values, table):
    high, low = halves(values)
    out = mm(jnp.concatenate([high, low], 0), table)
    return out[: values.shape[0]] + out[values.shape[0] :]


GROUPS = ((0, 512), (512, 384))
CHUNKS = (((0, 256), (256, 256)), ((512, 256), (768, 128)))
ROWS = 13


def body(
    pw, bias, wz, t1, a16, spread, gather, t1i, e1, r2,
    t2_hbm, t2i_hbm, zz_hbm, e2_hbm, rr_hbm, f_hbm, cot_hbm, w_hbm,
    ig, wg_out,
    t2, t2i, zz, e2, rr, f, cot, w_in, w, wg, pg, lin, kron,
    u, r0, vs, r1, rsb, r3a, md, xb, mexp, gexp, acc,
    mq, r3b, xb2, vs2, r1s, ys, r0s, zb,
    f_sem, local_sem, s1s, s1r, s2s, s2r, s3s, s3r, g3s, g3r, g2s, g2r, g1s, g1r,
):
    gx = lax.axis_index("gx")
    gy = lax.axis_index("gy")
    zl, s = lax.div(gx, 8), lax.rem(gx, 8)
    zh, yy = lax.div(gy, 4), lax.rem(gy, 4)
    me = (zh * 4 + zl) * 4 + yy

    def y_id(to):
        return (gx, zh * 4 + to)

    def s_id(to):
        return (zl * 8 + to, gy)

    def m_id(zl_to, zh_to, y_to):
        return (zl_to * 8 + s, zh_to * 4 + y_to)

    def others(first):
        def one(z, y):
            pl.when(me != z * 4 + y)(lambda: first(z, z % 4, z // 4, y))

        for z in range(8):
            for y in range(4):
                one(z, y)

    def y_at(d):
        return lax.rem(yy + d, 4)

    def s_at(d):
        return lax.rem(s + d, 8)

    def each(low, high, fn):
        def step(d, carry):
            fn(d)
            return carry

        lax.fori_loop(low, high, step, 0)

    def f_load(to, h):
        return pltpu.make_async_copy(f_hbm.at[to, h], f.at[to, h], f_sem.at[to, h])

    for h in range(2):
        each(1, 5, lambda d, h=h: f_load(y_at(d), h).start())

    barrier = pltpu.get_barrier_semaphore()

    r3a[:, :, 8:16, :] = jnp.zeros((2, 32, 8, 128), F32)
    r3b[:, :, 8:16, :] = jnp.zeros((2, 32, 8, 128), F32)

    def greet(device):
        pl.semaphore_signal(barrier, inc=1, device_id=device, device_id_type=MESH)

    for d in range(1, 8):
        greet(s_id(s_at(d)))
    others(lambda z, zl_to, zh_to, y: greet(m_id(zl_to, zh_to, y)))

    loads = [
        pltpu.make_async_copy(src, dst, local_sem.at[n])
        for n, (src, dst) in enumerate(
            [
                (w_hbm, w_in),
                (t2_hbm.at[zl], t2),
                (rr_hbm, rr),
                (t2i_hbm.at[zl], t2i),
                (cot_hbm, cot),
                (zz_hbm, zz),
                (e2_hbm, e2),
            ]
        )
    ]
    for load in loads:
        load.start()
    def send(src, dst, send_sem, recv_sem, device):
        return pltpu.make_async_remote_copy(src, dst, send_sem, recv_sem, device_id=device, device_id_type=MESH)

    def c1(h, to, g):
        cells = pl.ds(*GROUPS[g])
        return send(u.at[h, to, :, cells], r0.at[h, yy, :, cells], s1s.at[h], s1r.at[h, g], y_id(to))

    def c2(h, to, g):
        cells = pl.ds(*GROUPS[g])
        return send(vs.at[h, to, :, cells], r1.at[h, s, :, cells], s2s.at[h], s2r.at[h], s_id(to))

    def c3(h, z, device_y):
        rows = pl.ds(0, ROWS)
        device = m_id(lax.rem(z, 4), lax.div(z, 4), device_y)
        return send(rsb.at[h, z * 4 + device_y, rows], r3a.at[h, me, rows], s3s.at[h], s3r.at[h], device)

    def k3(h, zl_to, zh_to, y):
        rows = pl.ds(0, ROWS)
        device = m_id(zl_to, zh_to, y)
        return send(mq.at[h, y, rows], r3b.at[h, me, rows], g3s.at[h], g3r.at[h], device)

    def k2(h, to, g):
        cells = pl.ds(*GROUPS[g])
        return send(vs2.at[h, to, :, cells], r1s.at[h, s, :, cells], g2s.at[h], g2r.at[h, g], s_id(to))

    def k1(h, to, g):
        cells = pl.ds(*GROUPS[g])
        return send(ys.at[h, to, :, cells], r0s.at[h, yy, :, cells], g1s.at[h], g1r.at[h, yy], y_id(to))

    def whole(part, sem):
        pltpu.make_async_copy(part, part, sem).wait()

    def all_of(buffer, h, count, sem):
        whole(buffer.at[h, pl.ds(0, count)], sem.at[h])

    def all_of_group(buffer, h, count, sem, g):
        whole(buffer.at[h, pl.ds(0, count), :, pl.ds(*GROUPS[g])], sem.at[h, g])

    def all_modes(buffer, h, sem):
        whole(buffer.at[h, pl.ds(0, 31), pl.ds(0, ROWS)], sem.at[h])

    def z_analysis(source, h, to, dest):
        total = mm(jnp.concatenate([source[to, h, q].reshape(192, 256) for q in range(4)], 1), wz[...])
        slots = slot_of((32, 128))
        last = None
        for x in range(6):
            rows = total[32 * x : 32 * x + 32]
            dest[:, 128 * x : 128 * x + 128] = rows[:, :128]
            part = jnp.where(slots == x, rows[:, 128:], 0.0)
            last = part if last is None else last + part
        dest[:, 768:896] = last

    def analysis_start(source, h, greeted):
        def one(d):
            to = y_at(d)
            f_load(to, h).wait()
            z_analysis(source, h, to, u.at[h, to])
            if greeted:
                c1(h, to, 0).start()

        each(1, 4, one)
        if not greeted:
            pl.semaphore_wait(barrier, 38)
            for d in range(1, 4):
                c1(h, y_at(d), 0).start()
        for d in range(1, 4):
            c1(h, y_at(d), 1).start()
        f_load(yy, h).wait()
        z_analysis(source, h, yy, r0.at[h, yy])

    def y_analysis(h, g):
        table = t1.at[zh]
        for at, wide in CHUNKS[g]:
            high, low = halves(r0[h, :, :, at : at + wide].reshape(128, wide))
            out = mm(table[...], jnp.concatenate([high, low, high], 0))
            vs[h, :, :, at : at + wide] = (out[:64] + swap(out[64:], 1.0)).reshape(8, 8, wide)

    def x_analysis_load(h):
        last = r1[h, :, :, 768:896].reshape(64, 128).astype(BF16)
        last = mm(last, spread[...]).astype(BF16)
        for x in range(6):
            at = 128 * x
            xb[64 * x : 64 * x + 64, 0:128] = r1[h, :, :, at : at + 128].reshape(64, 128).astype(BF16)
            xb[64 * x : 64 * x + 64, 128:256] = last[:, at : at + 128]

    def x_analysis_store(out, h, z):
        out = out[:64] + swap(out[64:], 1.0)
        rows = row_of((64, 128))
        last = jnp.where(slot_of((64, 128)) == rows, out[:, 128:], 0.0)
        last = jnp.sum(last.reshape(4, 16, 128), axis=1, keepdims=True)
        last = jnp.broadcast_to(last, (4, 16, 128)).reshape(64, 128)
        rsb[h, pl.ds(4 * z, 4)] = jnp.where(rows == 12, last, out[:, :128]).reshape(4, 16, 128)

    def x_analysis(h):
        mine = zh * 4 + zl
        for group in ((1, 2, 3, 4), (5, 6, 7, 8)):
            to = [lax.rem(mine + d, 8) for d in group]
            out = mm(jnp.concatenate([t2[z] for z in to], 0), xb[...])
            for n, d in enumerate(group):
                x_analysis_store(out[128 * n : 128 * n + 128], h, to[n])
                for y in range(4 if d < 8 else 3):
                    c3(h, to[n], y if d < 8 else y_at(y + 1)).start()
        r3a[h, me] = rsb[h, me]

    def analysis(first, middle, second, received):
        first()
        for h in range(2):
            for g in range(2):
                all_of_group(r0, h, 3, s1r, g)
                y_analysis(h, g)
                for d in range(1, 8):
                    c2(h, s_at(d), g).start()
            r1[h, s] = vs[h, s]
        middle()
        for h in range(2):
            all_of(r1, h, 7, s2r)
            x_analysis_load(h)
            x_analysis(h)
        second()
        for h in range(2):
            all_modes(r3a, h, s3r)
            total = r3a[h, 0:4]
            for z in range(1, 8):
                total = total + r3a[h, 4 * z : 4 * z + 4]
            md[h] = total
            received(h)

    def analysis_end():
        for h in range(2):
            all_of(u, h, 3, s1s)
            all_of(vs, h, 7, s2s)
            all_modes(rsb, h, s3s)

    def x_synthesis_load(h):
        main = r3b[h]
        rows = row_of((512, 128))
        last = jnp.broadcast_to(main[:, 12:13], (32, 16, 128)).reshape(512, 128)
        xb2[:, 0:128] = main.reshape(512, 128).astype(BF16)
        xb2[:, 128:256] = jnp.where(slot_of((512, 128)) == rows, last, 0.0).astype(BF16)

    def x_synthesis(h):
        total = None
        for group in ((0, 1), (2, 3), (4, 5)):
            out = mm(jnp.concatenate([t2i[x] for x in group], 0), xb2[...])
            for n, x in enumerate(group):
                part = out[128 * n : 128 * n + 128]
                part = part[:64] + swap(part[64:], -1.0)
                vs2[h, :, :, 128 * x : 128 * x + 128] = part[:, :128].reshape(8, 8, 128)
                high, low = halves(part[:, 128:])
                last = mm(high, gather[x]) + mm(low, gather[x])
                total = last if total is None else total + last
            if group == (2, 3):
                for d in range(1, 8):
                    k2(h, s_at(d), 0).start()
        vs2[h, :, :, 768:896] = total.reshape(8, 8, 128)
        for d in range(1, 8):
            k2(h, s_at(d), 1).start()

    def y_synthesis(h, g):
        table = t1i.at[zh]
        for at, wide in CHUNKS[g]:
            values = r1s[h, :, :, at : at + wide].reshape(64, wide)
            high, low = halves(jnp.concatenate([values, swap(values, -1.0)], 0))
            out = mm(table[...], jnp.concatenate([high, low, high], 0))
            ys[h, :, :, at : at + wide] = out.reshape(4, 32, wide)

    def z_synthesis(h, fr, finish):
        slots = slot_of((32, 128))
        last = r0s[h, fr, :, 768:896]
        for x in range(6):
            zb[32 * x : 32 * x + 32, 0:128] = r0s[h, fr, :, 128 * x : 128 * x + 128].astype(BF16)
            zb[32 * x : 32 * x + 32, 128:256] = jnp.where(slots == x, last, 0.0).astype(BF16)

        def one(pair):
            for n in range(2):
                q = 2 * pair + n
                finish(fr, h, q, mm(zb[...], zz[q]).reshape(6, 32, 256))

        each(0, 2, one)

    def synthesis(meanwhile, finish, own, after):
        meanwhile()
        for h in range(2):
            all_modes(r3b, h, g3r)
            x_synthesis_load(h)
            x_synthesis(h)
            r1s[h, s] = vs2[h, s]
        for h in range(2):
            for g in range(2):
                all_of_group(r1s, h, 7, g2r, g)
                y_synthesis(h, g)
                for d in range(1, 4):
                    k1(h, y_at(d), g).start()
            r0s[h, yy] = ys[h, yy]
        for h in range(2):
            z_synthesis(h, yy, finish)
            own(h)
        for h in range(2):

            def one(d, h=h):
                fr = y_at(2 * d - 1 - lax.div(d, 3) * 3)
                whole(r0s.at[h, fr], g1r.at[h, fr])
                z_synthesis(h, fr, finish)
                after(h, fr)

            each(1, 4, one)
        for h in range(2):
            all_modes(r3b, h, g3s)
            all_of(vs2, h, 7, g2s)
            all_of(ys, h, 3, g1s)

    def channel_matrix(wide):
        rows = row_of((512, 512))
        columns = slot_of((512, 512))
        full = lax.dot_general(
            wide.astype(BF16), a16[...], (((1,), (1,)), ((), ())), preferred_element_type=F32
        )
        kron[...] = jnp.where(rows == columns, full, 0.0).astype(BF16)

    def channel_map(source, low, high):
        def one(x):
            for at in (0, 16):
                block = source[:, :, :, x, at : at + 16, :].reshape(512, 256)
                out = mm(kron[...], block)
                lin[:, :, :, x, at : at + 16, :] = out.reshape(4, 2, 4, 16, 256)

        each(low, high, one)

    def lanes(b):
        return pl.ds(pl.multiple_of(b * 128, 128), 128)

    def weights_in():
        loads[0].wait()

        def one(k):
            for part in range(2):
                for i in range(6):
                    w[part, k, 2 * i : 2 * i + 2, :] = w_in[part, k, i]
                w[part, k, 12:16, :] = jnp.zeros((4, 1024), F32)

        each(0, KZ, one)

    def weight_grad_out():
        def one(k):
            for part in range(2):
                for i in range(6):
                    wg_out[part, k, i] = wg[part, k, 2 * i : 2 * i + 2, :]

        each(0, KZ, one)

    def w_at(part, b):
        return w[part, :, :, lanes(b)].reshape(272, 128)

    def mix_one(h):
        def one(y):
            b = 2 * y + h
            modes = split_left(spread_rows(md[h, y]), e1[...])
            mexp[b] = modes
            real, imag = modes[:, :128], modes[:, 128:]
            w_real, w_imag = w_at(0, b), w_at(1, b)
            acc[:, :128] += w_real * real - w_imag * imag
            acc[:, 128:] += w_real * imag + w_imag * real

        each(0, 4, one)

    def spread_out(h, y):
        def one(z):
            pl.when(me != z * 4 + y)(lambda: k3(h, z % 4, z // 4, y).start())

        for z in range(8):
            one(z)

    def keep_own(h):
        r3b[h, me] = mq[h, yy]

    def mix_two():
        for h in range(2):
            for pair in range(2):
                out = split_left(acc[...], rr[h, pair])
                for n in range(2):
                    y = 2 * pair + n
                    mq[h, y] = gather_rows(out[:, 128 * n : 128 * n + 128])
                    spread_out(h, y)
            keep_own(h)

    def back_one(h):
        def one(y):
            gexp[...] += split_left(spread_rows(md[h, y]), e2[2 * y + h])

        each(0, 4, one)

    def back_two():
        for h in range(2):

            def two(y, h=h):
                b = 2 * y + h
                g_real, g_imag = gexp[:, :128], gexp[:, 128:]
                w_real, w_imag = w_at(0, b), w_at(1, b)
                real = w_real * g_real + w_imag * g_imag
                imag = w_real * g_imag - w_imag * g_real
                mq[h, y] = gather_rows(split_left(jnp.concatenate([real, imag], 1), r2[...]))
                spread_out(h, y)

            each(0, 4, two)
            keep_own(h)

    def weight_grad():
        def one(b):
            g_real, g_imag = gexp[:, :128], gexp[:, 128:]
            real, imag = mexp[b, :, :128], mexp[b, :, 128:]
            wg[0, :, :, lanes(b)] = (real * g_real + imag * g_imag).reshape(KZ, 16, 128)
            wg[1, :, :, lanes(b)] = (real * g_imag - imag * g_real).reshape(KZ, 16, 128)

        each(0, 8, one)
        weight_grad_out()

    def finish_pre(fr, h, q, spectral):
        pre = spectral + lin[fr, h, q] + bias[fr * 8 + h * 4 + q]
        pg[fr, h, q] = (cot[fr, h, q].astype(F32) * gelu_slope(pre)).astype(BF16)

    def finish_grad(fr, h, q, spectral):
        ig[fr, h, q] = (spectral + lin[fr, h, q]).astype(BF16)

    def second_own(h):
        z_analysis(pg, h, yy, r0.at[h, yy])

    def second_start(h, to):
        z_analysis(pg, h, to, u.at[h, to])
        for g in range(2):
            c1(h, to, g).start()

    def first_y_wait():
        weights_in()
        acc[...] = jnp.zeros_like(acc)
        loads[1].wait()

    def second_x_wait():
        wide = lax.dot_general(a16[...], pw[...], (((1,), (1,)), ((), ())), preferred_element_type=F32)
        channel_matrix(wide)
        channel_map(pg, 0, 3)

    def second_z_wait():
        channel_map(pg, 3, 6)
        gexp[...] = jnp.zeros_like(gexp)

    def first_gather_wait():
        channel_matrix(mm(a16[...], pw[...]))
        channel_map(f, 0, 6)
        for load in loads[3:]:
            load.wait()

    for h in range(2):
        analysis_start(f, h, h == 1)
    analysis(first_y_wait, lambda: None, lambda: None, mix_one)
    loads[2].wait()
    mix_two()
    analysis_end()
    synthesis(first_gather_wait, finish_pre, second_own, second_start)
    analysis(lambda: None, second_x_wait, second_z_wait, back_one)
    back_two()
    synthesis(weight_grad, finish_grad, lambda h: None, lambda h, fr: None)
    analysis_end()


def per_device(input_field, cotangent, spectral_weights, point_weight, point_bias):
    field_shape = (4, 2, 4, 6, 32, 256)
    w_shape = spectral_weights.shape
    tabs = {name: jnp.asarray(value) for name, value in TABLES.items()}
    vmem = pl.BlockSpec(memory_space=pltpu.VMEM)
    smem = pl.BlockSpec(memory_space=pltpu.SMEM)
    hbm = pl.BlockSpec(memory_space=pl.ANY)
    dma = pltpu.SemaphoreType.DMA
    scratch = [
        pltpu.VMEM((8, 128, 384), BF16),
        pltpu.VMEM((6, 128, 512), BF16),
        pltpu.VMEM((4, 256, 256), BF16),
        pltpu.VMEM((8, 128, 256), BF16),
        pltpu.VMEM((2, 2, 256, 256), BF16),
        pltpu.VMEM(field_shape, BF16),
        pltpu.VMEM(field_shape, BF16),
        pltpu.VMEM(w_shape, F32),
        pltpu.VMEM((2, KZ, 16, 1024), F32),
        pltpu.VMEM((2, KZ, 16, 1024), F32),
        pltpu.VMEM(field_shape, BF16),
        pltpu.VMEM(field_shape, F32),
        pltpu.VMEM((512, 512), BF16),
        pltpu.VMEM((2, 4, 32, 896), F32),
        pltpu.VMEM((2, 4, 32, 896), F32),
        pltpu.VMEM((2, 8, 8, 896), F32),
        pltpu.VMEM((2, 8, 8, 896), F32),
        pltpu.VMEM((2, 32, 16, 128), F32),
        pltpu.VMEM((2, 32, 16, 128), F32),
        pltpu.VMEM((2, 4, 16, 128), F32),
        pltpu.VMEM((384, 256), BF16),
        pltpu.VMEM((8, 272, 256), F32),
        pltpu.VMEM((272, 256), F32),
        pltpu.VMEM((272, 256), F32),
        pltpu.VMEM((2, 4, 16, 128), F32),
        pltpu.VMEM((2, 32, 16, 128), F32),
        pltpu.VMEM((512, 256), BF16),
        pltpu.VMEM((2, 8, 8, 896), F32),
        pltpu.VMEM((2, 8, 8, 896), F32),
        pltpu.VMEM((2, 4, 32, 896), F32),
        pltpu.VMEM((2, 4, 32, 896), F32),
        pltpu.VMEM((192, 256), BF16),
        dma((4, 2)),
        dma((7,)),
        dma((2,)), dma((2, 2)), dma((2,)), dma((2,)), dma((2,)), dma((2,)),
        dma((2,)), dma((2,)), dma((2,)), dma((2, 2)), dma((2,)), dma((2, 4)),
    ]
    ig, wg = pl.pallas_call(
        body,
        out_shape=(
            pltpu.VMEM(field_shape, BF16),
            pltpu.VMEM(w_shape, F32),
        ),
        in_specs=[vmem, smem] + [vmem] * len(IN_VMEM) + [hbm] * (len(IN_HBM) + 3),
        out_specs=(vmem, vmem),
        scratch_shapes=scratch,
        compiler_params=pltpu.CompilerParams(
            collective_id=0, has_side_effects=True, vmem_limit_bytes=50 * 1024 * 1024
        ),
        cost_estimate=pl.CostEstimate(flops=10**10, bytes_accessed=2 * 10**7, transcendentals=0),
    )(
        point_weight, point_bias,
        *[tabs[name] for name in IN_VMEM],
        *[tabs[name] for name in IN_HBM],
        input_field.reshape(field_shape), cotangent.reshape(field_shape), spectral_weights,
    )
    return (ig.reshape(input_field.shape), wg)


def solution(mesh):
    return jax.shard_map(
        per_device,
        mesh=mesh,
        in_specs=(
            P(None, None, "gx", "gy", None),
            P(None, None, "gx", "gy", None),
            P(None, None, "gy", "gx", None),
            P(),
            P(),
        ),
        out_specs=(P(None, None, "gx", "gy", None), P(None, None, "gy", "gx", None)),
        check_vma=False,
    )
```

```python
import math

import jax
import jax.numpy as jnp
import ml_dtypes
import numpy as np
from jax import lax
from jax.experimental import pallas as pl
from jax.experimental.pallas import tpu as pltpu
from jax.sharding import PartitionSpec as P

C = 32
NX = 192
NY = 256
NZ = 256
KX = 48
KY = 64
KZ = 17
SCALE = (NX * NY * NZ) ** (-0.5)
MESH = pl.DeviceIdType.MESH
F32 = jnp.float32
BF16 = jnp.bfloat16


def kept(count, number):
    half = number // 2
    return np.concatenate([np.arange(half), np.arange(half) + count - half])


def trig(points, freqs, count):
    angle = 2.0 * np.pi * ((points[:, None] * freqs[None, :]) % count) / count
    return np.cos(angle), np.sin(angle)


def hi_lo(table):
    table = np.asarray(table, np.float32)
    high = table.astype(ml_dtypes.bfloat16)
    low = (table - high.astype(np.float32)).astype(ml_dtypes.bfloat16)
    return high, low


def make_tables():
    z_cos, z_sin = trig(np.arange(NZ), np.arange(KZ), NZ)
    y_cos, y_sin = trig(np.arange(NY), kept(NY, KY), NY)
    x_cos, x_sin = trig(np.arange(NX), kept(NX, KX), NX)
    tabs = {}
    wz = np.zeros((4, NZ, 2, 2, 4, 16))
    zz = np.zeros((4, 2, 2, 4, 16, NZ))
    for c4 in range(4):
        wz[c4, :, 0, 0, c4, :] = z_cos[:, :16]
        wz[c4, :, 0, 1, c4, :] = -z_sin[:, :16]
        wz[c4, :, 1, 0, c4, :] = z_cos[:, 16:17]
        wz[c4, :, 1, 1, c4, :] = -z_sin[:, 16:17]
        zz[c4, 0, 0, c4] = z_cos[:, :16].T
        zz[c4, 0, 1, c4] = -z_sin[:, :16].T
        zz[c4, 1, 0, c4] = z_cos[:, 16:17].T
        zz[c4, 1, 1, c4] = -z_sin[:, 16:17].T
    tabs["wz"] = wz.reshape(4 * NZ, 256).astype(np.float32).astype(ml_dtypes.bfloat16)
    tabs["zz"] = hi_lo(zz.reshape(4, 256, NZ))[0]
    s_at, zl_at, j_at = np.meshgrid(np.arange(8), np.arange(4), np.arange(2), indexing="ij")
    order = ((zl_at * 8 + s_at) * 2 + j_at).reshape(-1)
    yc = (y_cos * SCALE)[:, order].reshape(2, 128, 64)
    ys = (y_sin * SCALE)[:, order].reshape(2, 128, 64)
    inv = np.concatenate([yc, ys], 2)
    fwd = inv.transpose(0, 2, 1)
    tabs["t1"] = np.stack([np.concatenate([h, h, l], -1) for h, l in [hi_lo(fwd[0]), hi_lo(fwd[1])]])
    tabs["t1i"] = np.stack([np.concatenate([h, h, l], -1) for h, l in [hi_lo(inv[0]), hi_lo(inv[1])]])
    xt = np.stack([x_cos, x_sin]).reshape(2, 4, 8, 6, 2, 4, 6)
    t2 = np.zeros((4, 2, 4, 2, 4, 16, 6, 8, 8))
    for zl_to in range(4):
        for i in range(6):
            for j in range(2):
                block = xt[:, :, :, :, :, :, i]
                t2[:, :, zl_to, :, :, 2 * i + j, :, :, zl_to * 2 + j] = block.transpose(1, 4, 0, 5, 3, 2)
    fwd = t2.reshape(4, 8, 128, 384)
    tabs["t2"] = hi_lo(fwd)[0]
    inv = t2.transpose(0, 6, 3, 7, 8, 1, 2, 4, 5).reshape(4, 6, 128, 512)
    tabs["t2i"] = hi_lo(inv)[0]
    eye2, eye4 = np.eye(2), np.eye(4)
    ones16, ones32 = np.ones(16), np.ones(32)
    e1 = np.einsum("qr,cd,s,o->qcsrdo", eye2, eye4, ones16, ones32)
    tabs["e1"] = e1.reshape(128, 256)
    tabs["r2"] = e1.reshape(128, 256).T
    pick = np.eye(32).reshape(8, 4, 32)
    e2 = np.einsum("qr,bio,s,c->bqisrco", eye2, pick, ones16, np.ones(4)).reshape(8, 128, 256)
    tabs["e2"] = e2
    tabs["rr"] = e2.reshape(2, 2, 2, 128, 256).transpose(2, 0, 4, 1, 3).reshape(2, 2, 256, 256)
    slot = np.zeros((6, 16, 16))
    for x in range(6):
        slot[x, x, :] = 1.0
    spread = np.einsum("qr,cd,xst->xqcsrdt", eye2, eye4, slot).reshape(6, 128, 128)
    tabs["spread"] = spread.transpose(1, 0, 2).reshape(128, 768)
    tabs["gather"] = spread.transpose(0, 2, 1)
    tabs["a16"] = np.repeat(np.eye(32), 16, axis=0)
    for name in ("e1", "r2", "e2", "rr", "spread", "gather", "a16"):
        tabs[name] = tabs[name].astype(ml_dtypes.bfloat16)
    return tabs


TABLES = make_tables()
IN_VMEM = ("wz", "t1", "a16", "spread", "gather", "t1i", "e1", "r2")
IN_HBM = ("t2", "t2i", "zz", "e2", "rr")


def mm(left, right):
    return jnp.dot(left, right, preferred_element_type=F32)


def halves(values):
    high = values.astype(BF16)
    return high, (values - high.astype(F32)).astype(BF16)


def gelu_slope(values):
    size = jnp.abs(values)
    below = 1.0 + (0.3275911 / math.sqrt(2.0)) * size
    t = pl.reciprocal(below, approx=True)
    t = t * (2.0 - below * t)
    poly = t * (0.127414796 + t * (-0.142248368 + t * (0.7107068705 + t * (-0.7265760135 + t * 0.5307027145))))
    bell = jnp.exp2((-0.5 / math.log(2.0)) * (values * values))
    part = bell * (poly - (1.0 / math.sqrt(2.0 * math.pi)) * size)
    return jnp.where(values >= 0.0, 1.0 - part, part)


def swap(values, first):
    lane = lax.broadcasted_iota(jnp.int32, (values.shape[0], 128), 1)
    sign = jnp.where(lane < 64, first, -first)
    parts = [
        pltpu.roll(values[:, at : at + 128], 64, 1) * sign for at in range(0, values.shape[1], 128)
    ]
    return parts[0] if len(parts) == 1 else jnp.concatenate(parts, 1)


def slot_of(shape):
    return jnp.bitwise_and(lax.broadcasted_iota(jnp.int32, shape, len(shape) - 1), 15)


def row_of(shape):
    return jnp.bitwise_and(lax.broadcasted_iota(jnp.int32, shape, 0), 15)


def spread_rows(block):
    slots = slot_of((16, 128))
    rows = lax.broadcasted_iota(jnp.int32, (16, 128), 0)
    parts = [jnp.where(slots == k, block, 0.0) for k in range(16)]
    parts.append(jnp.where(slots == rows, jnp.broadcast_to(block[12:13], (16, 128)), 0.0))
    return jnp.concatenate(parts, 0)


def gather_rows(values):
    slots = slot_of((16, 128))
    rows = lax.broadcasted_iota(jnp.int32, (16, 128), 0)
    total = jnp.where(slots == 0, values[0:16], 0.0)
    for k in range(1, 16):
        total = total + jnp.where(slots == k, values[16 * k : 16 * k + 16], 0.0)
    last = jnp.sum(jnp.where(slots == rows, values[256:272], 0.0), axis=0, keepdims=True)
    return jnp.where(rows == 12, jnp.broadcast_to(last, (16, 128)), total)


def split_left(values, table):
    high, low = halves(values)
    out = mm(jnp.concatenate([high, low], 0), table)
    return out[: values.shape[0]] + out[values.shape[0] :]


GROUPS = ((0, 512), (512, 384))
CHUNKS = (((0, 256), (256, 256)), ((512, 256), (768, 128)))
ROWS = 13


def body(
    pw, bias, wz, t1, a16, spread, gather, t1i, e1, r2,
    t2_hbm, t2i_hbm, zz_hbm, e2_hbm, rr_hbm, f_hbm, cot_hbm, w_hbm,
    ig, wg_out,
    t2, t2i, zz, e2, rr, f, cot, w_in, w, wg, pg, lin, kron,
    u, r0, vs, r1, rsb, r3a, md, xb, mexp, gexp, acc,
    mq, r3b, xb2, vs2, r1s, ys, r0s, zb,
    f_sem, local_sem, s1s, s1r, s2s, s2r, s3s, s3r, g3s, g3r, g2s, g2r, g1s, g1r,
):
    gx = lax.axis_index("gx")
    gy = lax.axis_index("gy")
    zl, s = lax.div(gx, 8), lax.rem(gx, 8)
    zh, yy = lax.div(gy, 4), lax.rem(gy, 4)
    me = (zh * 4 + zl) * 4 + yy

    def y_id(to):
        return (gx, zh * 4 + to)

    def s_id(to):
        return (zl * 8 + to, gy)

    def m_id(zl_to, zh_to, y_to):
        return (zl_to * 8 + s, zh_to * 4 + y_to)

    def others(first):
        def one(z, y):
            pl.when(me != z * 4 + y)(lambda: first(z, z % 4, z // 4, y))

        for z in range(8):
            for y in range(4):
                one(z, y)

    def y_at(d):
        return lax.rem(yy + d, 4)

    def s_at(d):
        return lax.rem(s + d, 8)

    def each(low, high, fn):
        def step(d, carry):
            fn(d)
            return carry

        lax.fori_loop(low, high, step, 0)

    def f_load(to, h):
        return pltpu.make_async_copy(f_hbm.at[to, h], f.at[to, h], f_sem.at[to, h])

    for h in range(2):
        each(1, 5, lambda d, h=h: f_load(y_at(d), h).start())

    barrier = pltpu.get_barrier_semaphore()

    r3a[:, :, 8:16, :] = jnp.zeros((2, 32, 8, 128), F32)
    r3b[:, :, 8:16, :] = jnp.zeros((2, 32, 8, 128), F32)

    def greet(device):
        pl.semaphore_signal(barrier, inc=1, device_id=device, device_id_type=MESH)

    for d in range(1, 8):
        greet(s_id(s_at(d)))
    others(lambda z, zl_to, zh_to, y: greet(m_id(zl_to, zh_to, y)))

    loads = [
        pltpu.make_async_copy(src, dst, local_sem.at[n])
        for n, (src, dst) in enumerate(
            [
                (w_hbm, w_in),
                (t2_hbm.at[zl], t2),
                (rr_hbm, rr),
                (t2i_hbm.at[zl], t2i),
                (cot_hbm, cot),
                (zz_hbm, zz),
                (e2_hbm, e2),
            ]
        )
    ]
    for load in loads:
        load.start()
    def send(src, dst, send_sem, recv_sem, device):
        return pltpu.make_async_remote_copy(src, dst, send_sem, recv_sem, device_id=device, device_id_type=MESH)

    def c1(h, to, g):
        cells = pl.ds(*GROUPS[g])
        return send(u.at[h, to, :, cells], r0.at[h, yy, :, cells], s1s.at[h], s1r.at[h, g], y_id(to))

    def c2(h, to, g):
        cells = pl.ds(*GROUPS[g])
        return send(vs.at[h, to, :, cells], r1.at[h, s, :, cells], s2s.at[h], s2r.at[h], s_id(to))

    def c3(h, z, device_y):
        rows = pl.ds(0, ROWS)
        device = m_id(lax.rem(z, 4), lax.div(z, 4), device_y)
        return send(rsb.at[h, z * 4 + device_y, rows], r3a.at[h, me, rows], s3s.at[h], s3r.at[h], device)

    def k3(h, zl_to, zh_to, y):
        rows = pl.ds(0, ROWS)
        device = m_id(zl_to, zh_to, y)
        return send(mq.at[h, y, rows], r3b.at[h, me, rows], g3s.at[h], g3r.at[h], device)

    def k2(h, to, g):
        cells = pl.ds(*GROUPS[g])
        return send(vs2.at[h, to, :, cells], r1s.at[h, s, :, cells], g2s.at[h], g2r.at[h, g], s_id(to))

    def k1(h, to, g):
        cells = pl.ds(*GROUPS[g])
        return send(ys.at[h, to, :, cells], r0s.at[h, yy, :, cells], g1s.at[h], g1r.at[h, yy], y_id(to))

    def whole(part, sem):
        pltpu.make_async_copy(part, part, sem).wait()

    def all_of(buffer, h, count, sem):
        whole(buffer.at[h, pl.ds(0, count)], sem.at[h])

    def all_of_group(buffer, h, count, sem, g):
        whole(buffer.at[h, pl.ds(0, count), :, pl.ds(*GROUPS[g])], sem.at[h, g])

    def all_modes(buffer, h, sem):
        whole(buffer.at[h, pl.ds(0, 31), pl.ds(0, ROWS)], sem.at[h])

    def z_analysis(source, h, to, dest):
        total = mm(jnp.concatenate([source[to, h, q].reshape(192, 256) for q in range(4)], 1), wz[...])
        slots = slot_of((32, 128))
        last = None
        for x in range(6):
            rows = total[32 * x : 32 * x + 32]
            dest[:, 128 * x : 128 * x + 128] = rows[:, :128]
            part = jnp.where(slots == x, rows[:, 128:], 0.0)
            last = part if last is None else last + part
        dest[:, 768:896] = last

    def analysis_start(source, h, greeted):
        def one(d):
            to = y_at(d)
            f_load(to, h).wait()
            z_analysis(source, h, to, u.at[h, to])
            if greeted:
                c1(h, to, 0).start()

        each(1, 4, one)
        if not greeted:
            pl.semaphore_wait(barrier, 38)
            for d in range(1, 4):
                c1(h, y_at(d), 0).start()
        for d in range(1, 4):
            c1(h, y_at(d), 1).start()
        f_load(yy, h).wait()
        z_analysis(source, h, yy, r0.at[h, yy])

    def y_analysis(h, g):
        table = t1.at[zh]
        for at, wide in CHUNKS[g]:
            high, low = halves(r0[h, :, :, at : at + wide].reshape(128, wide))
            out = mm(table[...], jnp.concatenate([high, low, high], 0))
            vs[h, :, :, at : at + wide] = (out[:64] + swap(out[64:], 1.0)).reshape(8, 8, wide)

    def x_analysis_load(h):
        last = r1[h, :, :, 768:896].reshape(64, 128).astype(BF16)
        last = mm(last, spread[...]).astype(BF16)
        for x in range(6):
            at = 128 * x
            xb[64 * x : 64 * x + 64, 0:128] = r1[h, :, :, at : at + 128].reshape(64, 128).astype(BF16)
            xb[64 * x : 64 * x + 64, 128:256] = last[:, at : at + 128]

    def x_analysis_store(out, h, z):
        out = out[:64] + swap(out[64:], 1.0)
        rows = row_of((64, 128))
        last = jnp.where(slot_of((64, 128)) == rows, out[:, 128:], 0.0)
        last = jnp.sum(last.reshape(4, 16, 128), axis=1, keepdims=True)
        last = jnp.broadcast_to(last, (4, 16, 128)).reshape(64, 128)
        rsb[h, pl.ds(4 * z, 4)] = jnp.where(rows == 12, last, out[:, :128]).reshape(4, 16, 128)

    def x_analysis(h):
        mine = zh * 4 + zl
        for group in ((1, 2, 3, 4), (5, 6, 7, 8)):
            to = [lax.rem(mine + d, 8) for d in group]
            out = mm(jnp.concatenate([t2[z] for z in to], 0), xb[...])
            for n, d in enumerate(group):
                x_analysis_store(out[128 * n : 128 * n + 128], h, to[n])
                for y in range(4 if d < 8 else 3):
                    c3(h, to[n], y if d < 8 else y_at(y + 1)).start()
        r3a[h, me] = rsb[h, me]

    def analysis(first, second, received):
        first()
        for h in range(2):
            for g in range(2):
                all_of_group(r0, h, 3, s1r, g)
                y_analysis(h, g)
                for d in range(1, 8):
                    c2(h, s_at(d), g).start()
            r1[h, s] = vs[h, s]
        for h in range(2):
            all_of(r1, h, 7, s2r)
            x_analysis_load(h)
            x_analysis(h)
        second()
        for h in range(2):
            all_modes(r3a, h, s3r)
            total = r3a[h, 0:4]
            for z in range(1, 8):
                total = total + r3a[h, 4 * z : 4 * z + 4]
            md[h] = total
            received(h)

    def analysis_end():
        for h in range(2):
            all_of(u, h, 3, s1s)
            all_of(vs, h, 7, s2s)
            all_modes(rsb, h, s3s)

    def x_synthesis_load(h):
        main = r3b[h]
        rows = row_of((512, 128))
        last = jnp.broadcast_to(main[:, 12:13], (32, 16, 128)).reshape(512, 128)
        xb2[:, 0:128] = main.reshape(512, 128).astype(BF16)
        xb2[:, 128:256] = jnp.where(slot_of((512, 128)) == rows, last, 0.0).astype(BF16)

    def x_synthesis(h):
        total = None
        for group in ((0, 1), (2, 3), (4, 5)):
            out = mm(jnp.concatenate([t2i[x] for x in group], 0), xb2[...])
            for n, x in enumerate(group):
                part = out[128 * n : 128 * n + 128]
                part = part[:64] + swap(part[64:], -1.0)
                vs2[h, :, :, 128 * x : 128 * x + 128] = part[:, :128].reshape(8, 8, 128)
                high, low = halves(part[:, 128:])
                last = mm(high, gather[x]) + mm(low, gather[x])
                total = last if total is None else total + last
            if group == (2, 3):
                for d in range(1, 8):
                    k2(h, s_at(d), 0).start()
        vs2[h, :, :, 768:896] = total.reshape(8, 8, 128)
        for d in range(1, 8):
            k2(h, s_at(d), 1).start()

    def y_synthesis(h, g):
        table = t1i.at[zh]
        for at, wide in CHUNKS[g]:
            values = r1s[h, :, :, at : at + wide].reshape(64, wide)
            high, low = halves(jnp.concatenate([values, swap(values, -1.0)], 0))
            out = mm(table[...], jnp.concatenate([high, low, high], 0))
            ys[h, :, :, at : at + wide] = out.reshape(4, 32, wide)

    def z_synthesis(h, fr, finish):
        slots = slot_of((32, 128))
        last = r0s[h, fr, :, 768:896]
        for x in range(6):
            zb[32 * x : 32 * x + 32, 0:128] = r0s[h, fr, :, 128 * x : 128 * x + 128].astype(BF16)
            zb[32 * x : 32 * x + 32, 128:256] = jnp.where(slots == x, last, 0.0).astype(BF16)

        def one(pair):
            for n in range(2):
                q = 2 * pair + n
                finish(fr, h, q, mm(zb[...], zz[q]).reshape(6, 32, 256))

        each(0, 2, one)

    def synthesis(meanwhile, finish, own, after):
        meanwhile()
        for h in range(2):
            all_modes(r3b, h, g3r)
            x_synthesis_load(h)
            x_synthesis(h)
            r1s[h, s] = vs2[h, s]
        for h in range(2):
            for g in range(2):
                all_of_group(r1s, h, 7, g2r, g)
                y_synthesis(h, g)
                for d in range(1, 4):
                    k1(h, y_at(d), g).start()
            r0s[h, yy] = ys[h, yy]
        for h in range(2):
            z_synthesis(h, yy, finish)
            own(h)
        for h in range(2):

            def one(d, h=h):
                fr = y_at(2 * d - 1 - lax.div(d, 3) * 3)
                whole(r0s.at[h, fr], g1r.at[h, fr])
                z_synthesis(h, fr, finish)
                after(h, fr)

            each(1, 4, one)
        for h in range(2):
            all_modes(r3b, h, g3s)
            all_of(vs2, h, 7, g2s)
            all_of(ys, h, 3, g1s)

    def channel_matrix(wide):
        rows = row_of((512, 512))
        columns = slot_of((512, 512))
        full = lax.dot_general(
            wide.astype(BF16), a16[...], (((1,), (1,)), ((), ())), preferred_element_type=F32
        )
        kron[...] = jnp.where(rows == columns, full, 0.0).astype(BF16)

    def channel_map(source, low, high):
        def one(x):
            for at in (0, 16):
                block = source[:, :, :, x, at : at + 16, :].reshape(512, 256)
                out = mm(kron[...], block)
                lin[:, :, :, x, at : at + 16, :] = out.reshape(4, 2, 4, 16, 256)

        each(low, high, one)

    def lanes(b):
        return pl.ds(pl.multiple_of(b * 128, 128), 128)

    def weights_in():
        loads[0].wait()

        def one(k):
            for part in range(2):
                for i in range(6):
                    w[part, k, 2 * i : 2 * i + 2, :] = w_in[part, k, i]
                w[part, k, 12:16, :] = jnp.zeros((4, 1024), F32)

        each(0, KZ, one)

    def weight_grad_out():
        def one(k):
            for part in range(2):
                for i in range(6):
                    wg_out[part, k, i] = wg[part, k, 2 * i : 2 * i + 2, :]

        each(0, KZ, one)

    def w_at(part, b):
        return w[part, :, :, lanes(b)].reshape(272, 128)

    def mix_one(h):
        def one(y):
            b = 2 * y + h
            modes = split_left(spread_rows(md[h, y]), e1[...])
            mexp[b] = modes
            real, imag = modes[:, :128], modes[:, 128:]
            w_real, w_imag = w_at(0, b), w_at(1, b)
            acc[:, :128] += w_real * real - w_imag * imag
            acc[:, 128:] += w_real * imag + w_imag * real

        each(0, 4, one)

    def spread_out(h, y):
        def one(z):
            pl.when(me != z * 4 + y)(lambda: k3(h, z % 4, z // 4, y).start())

        for z in range(8):
            one(z)

    def keep_own(h):
        r3b[h, me] = mq[h, yy]

    def mix_two():
        for h in range(2):
            for pair in range(2):
                out = split_left(acc[...], rr[h, pair])
                for n in range(2):
                    y = 2 * pair + n
                    mq[h, y] = gather_rows(out[:, 128 * n : 128 * n + 128])
                    spread_out(h, y)
            keep_own(h)

    def back_one(h):
        def one(y):
            gexp[...] += split_left(spread_rows(md[h, y]), e2[2 * y + h])

        each(0, 4, one)

    def back_two():
        for h in range(2):

            def two(y, h=h):
                b = 2 * y + h
                g_real, g_imag = gexp[:, :128], gexp[:, 128:]
                w_real, w_imag = w_at(0, b), w_at(1, b)
                real = w_real * g_real + w_imag * g_imag
                imag = w_real * g_imag - w_imag * g_real
                mq[h, y] = gather_rows(split_left(jnp.concatenate([real, imag], 1), r2[...]))
                spread_out(h, y)

            each(0, 4, two)
            keep_own(h)

    def weight_grad():
        def one(b):
            g_real, g_imag = gexp[:, :128], gexp[:, 128:]
            real, imag = mexp[b, :, :128], mexp[b, :, 128:]
            wg[0, :, :, lanes(b)] = (real * g_real + imag * g_imag).reshape(KZ, 16, 128)
            wg[1, :, :, lanes(b)] = (real * g_imag - imag * g_real).reshape(KZ, 16, 128)

        each(0, 8, one)
        weight_grad_out()

    def finish_pre(fr, h, q, spectral):
        pre = spectral + lin[fr, h, q] + bias[fr * 8 + h * 4 + q]
        pg[fr, h, q] = (cot[fr, h, q].astype(F32) * gelu_slope(pre)).astype(BF16)

    def finish_grad(fr, h, q, spectral):
        ig[fr, h, q] = (spectral + lin[fr, h, q]).astype(BF16)

    def second_own(h):
        z_analysis(pg, h, yy, r0.at[h, yy])

    def second_start(h, to):
        z_analysis(pg, h, to, u.at[h, to])
        for g in range(2):
            c1(h, to, g).start()

    def first_y_wait():
        channel_matrix(mm(a16[...], pw[...]))
        channel_map(f, 0, 6)
        loads[1].wait()

    def first_z_wait():
        weights_in()
        acc[...] = jnp.zeros_like(acc)

    def second_z_wait():
        wide = lax.dot_general(a16[...], pw[...], (((1,), (1,)), ((), ())), preferred_element_type=F32)
        channel_matrix(wide)
        channel_map(pg, 0, 6)
        gexp[...] = jnp.zeros_like(gexp)

    def wait_loads():
        for load in loads[3:]:
            load.wait()

    for h in range(2):
        analysis_start(f, h, h == 1)
    analysis(first_y_wait, first_z_wait, mix_one)
    loads[2].wait()
    mix_two()
    analysis_end()
    synthesis(wait_loads, finish_pre, second_own, second_start)
    analysis(lambda: None, second_z_wait, back_one)
    back_two()
    synthesis(weight_grad, finish_grad, lambda h: None, lambda h, fr: None)
    analysis_end()


def per_device(input_field, cotangent, spectral_weights, point_weight, point_bias):
    field_shape = (4, 2, 4, 6, 32, 256)
    w_shape = spectral_weights.shape
    tabs = {name: jnp.asarray(value) for name, value in TABLES.items()}
    vmem = pl.BlockSpec(memory_space=pltpu.VMEM)
    smem = pl.BlockSpec(memory_space=pltpu.SMEM)
    hbm = pl.BlockSpec(memory_space=pl.ANY)
    dma = pltpu.SemaphoreType.DMA
    scratch = [
        pltpu.VMEM((8, 128, 384), BF16),
        pltpu.VMEM((6, 128, 512), BF16),
        pltpu.VMEM((4, 256, 256), BF16),
        pltpu.VMEM((8, 128, 256), BF16),
        pltpu.VMEM((2, 2, 256, 256), BF16),
        pltpu.VMEM(field_shape, BF16),
        pltpu.VMEM(field_shape, BF16),
        pltpu.VMEM(w_shape, F32),
        pltpu.VMEM((2, KZ, 16, 1024), F32),
        pltpu.VMEM((2, KZ, 16, 1024), F32),
        pltpu.VMEM(field_shape, BF16),
        pltpu.VMEM(field_shape, F32),
        pltpu.VMEM((512, 512), BF16),
        pltpu.VMEM((2, 4, 32, 896), F32),
        pltpu.VMEM((2, 4, 32, 896), F32),
        pltpu.VMEM((2, 8, 8, 896), F32),
        pltpu.VMEM((2, 8, 8, 896), F32),
        pltpu.VMEM((2, 32, 16, 128), F32),
        pltpu.VMEM((2, 32, 16, 128), F32),
        pltpu.VMEM((2, 4, 16, 128), F32),
        pltpu.VMEM((384, 256), BF16),
        pltpu.VMEM((8, 272, 256), F32),
        pltpu.VMEM((272, 256), F32),
        pltpu.VMEM((272, 256), F32),
        pltpu.VMEM((2, 4, 16, 128), F32),
        pltpu.VMEM((2, 32, 16, 128), F32),
        pltpu.VMEM((512, 256), BF16),
        pltpu.VMEM((2, 8, 8, 896), F32),
        pltpu.VMEM((2, 8, 8, 896), F32),
        pltpu.VMEM((2, 4, 32, 896), F32),
        pltpu.VMEM((2, 4, 32, 896), F32),
        pltpu.VMEM((192, 256), BF16),
        dma((4, 2)),
        dma((7,)),
        dma((2,)), dma((2, 2)), dma((2,)), dma((2,)), dma((2,)), dma((2,)),
        dma((2,)), dma((2,)), dma((2,)), dma((2, 2)), dma((2,)), dma((2, 4)),
    ]
    ig, wg = pl.pallas_call(
        body,
        out_shape=(
            pltpu.VMEM(field_shape, BF16),
            pltpu.VMEM(w_shape, F32),
        ),
        in_specs=[vmem, smem] + [vmem] * len(IN_VMEM) + [hbm] * (len(IN_HBM) + 3),
        out_specs=(vmem, vmem),
        scratch_shapes=scratch,
        compiler_params=pltpu.CompilerParams(
            collective_id=0, has_side_effects=True, vmem_limit_bytes=50 * 1024 * 1024
        ),
        cost_estimate=pl.CostEstimate(flops=10**10, bytes_accessed=2 * 10**7, transcendentals=0),
    )(
        point_weight, point_bias,
        *[tabs[name] for name in IN_VMEM],
        *[tabs[name] for name in IN_HBM],
        input_field.reshape(field_shape), cotangent.reshape(field_shape), spectral_weights,
    )
    return (ig.reshape(input_field.shape), wg)


def solution(mesh):
    return jax.shard_map(
        per_device,
        mesh=mesh,
        in_specs=(
            P(None, None, "gx", "gy", None),
            P(None, None, "gx", "gy", None),
            P(None, None, "gy", "gx", None),
            P(),
            P(),
        ),
        out_specs=(P(None, None, "gx", "gy", None), P(None, None, "gy", "gx", None)),
        check_vma=False,
    )
```

```python
import math

import jax
import jax.numpy as jnp
import ml_dtypes
import numpy as np
from jax import lax
from jax.experimental import pallas as pl
from jax.experimental.pallas import tpu as pltpu
from jax.sharding import PartitionSpec as P

C = 32
NX = 192
NY = 256
NZ = 256
KX = 48
KY = 64
KZ = 17
SCALE = (NX * NY * NZ) ** (-0.5)
MESH = pl.DeviceIdType.MESH
F32 = jnp.float32
BF16 = jnp.bfloat16


def kept(count, number):
    half = number // 2
    return np.concatenate([np.arange(half), np.arange(half) + count - half])


def trig(points, freqs, count):
    angle = 2.0 * np.pi * ((points[:, None] * freqs[None, :]) % count) / count
    return np.cos(angle), np.sin(angle)


def hi_lo(table):
    table = np.asarray(table, np.float32)
    high = table.astype(ml_dtypes.bfloat16)
    low = (table - high.astype(np.float32)).astype(ml_dtypes.bfloat16)
    return high, low


def make_tables():
    z_cos, z_sin = trig(np.arange(NZ), np.arange(KZ), NZ)
    y_cos, y_sin = trig(np.arange(NY), kept(NY, KY), NY)
    x_cos, x_sin = trig(np.arange(NX), kept(NX, KX), NX)
    tabs = {}
    wz = np.zeros((4, NZ, 2, 2, 4, 16))
    zz = np.zeros((4, 2, 2, 4, 16, NZ))
    for c4 in range(4):
        wz[c4, :, 0, 0, c4, :] = z_cos[:, :16]
        wz[c4, :, 0, 1, c4, :] = -z_sin[:, :16]
        wz[c4, :, 1, 0, c4, :] = z_cos[:, 16:17]
        wz[c4, :, 1, 1, c4, :] = -z_sin[:, 16:17]
        zz[c4, 0, 0, c4] = z_cos[:, :16].T
        zz[c4, 0, 1, c4] = -z_sin[:, :16].T
        zz[c4, 1, 0, c4] = z_cos[:, 16:17].T
        zz[c4, 1, 1, c4] = -z_sin[:, 16:17].T
    tabs["wz"] = wz.reshape(4 * NZ, 256).astype(np.float32).astype(ml_dtypes.bfloat16)
    tabs["zz"] = hi_lo(zz.reshape(4, 256, NZ))[0]
    s_at, zl_at, j_at = np.meshgrid(np.arange(8), np.arange(4), np.arange(2), indexing="ij")
    order = ((zl_at * 8 + s_at) * 2 + j_at).reshape(-1)
    yc = (y_cos * SCALE)[:, order].reshape(2, 128, 64)
    ys = (y_sin * SCALE)[:, order].reshape(2, 128, 64)
    inv = np.concatenate([yc, ys], 2)
    fwd = inv.transpose(0, 2, 1)
    tabs["t1"] = np.stack([np.concatenate([h, h, l], -1) for h, l in [hi_lo(fwd[0]), hi_lo(fwd[1])]])
    tabs["t1i"] = np.stack([np.concatenate([h, h, l], -1) for h, l in [hi_lo(inv[0]), hi_lo(inv[1])]])
    xt = np.stack([x_cos, x_sin]).reshape(2, 4, 8, 6, 2, 4, 6)
    t2 = np.zeros((4, 2, 4, 2, 4, 16, 6, 8, 8))
    for zl_to in range(4):
        for i in range(6):
            for j in range(2):
                block = xt[:, :, :, :, :, :, i]
                t2[:, :, zl_to, :, :, 2 * i + j, :, :, zl_to * 2 + j] = block.transpose(1, 4, 0, 5, 3, 2)
    fwd = t2.reshape(4, 8, 128, 384)
    tabs["t2"] = hi_lo(fwd)[0]
    inv = t2.transpose(0, 6, 3, 7, 8, 1, 2, 4, 5).reshape(4, 6, 128, 512)
    tabs["t2i"] = hi_lo(inv)[0]
    eye2, eye4 = np.eye(2), np.eye(4)
    ones16, ones32 = np.ones(16), np.ones(32)
    e1 = np.einsum("qr,cd,s,o->qcsrdo", eye2, eye4, ones16, ones32)
    tabs["e1"] = e1.reshape(128, 256)
    tabs["r2"] = e1.reshape(128, 256).T
    pick = np.eye(32).reshape(8, 4, 32)
    e2 = np.einsum("qr,bio,s,c->bqisrco", eye2, pick, ones16, np.ones(4)).reshape(8, 128, 256)
    tabs["e2"] = e2
    tabs["rr"] = e2.reshape(2, 2, 2, 128, 256).transpose(2, 0, 4, 1, 3).reshape(2, 2, 256, 256)
    slot = np.zeros((6, 16, 16))
    for x in range(6):
        slot[x, x, :] = 1.0
    spread = np.einsum("qr,cd,xst->xqcsrdt", eye2, eye4, slot).reshape(6, 128, 128)
    tabs["spread"] = spread.transpose(1, 0, 2).reshape(128, 768)
    tabs["gather"] = spread.transpose(0, 2, 1)
    tabs["a16"] = np.repeat(np.eye(32), 16, axis=0)
    for name in ("e1", "r2", "e2", "rr", "spread", "gather", "a16"):
        tabs[name] = tabs[name].astype(ml_dtypes.bfloat16)
    return tabs


TABLES = make_tables()
IN_VMEM = ("wz", "t1", "a16", "spread", "gather", "t1i", "e1", "r2")
IN_HBM = ("t2", "t2i", "zz", "e2", "rr")


def mm(left, right):
    return jnp.dot(left, right, preferred_element_type=F32)


def halves(values):
    high = values.astype(BF16)
    return high, (values - high.astype(F32)).astype(BF16)


def gelu_slope(values):
    size = jnp.abs(values)
    below = 1.0 + (0.3275911 / math.sqrt(2.0)) * size
    t = pl.reciprocal(below, approx=True)
    t = t * (2.0 - below * t)
    poly = t * (0.127414796 + t * (-0.142248368 + t * (0.7107068705 + t * (-0.7265760135 + t * 0.5307027145))))
    bell = jnp.exp2((-0.5 / math.log(2.0)) * (values * values))
    part = bell * (poly - (1.0 / math.sqrt(2.0 * math.pi)) * size)
    return jnp.where(values >= 0.0, 1.0 - part, part)


def swap(values, first):
    lane = lax.broadcasted_iota(jnp.int32, (values.shape[0], 128), 1)
    sign = jnp.where(lane < 64, first, -first)
    parts = [
        pltpu.roll(values[:, at : at + 128], 64, 1) * sign for at in range(0, values.shape[1], 128)
    ]
    return parts[0] if len(parts) == 1 else jnp.concatenate(parts, 1)


def slot_of(shape):
    return jnp.bitwise_and(lax.broadcasted_iota(jnp.int32, shape, len(shape) - 1), 15)


def row_of(shape):
    return jnp.bitwise_and(lax.broadcasted_iota(jnp.int32, shape, 0), 15)


def spread_rows(block):
    slots = slot_of((16, 128))
    rows = lax.broadcasted_iota(jnp.int32, (16, 128), 0)
    parts = [jnp.where(slots == k, block, 0.0) for k in range(16)]
    parts.append(jnp.where(slots == rows, jnp.broadcast_to(block[12:13], (16, 128)), 0.0))
    return jnp.concatenate(parts, 0)


def gather_rows(values):
    slots = slot_of((16, 128))
    rows = lax.broadcasted_iota(jnp.int32, (16, 128), 0)
    total = jnp.where(slots == 0, values[0:16], 0.0)
    for k in range(1, 16):
        total = total + jnp.where(slots == k, values[16 * k : 16 * k + 16], 0.0)
    last = jnp.sum(jnp.where(slots == rows, values[256:272], 0.0), axis=0, keepdims=True)
    return jnp.where(rows == 12, jnp.broadcast_to(last, (16, 128)), total)


def split_left(values, table):
    high, low = halves(values)
    out = mm(jnp.concatenate([high, low], 0), table)
    return out[: values.shape[0]] + out[values.shape[0] :]


GROUPS = ((0, 512), (512, 384))
CHUNKS = (((0, 256), (256, 256)), ((512, 256), (768, 128)))
ROWS = 13


def body(
    pw, bias, wz, t1, a16, spread, gather, t1i, e1, r2,
    t2_hbm, t2i_hbm, zz_hbm, e2_hbm, rr_hbm, f_hbm, cot_hbm, w_hbm,
    ig, wg_out,
    t2, t2i, zz, e2, rr, f, cot, w_in, w, wg, pg, lin, kron,
    u, r0, vs, r1, rsb, r3a, md, xb, mexp, gexp, acc,
    mq, r3b, xb2, vs2, r1s, ys, r0s, zb,
    f_sem, local_sem, s1s, s1r, s2s, s2r, s3s, s3r, g3s, g3r, g2s, g2r, g1s, g1r,
):
    gx = lax.axis_index("gx")
    gy = lax.axis_index("gy")
    zl, s = lax.div(gx, 8), lax.rem(gx, 8)
    zh, yy = lax.div(gy, 4), lax.rem(gy, 4)
    me = (zh * 4 + zl) * 4 + yy

    def y_id(to):
        return (gx, zh * 4 + to)

    def s_id(to):
        return (zl * 8 + to, gy)

    def m_id(zl_to, zh_to, y_to):
        return (zl_to * 8 + s, zh_to * 4 + y_to)

    def others(first):
        def one(z, y):
            pl.when(me != z * 4 + y)(lambda: first(z, z % 4, z // 4, y))

        for z in range(8):
            for y in range(4):
                one(z, y)

    def y_at(d):
        return lax.rem(yy + d, 4)

    def s_at(d):
        return lax.rem(s + d, 8)

    def each(low, high, fn):
        def step(d, carry):
            fn(d)
            return carry

        lax.fori_loop(low, high, step, 0)

    def f_load(to, h):
        return pltpu.make_async_copy(f_hbm.at[to, h], f.at[to, h], f_sem.at[to, h])

    for h in range(2):
        each(1, 5, lambda d, h=h: f_load(y_at(d), h).start())

    barrier = pltpu.get_barrier_semaphore()

    r3a[:, :, 8:16, :] = jnp.zeros((2, 32, 8, 128), F32)
    r3b[:, :, 8:16, :] = jnp.zeros((2, 32, 8, 128), F32)

    def greet(device):
        pl.semaphore_signal(barrier, inc=1, device_id=device, device_id_type=MESH)

    for d in range(1, 8):
        greet(s_id(s_at(d)))
    others(lambda z, zl_to, zh_to, y: greet(m_id(zl_to, zh_to, y)))

    loads = [
        pltpu.make_async_copy(src, dst, local_sem.at[n])
        for n, (src, dst) in enumerate(
            [
                (w_hbm, w_in),
                (t2_hbm.at[zl], t2),
                (rr_hbm, rr),
                (t2i_hbm.at[zl], t2i),
                (cot_hbm, cot),
                (zz_hbm, zz),
                (e2_hbm, e2),
            ]
        )
    ]
    for load in loads:
        load.start()
    def send(src, dst, send_sem, recv_sem, device):
        return pltpu.make_async_remote_copy(src, dst, send_sem, recv_sem, device_id=device, device_id_type=MESH)

    def c1(h, to, g):
        cells = pl.ds(*GROUPS[g])
        return send(u.at[h, to, :, cells], r0.at[h, yy, :, cells], s1s.at[h], s1r.at[h, g], y_id(to))

    def c2(h, to, g):
        cells = pl.ds(*GROUPS[g])
        return send(vs.at[h, to, :, cells], r1.at[h, s, :, cells], s2s.at[h], s2r.at[h], s_id(to))

    def c3(h, z, device_y):
        rows = pl.ds(0, ROWS)
        device = m_id(lax.rem(z, 4), lax.div(z, 4), device_y)
        return send(rsb.at[h, z * 4 + device_y, rows], r3a.at[h, me, rows], s3s.at[h], s3r.at[h], device)

    def k3(h, zl_to, zh_to, y):
        rows = pl.ds(0, ROWS)
        device = m_id(zl_to, zh_to, y)
        return send(mq.at[h, y, rows], r3b.at[h, me, rows], g3s.at[h], g3r.at[h], device)

    def k2(h, to, g):
        cells = pl.ds(*GROUPS[g])
        return send(vs2.at[h, to, :, cells], r1s.at[h, s, :, cells], g2s.at[h], g2r.at[h, g], s_id(to))

    def k1(h, to, g):
        cells = pl.ds(*GROUPS[g])
        return send(ys.at[h, to, :, cells], r0s.at[h, yy, :, cells], g1s.at[h], g1r.at[h, yy], y_id(to))

    def whole(part, sem):
        pltpu.make_async_copy(part, part, sem).wait()

    def all_of(buffer, h, count, sem):
        whole(buffer.at[h, pl.ds(0, count)], sem.at[h])

    def all_of_group(buffer, h, count, sem, g):
        whole(buffer.at[h, pl.ds(0, count), :, pl.ds(*GROUPS[g])], sem.at[h, g])

    def all_modes(buffer, h, sem):
        whole(buffer.at[h, pl.ds(0, 31), pl.ds(0, ROWS)], sem.at[h])

    def z_analysis(source, h, to, dest):
        total = mm(jnp.concatenate([source[to, h, q].reshape(192, 256) for q in range(4)], 1), wz[...])
        slots = slot_of((32, 128))
        last = None
        for x in range(6):
            rows = total[32 * x : 32 * x + 32]
            dest[:, 128 * x : 128 * x + 128] = rows[:, :128]
            part = jnp.where(slots == x, rows[:, 128:], 0.0)
            last = part if last is None else last + part
        dest[:, 768:896] = last

    def analysis_start(source, h, greeted):
        def one(d):
            to = y_at(d)
            f_load(to, h).wait()
            z_analysis(source, h, to, u.at[h, to])
            if greeted:
                c1(h, to, 0).start()

        each(1, 4, one)
        if not greeted:
            pl.semaphore_wait(barrier, 38)
            for d in range(1, 4):
                c1(h, y_at(d), 0).start()
        for d in range(1, 4):
            c1(h, y_at(d), 1).start()
        f_load(yy, h).wait()
        z_analysis(source, h, yy, r0.at[h, yy])

    def y_analysis(h, g):
        table = t1.at[zh]
        for at, wide in CHUNKS[g]:
            high, low = halves(r0[h, :, :, at : at + wide].reshape(128, wide))
            out = mm(table[...], jnp.concatenate([high, low, high], 0))
            vs[h, :, :, at : at + wide] = (out[:64] + swap(out[64:], 1.0)).reshape(8, 8, wide)

    def x_analysis_load(h):
        last = r1[h, :, :, 768:896].reshape(64, 128).astype(BF16)
        last = mm(last, spread[...]).astype(BF16)
        for x in range(6):
            at = 128 * x
            xb[64 * x : 64 * x + 64, 0:128] = r1[h, :, :, at : at + 128].reshape(64, 128).astype(BF16)
            xb[64 * x : 64 * x + 64, 128:256] = last[:, at : at + 128]

    def x_analysis_store(out, h, z):
        out = out[:64] + swap(out[64:], 1.0)
        rows = row_of((64, 128))
        last = jnp.where(slot_of((64, 128)) == rows, out[:, 128:], 0.0)
        last = jnp.sum(last.reshape(4, 16, 128), axis=1, keepdims=True)
        last = jnp.broadcast_to(last, (4, 16, 128)).reshape(64, 128)
        rsb[h, pl.ds(4 * z, 4)] = jnp.where(rows == 12, last, out[:, :128]).reshape(4, 16, 128)

    def x_analysis(h):
        mine = zh * 4 + zl
        for group in ((1, 2, 3, 4), (5, 6, 7, 8)):
            to = [lax.rem(mine + d, 8) for d in group]
            out = mm(jnp.concatenate([t2[z] for z in to], 0), xb[...])
            for n, d in enumerate(group):
                x_analysis_store(out[128 * n : 128 * n + 128], h, to[n])
                for y in range(4 if d < 8 else 3):
                    c3(h, to[n], y if d < 8 else y_at(y + 1)).start()
        r3a[h, me] = rsb[h, me]

    def analysis(first, second, received):
        first()
        for h in range(2):
            for g in range(2):
                all_of_group(r0, h, 3, s1r, g)
                y_analysis(h, g)
                for d in range(1, 8):
                    c2(h, s_at(d), g).start()
            r1[h, s] = vs[h, s]
        for h in range(2):
            all_of(r1, h, 7, s2r)
            x_analysis_load(h)
            x_analysis(h)
        second()
        for h in range(2):
            all_modes(r3a, h, s3r)
            total = r3a[h, 0:4]
            for z in range(1, 8):
                total = total + r3a[h, 4 * z : 4 * z + 4]
            md[h] = total
            received(h)

    def analysis_end():
        for h in range(2):
            all_of(u, h, 3, s1s)
            all_of(vs, h, 7, s2s)
            all_modes(rsb, h, s3s)

    def x_synthesis_load(h):
        main = r3b[h]
        rows = row_of((512, 128))
        last = jnp.broadcast_to(main[:, 12:13], (32, 16, 128)).reshape(512, 128)
        xb2[:, 0:128] = main.reshape(512, 128).astype(BF16)
        xb2[:, 128:256] = jnp.where(slot_of((512, 128)) == rows, last, 0.0).astype(BF16)

    def x_synthesis(h):
        total = None
        for group in ((0, 1), (2, 3), (4, 5)):
            out = mm(jnp.concatenate([t2i[x] for x in group], 0), xb2[...])
            for n, x in enumerate(group):
                part = out[128 * n : 128 * n + 128]
                part = part[:64] + swap(part[64:], -1.0)
                vs2[h, :, :, 128 * x : 128 * x + 128] = part[:, :128].reshape(8, 8, 128)
                high, low = halves(part[:, 128:])
                last = mm(high, gather[x]) + mm(low, gather[x])
                total = last if total is None else total + last
            if group == (2, 3):
                for d in range(1, 8):
                    k2(h, s_at(d), 0).start()
        vs2[h, :, :, 768:896] = total.reshape(8, 8, 128)
        for d in range(1, 8):
            k2(h, s_at(d), 1).start()

    def y_synthesis(h, g):
        table = t1i.at[zh]
        for at, wide in CHUNKS[g]:
            values = r1s[h, :, :, at : at + wide].reshape(64, wide)
            high, low = halves(jnp.concatenate([values, swap(values, -1.0)], 0))
            out = mm(table[...], jnp.concatenate([high, low, high], 0))
            ys[h, :, :, at : at + wide] = out.reshape(4, 32, wide)

    def z_synthesis(h, fr, finish):
        slots = slot_of((32, 128))
        last = r0s[h, fr, :, 768:896]
        for x in range(6):
            zb[32 * x : 32 * x + 32, 0:128] = r0s[h, fr, :, 128 * x : 128 * x + 128].astype(BF16)
            zb[32 * x : 32 * x + 32, 128:256] = jnp.where(slots == x, last, 0.0).astype(BF16)

        def one(pair):
            for n in range(2):
                q = 2 * pair + n
                finish(fr, h, q, mm(zb[...], zz[q]).reshape(6, 32, 256))

        each(0, 2, one)

    def synthesis(meanwhile, finish, own, after):
        meanwhile()
        for h in range(2):
            all_modes(r3b, h, g3r)
            x_synthesis_load(h)
            x_synthesis(h)
            r1s[h, s] = vs2[h, s]
        for h in range(2):
            for g in range(2):
                all_of_group(r1s, h, 7, g2r, g)
                y_synthesis(h, g)
                for d in range(1, 4):
                    k1(h, y_at(d), g).start()
            r0s[h, yy] = ys[h, yy]
        for h in range(2):
            z_synthesis(h, yy, finish)
            own(h)
        for h in range(2):

            def one(d, h=h):
                fr = y_at(2 * d - 1 - lax.div(d, 3) * 3)
                whole(r0s.at[h, fr], g1r.at[h, fr])
                z_synthesis(h, fr, finish)
                after(h, fr)

            each(1, 4, one)
        for h in range(2):
            all_modes(r3b, h, g3s)
            all_of(vs2, h, 7, g2s)
            all_of(ys, h, 3, g1s)

    def channel_matrix(wide):
        rows = row_of((512, 512))
        columns = slot_of((512, 512))
        full = lax.dot_general(
            wide.astype(BF16), a16[...], (((1,), (1,)), ((), ())), preferred_element_type=F32
        )
        kron[...] = jnp.where(rows == columns, full, 0.0).astype(BF16)

    def channel_map(source, low, high):
        def one(x):
            for at in (0, 16):
                block = source[:, :, :, x, at : at + 16, :].reshape(512, 256)
                out = mm(kron[...], block)
                lin[:, :, :, x, at : at + 16, :] = out.reshape(4, 2, 4, 16, 256)

        each(low, high, one)

    def lanes(b):
        return pl.ds(b * 128, 128) if isinstance(b, int) else pl.ds(pl.multiple_of(b * 128, 128), 128)

    def unrolled(count, fn):
        for y in range(count):
            fn(y)

    def weights_in():
        loads[0].wait()

        def one(k):
            for part in range(2):
                for i in range(6):
                    w[part, k, 2 * i : 2 * i + 2, :] = w_in[part, k, i]
                w[part, k, 12:16, :] = jnp.zeros((4, 1024), F32)

        each(0, KZ, one)

    def weight_grad_out():
        def one(k):
            for part in range(2):
                for i in range(6):
                    wg_out[part, k, i] = wg[part, k, 2 * i : 2 * i + 2, :]

        each(0, KZ, one)

    def w_at(part, b):
        return w[part, :, :, lanes(b)].reshape(272, 128)

    def mix_one(h):
        def one(y):
            b = 2 * y + h
            modes = split_left(spread_rows(md[h, y]), e1[...])
            mexp[b] = modes
            real, imag = modes[:, :128], modes[:, 128:]
            w_real, w_imag = w_at(0, b), w_at(1, b)
            acc[:, :128] += w_real * real - w_imag * imag
            acc[:, 128:] += w_real * imag + w_imag * real

        unrolled(4, one)

    def spread_out(h, y):
        def one(z):
            pl.when(me != z * 4 + y)(lambda: k3(h, z % 4, z // 4, y).start())

        for z in range(8):
            one(z)

    def keep_own(h):
        r3b[h, me] = mq[h, yy]

    def mix_two():
        for h in range(2):
            for pair in range(2):
                out = split_left(acc[...], rr[h, pair])
                for n in range(2):
                    y = 2 * pair + n
                    mq[h, y] = gather_rows(out[:, 128 * n : 128 * n + 128])
                    spread_out(h, y)
            keep_own(h)

    def back_one(h):
        def one(y):
            gexp[...] += split_left(spread_rows(md[h, y]), e2[2 * y + h])

        unrolled(4, one)

    def back_two():
        for h in range(2):

            def two(y, h=h):
                b = 2 * y + h
                g_real, g_imag = gexp[:, :128], gexp[:, 128:]
                w_real, w_imag = w_at(0, b), w_at(1, b)
                real = w_real * g_real + w_imag * g_imag
                imag = w_real * g_imag - w_imag * g_real
                mq[h, y] = gather_rows(split_left(jnp.concatenate([real, imag], 1), r2[...]))
                spread_out(h, y)

            unrolled(4, two)
            keep_own(h)

    def weight_grad():
        def one(b):
            g_real, g_imag = gexp[:, :128], gexp[:, 128:]
            real, imag = mexp[b, :, :128], mexp[b, :, 128:]
            wg[0, :, :, lanes(b)] = (real * g_real + imag * g_imag).reshape(KZ, 16, 128)
            wg[1, :, :, lanes(b)] = (real * g_imag - imag * g_real).reshape(KZ, 16, 128)

        each(0, 8, one)
        weight_grad_out()

    def finish_pre(fr, h, q, spectral):
        pre = spectral + lin[fr, h, q] + bias[fr * 8 + h * 4 + q]
        pg[fr, h, q] = (cot[fr, h, q].astype(F32) * gelu_slope(pre)).astype(BF16)

    def finish_grad(fr, h, q, spectral):
        ig[fr, h, q] = (spectral + lin[fr, h, q]).astype(BF16)

    def second_own(h):
        z_analysis(pg, h, yy, r0.at[h, yy])

    def second_start(h, to):
        z_analysis(pg, h, to, u.at[h, to])
        for g in range(2):
            c1(h, to, g).start()

    def first_y_wait():
        channel_matrix(mm(a16[...], pw[...]))
        channel_map(f, 0, 6)
        loads[1].wait()

    def first_z_wait():
        weights_in()
        acc[...] = jnp.zeros_like(acc)

    def second_z_wait():
        wide = lax.dot_general(a16[...], pw[...], (((1,), (1,)), ((), ())), preferred_element_type=F32)
        channel_matrix(wide)
        channel_map(pg, 0, 6)
        gexp[...] = jnp.zeros_like(gexp)

    def wait_loads():
        for load in loads[3:]:
            load.wait()

    for h in range(2):
        analysis_start(f, h, h == 1)
    analysis(first_y_wait, first_z_wait, mix_one)
    loads[2].wait()
    mix_two()
    analysis_end()
    synthesis(wait_loads, finish_pre, second_own, second_start)
    analysis(lambda: None, second_z_wait, back_one)
    back_two()
    synthesis(weight_grad, finish_grad, lambda h: None, lambda h, fr: None)
    analysis_end()


def per_device(input_field, cotangent, spectral_weights, point_weight, point_bias):
    field_shape = (4, 2, 4, 6, 32, 256)
    w_shape = spectral_weights.shape
    tabs = {name: jnp.asarray(value) for name, value in TABLES.items()}
    vmem = pl.BlockSpec(memory_space=pltpu.VMEM)
    smem = pl.BlockSpec(memory_space=pltpu.SMEM)
    hbm = pl.BlockSpec(memory_space=pl.ANY)
    dma = pltpu.SemaphoreType.DMA
    scratch = [
        pltpu.VMEM((8, 128, 384), BF16),
        pltpu.VMEM((6, 128, 512), BF16),
        pltpu.VMEM((4, 256, 256), BF16),
        pltpu.VMEM((8, 128, 256), BF16),
        pltpu.VMEM((2, 2, 256, 256), BF16),
        pltpu.VMEM(field_shape, BF16),
        pltpu.VMEM(field_shape, BF16),
        pltpu.VMEM(w_shape, F32),
        pltpu.VMEM((2, KZ, 16, 1024), F32),
        pltpu.VMEM((2, KZ, 16, 1024), F32),
        pltpu.VMEM(field_shape, BF16),
        pltpu.VMEM(field_shape, F32),
        pltpu.VMEM((512, 512), BF16),
        pltpu.VMEM((2, 4, 32, 896), F32),
        pltpu.VMEM((2, 4, 32, 896), F32),
        pltpu.VMEM((2, 8, 8, 896), F32),
        pltpu.VMEM((2, 8, 8, 896), F32),
        pltpu.VMEM((2, 32, 16, 128), F32),
        pltpu.VMEM((2, 32, 16, 128), F32),
        pltpu.VMEM((2, 4, 16, 128), F32),
        pltpu.VMEM((384, 256), BF16),
        pltpu.VMEM((8, 272, 256), F32),
        pltpu.VMEM((272, 256), F32),
        pltpu.VMEM((272, 256), F32),
        pltpu.VMEM((2, 4, 16, 128), F32),
        pltpu.VMEM((2, 32, 16, 128), F32),
        pltpu.VMEM((512, 256), BF16),
        pltpu.VMEM((2, 8, 8, 896), F32),
        pltpu.VMEM((2, 8, 8, 896), F32),
        pltpu.VMEM((2, 4, 32, 896), F32),
        pltpu.VMEM((2, 4, 32, 896), F32),
        pltpu.VMEM((192, 256), BF16),
        dma((4, 2)),
        dma((7,)),
        dma((2,)), dma((2, 2)), dma((2,)), dma((2,)), dma((2,)), dma((2,)),
        dma((2,)), dma((2,)), dma((2,)), dma((2, 2)), dma((2,)), dma((2, 4)),
    ]
    ig, wg = pl.pallas_call(
        body,
        out_shape=(
            pltpu.VMEM(field_shape, BF16),
            pltpu.VMEM(w_shape, F32),
        ),
        in_specs=[vmem, smem] + [vmem] * len(IN_VMEM) + [hbm] * (len(IN_HBM) + 3),
        out_specs=(vmem, vmem),
        scratch_shapes=scratch,
        compiler_params=pltpu.CompilerParams(
            collective_id=0, has_side_effects=True, vmem_limit_bytes=50 * 1024 * 1024
        ),
        cost_estimate=pl.CostEstimate(flops=10**10, bytes_accessed=2 * 10**7, transcendentals=0),
    )(
        point_weight, point_bias,
        *[tabs[name] for name in IN_VMEM],
        *[tabs[name] for name in IN_HBM],
        input_field.reshape(field_shape), cotangent.reshape(field_shape), spectral_weights,
    )
    return (ig.reshape(input_field.shape), wg)


def solution(mesh):
    return jax.shard_map(
        per_device,
        mesh=mesh,
        in_specs=(
            P(None, None, "gx", "gy", None),
            P(None, None, "gx", "gy", None),
            P(None, None, "gy", "gx", None),
            P(),
            P(),
        ),
        out_specs=(P(None, None, "gx", "gy", None), P(None, None, "gy", "gx", None)),
        check_vma=False,
    )
```
